128 devices in a mesh: gx: 4 (over z), gy: 4 (over y), gz: 8 (over x, core).
Axes of the slice: x: 4, y: 4, z: 4, core: 2. Of those that a mesh axis runs over, the one named last changes fastest.
Arguments:
- rhs_old: float32 [512, 196608], P(None, ('gx', 'gy', 'gz'))
- diagonal_old: float32 [512, 196608], P(None, ('gx', 'gy', 'gz')), may hold values from 0.02 to 2
- new_owner: int32 [196608], P(('gx', 'gy', 'gz')), may hold values from -1 to 127, as said below
- face_source: int32 [6, 131072], P(None, ('gx', 'gy', 'gz')), may hold values from 0 to 6656, as said below
- send_layers: int32 [2, 32768], P(None, ('gx', 'gy', 'gz')), may hold values from 0 to 6143, as said below
- block_inverse: float32 [512, 512], replicated
Outputs:
- solution: float32 [512, 131072], P(None, ('gx', 'gy', 'gz'))
- residual: float32 [512, 131072], P(None, ('gx', 'gy', 'gz'))
The draws below stay inside these ranges and needn't reach their ends.
Inputs may be any that keep to these rules, and one draw needn't show every extreme that they name: `new_owner`: A device's 1536 slots hold, in order, the blocks it hands to device e - 1, those it keeps, those it hands to device e + 1, then empty slots (-1). It hands at most 256 to each neighbour; device 0 hands none down, the last device none up, device 1 hands exactly 256 down and device 0 exactly 256 up; every device ends with exactly 1024 blocks. `face_source`: codes as in the reference program. A device reads at most 256 layers through the codes of each neighbour, each such code at most once; device 1 reads all 256 from device 0, device 0 all 256 from device 1; device 0 reads none from below, the last device none from above. The layer named for face g is always face g xor 1 of its block. `send_layers`: entries are local layer codes g * 1024 + k; entries that no face_source code reads are arbitrary layers.
All inputs are finite; a program needn't handle non-finite values.
Results may differ from the reference program's by a relative error of at most 0.00014.
Values sent between devices are 32-bit elements; how exact they have to be, the bound alone decides.
No kernel may reach another device: no remote copies, remote signals or barrier semaphores. Data moves between devices by JAX's collectives and lax.ppermute only.
A program may use at most 128 MiB of HBM per device.

```python
import math
import jax
import jax.numpy as jnp
from jax import lax

BE = 8
BCELLS = 512
FACE = 64
BDEV = 1024
MOVE = 256
CAP = 1536
HMAX = 256
ITERS = 2
NB = 131072
NOLD = 196608
N_GX = 4
N_GY = 4
N_GZ = 8


def links(key):
    devices = N_GX * N_GY * N_GZ
    key = jax.random.fold_in(key, 23)
    keys = jax.random.split(key, 7)
    rank = jnp.arange(devices, dtype=jnp.int32)
    down = jax.random.randint(keys[0], (devices,), HMAX // 2, HMAX + 1).astype(jnp.int32)
    upward = jax.random.randint(keys[1], (devices,), HMAX // 2, HMAX + 1).astype(jnp.int32)
    down = jnp.where(rank == 0, 0, jnp.where(rank == 1, HMAX, down))
    upward = jnp.where(rank == devices - 1, 0, jnp.where(rank == 0, HMAX, upward))
    order = jax.vmap(lambda sub: jax.random.permutation(sub, 6 * BDEV))(jax.random.split(keys[2], devices)).astype(jnp.int32)
    where_is = jnp.argsort(order, axis=1, stable=True).astype(jnp.int32)
    slots = jnp.arange(6 * BDEV, dtype=jnp.int32)[None, :]
    facing = slots // BDEV
    opposite = facing + 1 - 2 * (facing % 2)
    nearby = jax.random.randint(keys[3], (devices, 6 * BDEV), 0, BDEV).astype(jnp.int32)
    border = jax.random.randint(keys[4], (devices, 6 * BDEV), 0, 10).astype(jnp.int32)
    first = down[:, None]
    second = (down + upward)[:, None]
    codes = jnp.where(where_is < first, 6 * BDEV + where_is, jnp.where(where_is < second, 6 * BDEV + HMAX + where_is - first, jnp.where(border == 0, 6 * BDEV + 2 * HMAX, opposite * BDEV + nearby)))
    face_source = codes.reshape(devices, 6, BDEV).transpose(1, 0, 2).reshape(6, devices * BDEV)
    request = jnp.arange(HMAX, dtype=jnp.int32)[None, :]
    down_slot = order[:, :HMAX]
    up_slot = jnp.take_along_axis(order, first + request, axis=1)
    down_face = down_slot // BDEV
    up_face = up_slot // BDEV
    down_layer = (down_face + 1 - 2 * (down_face % 2)) * BDEV + jax.random.randint(keys[5], (devices, HMAX), 0, BDEV).astype(jnp.int32)
    up_layer = (up_face + 1 - 2 * (up_face % 2)) * BDEV + jax.random.randint(keys[6], (devices, HMAX), 0, BDEV).astype(jnp.int32)
    row_lower = jnp.roll(up_layer, 1, axis=0)
    row_upper = jnp.roll(down_layer, -1, axis=0)
    send_layers = jnp.stack([row_lower.reshape(-1), row_upper.reshape(-1)])
    return (face_source.astype(jnp.int32), send_layers.astype(jnp.int32))


def draw_face_source(key, part):
    return links(key)[0]


def draw_send_layers(key, part):
    return links(key)[1]


def draw_new_owner(key, part):
    key = jax.random.fold_in(key, 11)
    devices = N_GX * N_GY * N_GZ
    first_key, second_key = jax.random.split(key)
    rank = jnp.arange(devices, dtype=jnp.int32)
    head = jax.random.randint(first_key, (devices,), 0, MOVE + 1).astype(jnp.int32)
    tail = jax.random.randint(second_key, (devices,), 0, MOVE + 1).astype(jnp.int32)
    head = jnp.where(rank == 0, 0, jnp.where(rank == 1, MOVE, head))
    tail = jnp.where(rank == devices - 1, 0, jnp.where(rank == 0, MOVE, tail))
    tail_prev = jnp.concatenate([jnp.zeros((1,), jnp.int32), tail[:-1]])
    head_next = jnp.concatenate([head[1:], jnp.zeros((1,), jnp.int32)])
    stay = BDEV - tail_prev - head_next
    slot = jnp.arange(CAP, dtype=jnp.int32)[None, :]
    lower = head[:, None]
    keep = (head + stay)[:, None]
    ends = (head + stay + tail)[:, None]
    owners = jnp.where(slot < lower, rank[:, None] - 1, jnp.where(slot < keep, rank[:, None], jnp.where(slot < ends, rank[:, None] + 1, -1)))
    return owners.reshape(-1).astype(jnp.int32)


def draw_rhs_old(key, part):
    key = jax.random.fold_in(key, 5)
    devices = N_GX * N_GY * N_GZ
    column = jnp.arange(devices * CAP, dtype=jnp.int32)
    rise = 3.0 ** ((column // CAP).astype(jnp.float32) / max(devices - 1, 1))
    values = jax.random.normal(key, (BCELLS, devices * CAP), jnp.float32) * rise[None, :]
    return values


def draw_block_inverse(key, part):
    key = jax.random.fold_in(key, 7)
    first_key, second_key = jax.random.split(key)
    leading = jax.random.uniform(first_key, (BCELLS,), jnp.float32, 0.12, 0.22)
    spread = jax.random.normal(second_key, (BCELLS, BCELLS), jnp.float32) * (0.05 / math.sqrt(BCELLS))
    return jnp.diag(leading) + spread


def shard_levels(rng, extent, shards, low, largest):
    loudness = 1.0
    for axis_at, parts in shards:
        steps = jax.random.uniform(jax.random.fold_in(jax.random.fold_in(rng, 6), axis_at), (parts,), jnp.float32, low / len(shards), largest / len(shards))
        loudness = loudness * jnp.repeat(jnp.exp(steps), extent[axis_at] // parts).reshape((-1,) + (1,) * (len(extent) - 1 - axis_at))
    return loudness


def setup_inputs(seed: int = 0) -> dict:
    arg_keys = jax.random.split(jax.random.key(seed), 7)
    return {
        "rhs_old": draw_rhs_old(jax.random.fold_in(arg_keys[6], 71), 0),
        "diagonal_old": jnp.clip(jnp.exp(math.log(2.0) - 4.6051702 * jax.random.uniform(arg_keys[1], (BCELLS, NOLD), jnp.float32) ** shard_levels(arg_keys[1], (BCELLS, NOLD), ((1, 128),), -0.2, 0.2)), 0.02, 2.0),
        "new_owner": draw_new_owner(jax.random.fold_in(arg_keys[6], 71), 0),
        "face_source": draw_face_source(jax.random.fold_in(arg_keys[6], 71), 0),
        "send_layers": draw_send_layers(jax.random.fold_in(arg_keys[6], 71), 0),
        "block_inverse": draw_block_inverse(jax.random.fold_in(arg_keys[6], 71), 0),
    }


def split_faces(field):
    columns = field.shape[1]
    volume = field.reshape(BE, BE, BE, columns)
    return [volume[0].reshape(FACE, columns), volume[BE - 1].reshape(FACE, columns),
            volume[:, 0].reshape(FACE, columns), volume[:, BE - 1].reshape(FACE, columns),
            volume[:, :, 0].reshape(FACE, columns), volume[:, :, BE - 1].reshape(FACE, columns)]


def apply_operator(field, diagonal, outside):
    columns = field.shape[1]
    volume = field.reshape(BE, BE, BE, columns)
    beside = jnp.concatenate([outside[0].reshape(1, BE, BE, columns), volume[:-1]], axis=0)
    beside = beside + jnp.concatenate([volume[1:], outside[1].reshape(1, BE, BE, columns)], axis=0)
    beside = beside + jnp.concatenate([outside[2].reshape(BE, 1, BE, columns), volume[:, :-1]], axis=1)
    beside = beside + jnp.concatenate([volume[:, 1:], outside[3].reshape(BE, 1, BE, columns)], axis=1)
    beside = beside + jnp.concatenate([outside[4].reshape(BE, BE, 1, columns), volume[:, :, :-1]], axis=2)
    beside = beside + jnp.concatenate([volume[:, :, 1:], outside[5].reshape(BE, BE, 1, columns)], axis=2)
    return (6.0 + diagonal) * field - beside.reshape(field.shape)


def reference(rhs_old, diagonal_old, new_owner, face_source, send_layers, block_inverse):
    devices = N_GX * N_GY * N_GZ
    owners = new_owner.reshape(devices, CAP)
    rank = jnp.arange(devices, dtype=jnp.int32)[:, None]
    slot = jnp.arange(CAP, dtype=jnp.int32)[None, :]
    filled = owners >= 0
    to_lower = (owners == rank - 1) & filled
    to_self = owners == rank
    to_upper = (owners == rank + 1) & filled
    head = jnp.sum(to_lower.astype(jnp.int32), axis=1, keepdims=True)
    stay = jnp.sum(to_self.astype(jnp.int32), axis=1, keepdims=True)
    tail = jnp.sum(to_upper.astype(jnp.int32), axis=1, keepdims=True)
    tail_prev = jnp.concatenate([jnp.zeros((1, 1), jnp.int32), tail[:-1]], axis=0)
    place = jnp.where(to_lower, rank * BDEV - head + slot,
                      jnp.where(to_self, rank * BDEV + tail_prev + slot - head,
                                jnp.where(to_upper, (rank + 1) * BDEV + slot - head - stay, NB)))
    place = place.reshape(-1).astype(jnp.int32)
    rhs = jnp.zeros((BCELLS, NB), jnp.float32).at[:, place].set(rhs_old, mode="drop")
    diagonal = jnp.zeros((BCELLS, NB), jnp.float32).at[:, place].set(diagonal_old, mode="drop")

    block = jnp.arange(NB, dtype=jnp.int32)[None, :]
    owner = block // BDEV
    codes = face_source
    local_cols = (codes // BDEV) * NB + owner * BDEV + codes % BDEV
    low_src = jnp.clip(owner - 1, 0, devices - 1)
    low_code = send_layers[1][low_src * HMAX + jnp.clip(codes - 6 * BDEV, 0, HMAX - 1)]
    low_cols = (low_code // BDEV) * NB + low_src * BDEV + low_code % BDEV
    high_src = jnp.clip(owner + 1, 0, devices - 1)
    high_code = send_layers[0][high_src * HMAX + jnp.clip(codes - 6 * BDEV - HMAX, 0, HMAX - 1)]
    high_cols = (high_code // BDEV) * NB + high_src * BDEV + high_code % BDEV
    cols = jnp.where(codes < 6 * BDEV, local_cols,
                     jnp.where(codes < 6 * BDEV + HMAX, low_cols,
                               jnp.where(codes < 6 * BDEV + 2 * HMAX, high_cols, 6 * NB))).astype(jnp.int32)
    zero_column = jnp.zeros((FACE, 1), jnp.float32)

    def operate(field):
        table = jnp.concatenate(split_faces(field) + [zero_column], axis=1)
        outside = [table[:, cols[which]] for which in range(6)]
        return apply_operator(field, diagonal, outside)

    def precondition(field):
        return jnp.dot(block_inverse, field, precision=lax.Precision.HIGHEST, preferred_element_type=jnp.float32)

    solution = jnp.zeros((BCELLS, NB), jnp.float32)
    residual = rhs
    shadow = rhs
    rho = jnp.sum(shadow * residual)
    direction = residual
    along = jnp.zeros((BCELLS, NB), jnp.float32)
    alpha = jnp.float32(1.0)
    omega = jnp.float32(1.0)
    rho_next = rho
    for step in range(ITERS):
        if step > 0:
            beta = (rho_next / rho) * (alpha / omega)
            rho = rho_next
            direction = residual + beta * (direction - omega * along)
        search = precondition(direction)
        along = operate(search)
        alpha = rho / jnp.sum(shadow * along)
        middle = residual - alpha * along
        middle_pre = precondition(middle)
        image = operate(middle_pre)
        omega = jnp.sum(image * middle) / jnp.sum(image * image)
        solution = solution + alpha * search + omega * middle_pre
        residual = middle - omega * image
        rho_next = jnp.sum(shadow * residual)
    return solution, residual
```

```python
import functools

import jax
import jax.numpy as jnp
from jax import lax
from jax.experimental import pallas as pl
from jax.experimental.pallas import tpu as pltpu
from jax.sharding import PartitionSpec as P

BE = 8
BCELLS = 512
FACE = 64
BDEV = 1024
MOVE = 256
CAP = 1536
HMAX = 256
ITERS = 2
LANES = 128
SUB = 8
CHUNKS = BDEV // LANES
AXES = ("gx", "gy", "gz")
REMOTE = 6 * BDEV
BASIS = 2 * ITERS + 1
MIB = 1024 * 1024
F32 = jnp.float32

VMEM = pl.BlockSpec(memory_space=pltpu.VMEM)
SMEM = pl.BlockSpec(memory_space=pltpu.SMEM)


def shifted(value, steps):
    count = lax.axis_size(AXES)
    initial, last = (max(0, -steps), min(count, count - steps))
    return lax.ppermute(value, AXES, [(source, source + steps) for source in range(initial, last)])


def call(kernel, outs, args, in_specs, out_specs, scratch=(), limit=24, flops=0, bytes_accessed=0):
    return pl.pallas_call(
        kernel,
        out_shape=outs,
        in_specs=in_specs,
        out_specs=out_specs,
        scratch_shapes=list(scratch),
        compiler_params=pltpu.CompilerParams(vmem_limit_bytes=limit * MIB),
        cost_estimate=pl.CostEstimate(
            flops=flops, bytes_accessed=bytes_accessed, transcendentals=0
        ),
    )(*args)


def lane_iota(rows=SUB):
    return lax.broadcasted_iota(jnp.int32, (rows, LANES), 1)


def lanes(start):
    return pl.ds(pl.multiple_of(start, LANES), LANES)


def pick(values, index):
    return jnp.take_along_axis(values, index, axis=1, mode="promise_in_bounds")


def counts_kernel(rank_ref, owner_ref, counts_ref):
    rank = rank_ref[0]
    owner = owner_ref[...]
    filled = owner >= 0
    counts_ref[0] = jnp.sum(((owner == rank - 1) & filled).astype(jnp.int32))
    counts_ref[1] = jnp.sum((owner == rank).astype(jnp.int32))
    counts_ref[2] = jnp.sum(((owner == rank + 1) & filled).astype(jnp.int32))


def cut_kernel(counts_ref, old_ref, lower_ref, upper_ref):
    start = counts_ref[0] + counts_ref[1]
    tile = start >> 7
    shift = start & (LANES - 1)
    rows = 64

    def body(step, carry):
        at = pl.ds(pl.multiple_of(step * rows, rows), rows)
        lower_ref[at, :] = old_ref[at, 0:MOVE]
        first = lane_iota(rows) < LANES - shift
        turned = []
        for part in range(3):
            source = jnp.minimum(tile + part, CAP // LANES - 1) * LANES
            turned.append(pltpu.roll(old_ref[at, lanes(source)], (LANES - shift) & (LANES - 1), 1))
        upper_ref[at, 0:LANES] = jnp.where(first, turned[0], turned[1])
        upper_ref[at, LANES:MOVE] = jnp.where(first, turned[1], turned[2])
        return carry

    lax.fori_loop(0, BCELLS // rows, body, 0)
    upper_ref[BCELLS : BCELLS + SUB, :] = jnp.full((SUB, MOVE), counts_ref[2].astype(F32))


def assemble(counts_ref, before, old_ref, lower_ref, upper_ref, out_ref, turned_ref):
    head = counts_ref[0]
    stay = counts_ref[1]
    own_start = head - before
    own_tile = own_start >> 7
    own_shift = own_start & (LANES - 1)
    up_start = -(before + stay)
    up_tile = up_start >> 7
    up_shift = up_start & (LANES - 1)
    rows = 16

    def body(step, carry):
        start = pl.multiple_of(step * rows, rows)
        at = pl.ds(start, rows)
        lane = lane_iota(rows)
        for part in range(2):
            turned_ref[part] = pltpu.roll(
                upper_ref[at, part * LANES : (part + 1) * LANES],
                (LANES - up_shift) & (LANES - 1),
                1,
            )
        last = None
        for chunk in range(CHUNKS + 1):
            source = jnp.clip(own_tile + chunk, 0, CAP // LANES - 1) * LANES
            now = pltpu.roll(
                old_ref[at, lanes(source)], (LANES - own_shift) & (LANES - 1), 1
            )
            if chunk > 0:
                place = chunk - 1
                column = lane + place * LANES
                own = jnp.where(lane < LANES - own_shift, last, now)
                low_half = turned_ref[jnp.clip(up_tile + place, 0, 1)]
                high_half = turned_ref[jnp.clip(up_tile + place + 1, 0, 1)]
                above = jnp.where(lane < LANES - up_shift, low_half, high_half)
                value = jnp.where(column < before + stay, own, above)
                if place < MOVE // LANES:
                    below = lower_ref[at, place * LANES : (place + 1) * LANES]
                    value = jnp.where(column < before, below, value)
                out_ref[pl.ds(place * BCELLS + start, rows), :] = value
            last = now
        return carry

    lax.fori_loop(0, BCELLS // rows, body, 0)


def diagonal_kernel(counts_ref, before_ref, old_ref, lower_ref, upper_ref, out_ref, turned_ref):
    assemble(counts_ref, before_ref[0], old_ref, lower_ref, upper_ref, out_ref, turned_ref)


def prepare_kernel(inverse_ref, high_ref, low_ref, theta_ref):
    inverse = inverse_ref[...]
    size = jnp.abs(inverse)
    by_row = jnp.max(jnp.sum(size, axis=1, keepdims=True), axis=0, keepdims=True)
    by_column = jnp.max(jnp.sum(size, axis=0, keepdims=True), axis=1, keepdims=True)
    bound = 14.5 * jnp.sqrt(by_row) * jnp.sqrt(by_column)
    scale = jnp.full((1, 1), 0.5, F32)
    for power in (64, 32, 16, 8, 4, 2, 1):
        large = bound >= 2.0**power
        bound = jnp.where(large, bound * 2.0**-power, bound)
        scale = jnp.where(large, scale * 2.0**-power, scale)
    for power in (64, 32, 16, 8, 4, 2, 1):
        small = bound < 2.0**-power
        bound = jnp.where(small, bound * 2.0**power, bound)
        scale = jnp.where(small, scale * 2.0**power, scale)
    scaled = inverse * scale
    high = scaled.astype(jnp.bfloat16)
    high_ref[...] = high
    low_ref[...] = (scaled - high.astype(F32)).astype(jnp.bfloat16)
    row = lax.broadcasted_iota(jnp.int32, (BCELLS, BCELLS), 0)
    column = lax.broadcasted_iota(jnp.int32, (BCELLS, BCELLS), 1)
    theta_ref[0] = jnp.sum(jnp.where(row == column, scaled, 0.0)) * (6.5 / BCELLS)


def precondition(high_ref, low_ref, field_ref, out_ref):
    def body(step, carry):
        base = pl.multiple_of(step * (2 * BCELLS), 2 * BCELLS)
        halves = [pl.ds(base + half * BCELLS, BCELLS) for half in range(2)]
        field = jnp.concatenate([field_ref[half, :] for half in halves], axis=1)
        top = field.astype(jnp.bfloat16)
        rest = (field - top.astype(F32)).astype(jnp.bfloat16)
        high = high_ref[...]
        small = jnp.dot(high, rest, preferred_element_type=F32)
        small = small + jnp.dot(low_ref[...], top, preferred_element_type=F32)
        found = small + jnp.dot(high, top, preferred_element_type=F32)
        out_ref[halves[0], :] = found[:, :LANES]
        out_ref[halves[1], :] = found[:, LANES:]
        return carry

    lax.fori_loop(0, CHUNKS // 2, body, 0)


def split_ends(field_ref, first_ref, last_ref):
    first_ref[...] = field_ref[pl.ds(0, CHUNKS * FACE, stride=BE), :]
    last_ref[...] = field_ref[pl.ds(BE - 1, CHUNKS * FACE, stride=BE), :]


def layer_tile(field_ref, ends, which, part, chunk):
    if which >= 4:
        row = chunk * FACE + part * SUB
        return ends[which - 4][row : row + SUB, :]
    row = (part * BE, (BE - 1) * FACE + part * BE, part * FACE, part * FACE + (BE - 1) * BE)[which]
    row = row + chunk * BCELLS
    return field_ref[row : row + SUB, :]


def pack(field_ref, ends, send_ref, to_lower_ref, to_upper_ref):
    for row, out_ref in ((0, to_lower_ref), (1, to_upper_ref)):

        def body(step, carry, row=row, out_ref=out_ref):
            code = jnp.broadcast_to(send_ref[row : row + 1, lanes(step * LANES)], (SUB, LANES))
            lane = code & (LANES - 1)
            tile = code >> 7
            found = [jnp.zeros((SUB, LANES), F32) for _ in range(8)]
            for which in range(6):
                for source in range(CHUNKS):
                    here = tile == which * CHUNKS + source
                    for part in range(8):
                        values = layer_tile(field_ref, ends, which, part, source)
                        found[part] = jnp.where(here, pick(values, lane), found[part])
            base = pl.multiple_of(step * FACE, FACE)
            for part in range(8):
                out_ref[pl.ds(base + part * SUB, SUB), :] = found[part]
            return carry

        lax.fori_loop(0, HMAX // LANES, body, 0)


def put_layers(which, found, faces_ref, ends_ref):
    for part in range(8):
        if which < 4:
            base = which * FACE + part * SUB
            faces_ref[base : base + SUB, :] = found[part]
        else:
            ends_ref[pl.ds(part * FACE + (which - 4) * (BE - 1), SUB, stride=BE), :] = found[part]


def local_kernel(codes_ref, field_ref, out_ref, first_ref, last_ref, faces_ref, ends_ref):
    split_ends(field_ref, first_ref, last_ref)
    ends = (first_ref, last_ref)
    cell = lax.broadcasted_iota(jnp.int32, (SUB, LANES), 0)

    def body(step, carry):
        at = lanes(step * LANES)
        start = pl.multiple_of(step * BCELLS, BCELLS)
        for which in range(6):
            partner = which ^ 1
            code = jnp.broadcast_to(codes_ref[which : which + 1, at], (SUB, LANES))
            code = code - partner * BDEV
            lane = code & (LANES - 1)
            tile = code >> 7
            found = [jnp.zeros((SUB, LANES), F32) for _ in range(8)]
            for source in range(CHUNKS):
                here = tile == source
                for part in range(8):
                    values = layer_tile(field_ref, ends, partner, part, source)
                    found[part] = jnp.where(here, pick(values, lane), found[part])
            put_layers(which, found, faces_ref, ends_ref)

        def block(i, j):
            row = (i * BE + j) * BE
            return field_ref[pl.ds(start + row, SUB), :]

        def layer(which, part):
            base = which * FACE + part * SUB
            return faces_ref[base : base + SUB, :]

        for i in range(BE):
            for j in range(BE):
                row = (i * BE + j) * BE
                here = block(i, j)
                edge = ends_ref[row : row + SUB, :]
                beside = block(i - 1, j) if i > 0 else layer(0, j)
                beside = beside + (block(i + 1, j) if i < BE - 1 else layer(1, j))
                beside = beside + (block(i, j - 1) if j > 0 else layer(2, i))
                beside = beside + (block(i, j + 1) if j < BE - 1 else layer(3, i))
                beside = beside + jnp.where(cell == 0, edge, pltpu.roll(here, 1, 0))
                beside = beside + jnp.where(cell == BE - 1, edge, pltpu.roll(here, BE - 1, 0))
                out_ref[pl.ds(start + row, SUB), :] = 6.0 * here - beside
        return carry

    lax.fori_loop(0, CHUNKS, body, 0)


def finish(
    theta, codes_ref, below_ref, above_ref, diagonal_ref, field_ref, partial_ref, basis, out_ref,
    faces_ref, ends_ref, sums_ref
):
    cell = lax.broadcasted_iota(jnp.int32, (SUB, LANES), 0)
    is_end = (cell == 0) | (cell == BE - 1)
    sums_ref[...] = jnp.zeros_like(sums_ref)

    def body(step, carry):
        at = lanes(step * LANES)
        start = pl.multiple_of(step * BCELLS, BCELLS)
        for which in range(6):
            code = jnp.broadcast_to(codes_ref[which : which + 1, at], (SUB, LANES)) - REMOTE
            lane = code & (LANES - 1)
            tile = code >> 7
            found = [jnp.zeros((SUB, LANES), F32) for _ in range(8)]
            for source in range(2 * HMAX // LANES):
                here = tile == source
                from_ref = below_ref if source < HMAX // LANES else above_ref
                base = source % (HMAX // LANES) * FACE
                for part in range(8):
                    values = from_ref[base + part * SUB : base + (part + 1) * SUB, :]
                    found[part] = jnp.where(here, pick(values, lane), found[part])
            put_layers(which, found, faces_ref, ends_ref)

        def layer(which, part):
            base = which * FACE + part * SUB
            return faces_ref[base : base + SUB, :]

        sums = [jnp.zeros((SUB, LANES), F32) for _ in range(len(basis) + 1)]
        for i in range(BE):
            for j in range(BE):
                row = (i * BE + j) * BE
                rows = pl.ds(start + row, SUB)
                beside = jnp.where(is_end, ends_ref[row : row + SUB, :], 0.0)
                if i == 0:
                    beside = beside + layer(0, j)
                if i == BE - 1:
                    beside = beside + layer(1, j)
                if j == 0:
                    beside = beside + layer(2, i)
                if j == BE - 1:
                    beside = beside + layer(3, i)
                value = partial_ref[rows, :] + diagonal_ref[rows, :] * field_ref[rows, :]
                value = value - beside - theta * basis[-1][rows, :]
                out_ref[rows, :] = value
                for k, ref in enumerate(basis):
                    sums[k] = sums[k] + value * ref[rows, :]
                sums[-1] = sums[-1] + value * value
        for k, part in enumerate(sums):
            sums_ref[k] += part
        return carry

    lax.fori_loop(0, CHUNKS, body, 0)


def place_sums(sums_ref, count, gram_in, gram_out_ref, first):
    lane = lax.broadcasted_iota(jnp.int32, (SUB, LANES), 1)
    row = gram_in
    for k in range(count):
        row = row + jnp.where(lane == first + k, jnp.sum(sums_ref[k]), 0.0)
    gram_out_ref[...] = row


def first_kernel(
    counts_ref, before_ref, old_ref, lower_ref, upper_ref, high_ref, low_ref, send_ref,
    rhs_ref, field_ref, to_lower_ref, to_upper_ref, gram_ref,
    turned_ref, first_ref, last_ref, sums_ref,
):
    assemble(counts_ref, before_ref[0], old_ref, lower_ref, upper_ref, rhs_ref, turned_ref)
    precondition(high_ref, low_ref, rhs_ref, field_ref)
    split_ends(field_ref, first_ref, last_ref)
    pack(field_ref, (first_ref, last_ref), send_ref, to_lower_ref, to_upper_ref)
    sums_ref[...] = jnp.zeros_like(sums_ref)

    def body(step, carry):
        total = jnp.zeros((SUB, LANES), F32)
        start = pl.multiple_of(step * BCELLS, BCELLS)
        for row in range(0, BCELLS, SUB):
            value = rhs_ref[pl.ds(start + row, SUB), :]
            total = total + value * value
        sums_ref[0] += total
        return carry

    lax.fori_loop(0, CHUNKS, body, 0)
    place_sums(sums_ref, 1, jnp.zeros((SUB, LANES), F32), gram_ref, 0)


def next_kernel(known, more, *refs):
    theta_ref, codes_ref, below_ref, above_ref, diagonal_ref, field_ref, partial_ref = refs[:7]
    basis = refs[7 : 7 + known]
    gram_in_ref = refs[7 + known]
    at = 8 + known
    if more:
        high_ref, low_ref, send_ref = refs[at : at + 3]
        at += 3
        out_ref, gram_ref, next_ref, to_lower_ref, to_upper_ref = refs[at : at + 5]
        at += 5
    else:
        out_ref, gram_ref = refs[at : at + 2]
        at += 2
    faces_ref, ends_ref, sums_ref, first_ref, last_ref = refs[at:]
    finish(
        theta_ref[0], codes_ref, below_ref, above_ref, diagonal_ref, field_ref, partial_ref,
        basis, out_ref, faces_ref, ends_ref, sums_ref,
    )
    if more:
        precondition(high_ref, low_ref, out_ref, next_ref)
        split_ends(next_ref, first_ref, last_ref)
        pack(next_ref, (first_ref, last_ref), send_ref, to_lower_ref, to_upper_ref)
    place_sums(sums_ref, known + 1, gram_in_ref[...], gram_ref, known * (known + 1) // 2)


def recurrence(gram, theta):
    def dot(left, right):
        total = None
        for a, x in enumerate(left):
            if x is None:
                continue
            part = None
            for b, y in enumerate(right):
                if y is not None:
                    term = gram[max(a, b)][min(a, b)] * y
                    part = term if part is None else part + term
            total = x * part if total is None else total + x * part
        return total

    def add(left, right):
        return [
            y if x is None else x if y is None else x + y for x, y in zip(left, right)
        ]

    def times(factor, vector):
        return [None if x is None else factor * x for x in vector]

    def apply(vector):
        return add([None] + vector[:-1], times(theta, vector))

    one = jnp.ones_like(theta)
    shadow = [one] + [None] * (BASIS - 1)
    residual = shadow
    direction = residual
    rho = gram[0][0]
    rho_next = rho
    total = [None] * BASIS
    along = alpha = omega = None
    for step in range(ITERS):
        if step > 0:
            beta = (rho_next / rho) * (alpha / omega)
            rho = rho_next
            direction = add(residual, times(beta, add(direction, times(-omega, along))))
        along = apply(direction)
        alpha = rho / dot(shadow, along)
        middle = add(residual, times(-alpha, along))
        image = apply(middle)
        omega = dot(image, middle) / dot(image, image)
        total = add(total, add(times(alpha, direction), times(omega, middle)))
        residual = add(middle, times(-omega, image))
        rho_next = dot(shadow, residual)
    return total, residual


def last_kernel(theta_ref, gathered_ref, *refs):
    basis = refs[:BASIS]
    fields = refs[BASIS : 2 * BASIS - 1]
    solution_ref, residual_ref = refs[2 * BASIS - 1 :]
    row = jnp.sum(gathered_ref[...], axis=0, keepdims=True)
    lane = lax.broadcasted_iota(jnp.int32, (1, LANES), 1)

    def entry(k):
        return jnp.sum(jnp.where(lane == k, row, 0.0), axis=1, keepdims=True)

    gram = [[entry(a * (a + 1) // 2 + b) for b in range(a + 1)] for a in range(BASIS)]
    theta = jnp.full((1, 1), theta_ref[0])
    total, residual = recurrence(gram, theta)
    total = [None if x is None else jnp.broadcast_to(x, (SUB, LANES)) for x in total]
    residual = [jnp.broadcast_to(x, (SUB, LANES)) for x in residual]

    def body(step, carry):
        start = pl.multiple_of(step * SUB, SUB)
        for chunk in range(CHUNKS):
            rows = pl.ds(chunk * BCELLS + start, SUB)
            at = slice(chunk * LANES, (chunk + 1) * LANES)
            value = total[0] * fields[0][rows, :]
            for k in range(1, BASIS - 1):
                value = value + total[k] * fields[k][rows, :]
            solution_ref[pl.ds(start, SUB), at] = value
            value = residual[0] * basis[0][rows, :]
            for k in range(1, BASIS):
                value = value + residual[k] * basis[k][rows, :]
            residual_ref[pl.ds(start, SUB), at] = value
        return carry

    lax.fori_loop(0, BCELLS // SUB, body, 0)


def per_device(rhs_old, diagonal_old, new_owner, face_source, send_layers, block_inverse):
    field_type = jax.ShapeDtypeStruct((CHUNKS * BCELLS, LANES), F32)
    out_type = jax.ShapeDtypeStruct((BCELLS, BDEV), F32)
    halo_type = jax.ShapeDtypeStruct((HMAX // LANES * FACE, LANES), F32)
    gram_type = jax.ShapeDtypeStruct((SUB, LANES), F32)
    half_type = jax.ShapeDtypeStruct((BCELLS, BCELLS), jnp.bfloat16)
    lower_type = jax.ShapeDtypeStruct((BCELLS, MOVE), F32)
    upper_type = jax.ShapeDtypeStruct((BCELLS + SUB, MOVE), F32)
    turned = pltpu.VMEM((2, 16, LANES), F32)
    end_layers = [pltpu.VMEM((CHUNKS * FACE, LANES), F32)] * 2
    layers = [pltpu.VMEM((4 * FACE, LANES), F32), pltpu.VMEM((BCELLS, LANES), F32)]
    sums = pltpu.VMEM((BASIS, SUB, LANES), F32)

    rank = lax.axis_index(AXES).astype(jnp.int32).reshape(1)
    counts = call(
        counts_kernel,
        jax.ShapeDtypeStruct((3,), jnp.int32),
        (rank, new_owner.reshape(CAP // LANES, LANES)),
        [SMEM, VMEM],
        SMEM,
    )

    def cut(old):
        return call(
            cut_kernel, (lower_type, upper_type), (counts, old), [SMEM, VMEM], (VMEM, VMEM)
        )

    lower, upper = cut(rhs_old)
    rhs_above = shifted(lower, -1)
    rhs_below = shifted(upper, 1)
    lower, upper = cut(diagonal_old)
    diagonal_above = shifted(lower, -1)
    diagonal_below = shifted(upper, 1)
    high, low, theta = call(
        prepare_kernel,
        (half_type, half_type, jax.ShapeDtypeStruct((1,), F32)),
        (block_inverse,),
        [VMEM],
        (VMEM, VMEM, SMEM),
    )
    before = rhs_below[BCELLS, 0:1].astype(jnp.int32)
    rhs, field, to_lower, to_upper, gram = call(
        first_kernel,
        (field_type, field_type, halo_type, halo_type, gram_type),
        (counts, before, rhs_old, rhs_below, rhs_above, high, low, send_layers),
        [SMEM, SMEM] + [VMEM] * 6,
        (VMEM,) * 5,
        [turned] + end_layers + [sums],
        flops=10**9,
        bytes_accessed=8 * MIB,
    )
    diagonal = call(
        diagonal_kernel,
        field_type,
        (counts, before, diagonal_old, diagonal_below, diagonal_above),
        [SMEM, SMEM] + [VMEM] * 3,
        VMEM,
        [turned],
        bytes_accessed=6 * MIB,
    )
    basis = [rhs]
    fields = [field]
    for known in range(1, BASIS):
        above = shifted(to_lower, -1)
        below = shifted(to_upper, 1)
        partial = call(
            local_kernel,
            field_type,
            (face_source, field),
            [VMEM] * 2,
            VMEM,
            end_layers + layers,
            flops=10**9,
            bytes_accessed=4 * MIB,
        )
        more = known < BASIS - 1
        args = [theta, face_source, below, above, diagonal, field, partial] + basis + [gram]
        outs = [field_type, gram_type]
        if more:
            args += [high, low, send_layers]
            outs += [field_type, halo_type, halo_type]
        found = call(
            functools.partial(next_kernel, known, more),
            tuple(outs),
            tuple(args),
            [SMEM] + [VMEM] * (len(args) - 1),
            (VMEM,) * len(outs),
            layers + [sums] + end_layers,
            limit=32,
            flops=10**9,
            bytes_accessed=12 * MIB,
        )
        if more:
            value, gram, field, to_lower, to_upper = found
            fields.append(field)
        else:
            value, gram = found
        basis.append(value)
    gathered = lax.all_gather(gram[0:1], AXES, axis=0, tiled=True)
    return call(
        last_kernel,
        (out_type, out_type),
        (theta, gathered, *basis, *fields),
        [SMEM] + [VMEM] * (2 * BASIS),
        (VMEM, VMEM),
        limit=32,
    )


def solution(mesh):
    return jax.shard_map(
        per_device,
        mesh=mesh,
        in_specs=(
            P(None, AXES),
            P(None, AXES),
            P(AXES),
            P(None, AXES),
            P(None, AXES),
            P(),
        ),
        out_specs=(P(None, AXES), P(None, AXES)),
        check_vma=False,
    )
```

```python
import functools

import jax
import jax.numpy as jnp
from jax import lax
from jax.experimental import pallas as pl
from jax.experimental.pallas import tpu as pltpu
from jax.sharding import PartitionSpec as P

BE = 8
BCELLS = 512
FACE = 64
BDEV = 1024
MOVE = 256
CAP = 1536
HMAX = 256
ITERS = 2
LANES = 128
SUB = 8
CHUNKS = BDEV // LANES
AXES = ("gx", "gy", "gz")
REMOTE = 6 * BDEV
BASIS = 2 * ITERS + 1
MIB = 1024 * 1024
PARTS = 8
PAIR = 2
F32 = jnp.float32

VMEM = pl.BlockSpec(memory_space=pltpu.VMEM)
SMEM = pl.BlockSpec(memory_space=pltpu.SMEM)
HBM = pl.BlockSpec(memory_space=pltpu.HBM)


def swapped(value, cross):
    count = lax.axis_size(AXES)
    first = 1 if cross else 0
    pairs = [(low, low + 1) for low in range(first, count - 1, 2)]
    return lax.ppermute(value, AXES, pairs + [(high, low) for low, high in pairs])


def call(kernel, outs, args, in_specs, out_specs, scratch=(), limit=24, flops=0, bytes_accessed=0):
    return pl.pallas_call(
        kernel,
        out_shape=outs,
        in_specs=in_specs,
        out_specs=out_specs,
        scratch_shapes=list(scratch),
        compiler_params=pltpu.CompilerParams(vmem_limit_bytes=limit * MIB),
        cost_estimate=pl.CostEstimate(
            flops=flops, bytes_accessed=bytes_accessed, transcendentals=0
        ),
    )(*args)


def lane_iota(rows=SUB):
    return lax.broadcasted_iota(jnp.int32, (rows, LANES), 1)


def lanes(start):
    return pl.ds(pl.multiple_of(start, LANES), LANES)


def pick(values, index):
    return jnp.take_along_axis(values, index, axis=1, mode="promise_in_bounds")


def cut_rows(start, low_ref, high_ref, odd, count, cross_ref, inside_ref):
    tile = start >> 7
    shift = start & (LANES - 1)
    rows = 128

    for step in range(BCELLS // rows):
        at = slice(step * rows, (step + 1) * rows)
        first = lane_iota(rows) < LANES - shift
        turned = []
        for part in range(3):
            source = jnp.minimum(tile + part, high_ref.shape[1] // LANES - 1) * LANES
            turned.append(pltpu.roll(high_ref[at, lanes(source)], (LANES - shift) & (LANES - 1), 1))
        for half in range(2):
            lower = low_ref[at, half * LANES : (half + 1) * LANES]
            upper = jnp.where(first, turned[half], turned[half + 1])
            to = slice(half * BCELLS + step * rows, half * BCELLS + (step + 1) * rows)
            cross_ref[to, :] = jnp.where(odd, upper, lower)
            inside_ref[to, :] = jnp.where(odd, lower, upper)
    if count is not None:
        row = jnp.full((SUB, LANES), count.astype(F32))
        cross_ref[2 * BCELLS : 2 * BCELLS + SUB, :] = row
        inside_ref[2 * BCELLS : 2 * BCELLS + SUB, :] = row


def front_kernel(
    rank_ref, owner_hbm, old_ref, counts_ref, cross_ref, inside_ref,
    owner_ref, low_ref, high_ref, sems
):
    owner_copy = pltpu.make_async_copy(owner_hbm, owner_ref, sems.at[2])
    owner_copy.start()
    low_copy = pltpu.make_async_copy(old_ref.at[:, pl.ds(0, MOVE)], low_ref, sems.at[0])
    low_copy.start()
    owner_copy.wait()
    rank = rank_ref[0]
    owner = owner_ref[...]
    filled = owner >= 0
    head = jnp.sum(((owner == rank - 1) & filled).astype(jnp.int32))
    stay = jnp.sum((owner == rank).astype(jnp.int32))
    tail = jnp.sum(((owner == rank + 1) & filled).astype(jnp.int32))
    odd = rank & 1
    counts_ref[0] = head
    counts_ref[1] = stay
    counts_ref[2] = tail
    counts_ref[3] = odd
    start = head + stay
    window = jnp.clip(start >> 7, 0, CAP // LANES - 3) * LANES
    high_copy = pltpu.make_async_copy(
        old_ref.at[:, pl.ds(pl.multiple_of(window, LANES), 3 * LANES)], high_ref, sems.at[1]
    )
    high_copy.start()
    low_copy.wait()
    high_copy.wait()
    cut_rows(start - window, low_ref, high_ref, odd == 1, tail, cross_ref, inside_ref)


def cut_kernel(counts_ref, old_ref, cross_ref, inside_ref):
    start = counts_ref[0] + counts_ref[1]
    cut_rows(start, old_ref, old_ref, counts_ref[3] == 1, None, cross_ref, inside_ref)


def count_before(odd, cross_ref, inside_ref):
    row = slice(2 * BCELLS, 2 * BCELLS + SUB)
    return jnp.max(jnp.where(odd, inside_ref[row, :], cross_ref[row, :])).astype(jnp.int32)


def assemble(counts_ref, before, old_ref, cross_ref, inside_ref, out_ref, turned_ref):
    head = counts_ref[0]
    stay = counts_ref[1]
    odd = counts_ref[3] == 1
    own_start = head - before
    own_tile = own_start >> 7
    own_shift = own_start & (LANES - 1)
    up_start = -(before + stay)
    up_tile = up_start >> 7
    up_shift = up_start & (LANES - 1)
    rows = 64

    def body(step, carry):
        start = pl.multiple_of(step * rows, rows)
        at = pl.ds(start, rows)
        lane = lane_iota(rows)
        for part in range(2):
            half = pl.ds(part * BCELLS + start, rows)
            turned_ref[part] = pltpu.roll(
                jnp.where(odd, cross_ref[half, :], inside_ref[half, :]),
                (LANES - up_shift) & (LANES - 1),
                1,
            )
        last = None
        for chunk in range(CHUNKS + 1):
            source = jnp.clip(own_tile + chunk, 0, CAP // LANES - 1) * LANES
            now = pltpu.roll(
                old_ref[at, lanes(source)], (LANES - own_shift) & (LANES - 1), 1
            )
            if chunk > 0:
                place = chunk - 1
                column = lane + place * LANES
                own = jnp.where(lane < LANES - own_shift, last, now)
                low_half = turned_ref[jnp.clip(up_tile + place, 0, 1)]
                high_half = turned_ref[jnp.clip(up_tile + place + 1, 0, 1)]
                above = jnp.where(lane < LANES - up_shift, low_half, high_half)
                value = jnp.where(column < before + stay, own, above)
                if place < MOVE // LANES:
                    half = pl.ds(place * BCELLS + start, rows)
                    below = jnp.where(odd, inside_ref[half, :], cross_ref[half, :])
                    value = jnp.where(column < before, below, value)
                out_ref[pl.ds(place * BCELLS + start, rows), :] = value
            last = now
        return carry

    lax.fori_loop(0, BCELLS // rows, body, 0)


def diagonal_kernel(counts_ref, before_ref, old_ref, cross_ref, inside_ref, out_ref, turned_ref):
    assemble(counts_ref, before_ref[0], old_ref, cross_ref, inside_ref, out_ref, turned_ref)


def prepare_kernel(inverse_ref, split_ref, theta_ref):
    inverse = inverse_ref[...]
    size = jnp.abs(inverse)
    by_row = jnp.max(jnp.sum(size, axis=1, keepdims=True), axis=0, keepdims=True)
    by_column = jnp.max(jnp.sum(size, axis=0, keepdims=True), axis=1, keepdims=True)
    bound = 14.5 * jnp.sqrt(by_row) * jnp.sqrt(by_column)
    scale = jnp.full((1, 1), 0.5, F32)
    for power in (64, 32, 16, 8, 4, 2, 1):
        large = bound >= 2.0**power
        bound = jnp.where(large, bound * 2.0**-power, bound)
        scale = jnp.where(large, scale * 2.0**-power, scale)
    for power in (64, 32, 16, 8, 4, 2, 1):
        small = bound < 2.0**-power
        bound = jnp.where(small, bound * 2.0**power, bound)
        scale = jnp.where(small, scale * 2.0**power, scale)
    scaled = inverse * scale
    high = scaled.astype(jnp.bfloat16)
    split_ref[:, 0:BCELLS] = high
    split_ref[:, BCELLS : 2 * BCELLS] = high
    split_ref[:, 2 * BCELLS : 3 * BCELLS] = (scaled - high.astype(F32)).astype(jnp.bfloat16)
    row = lax.broadcasted_iota(jnp.int32, (BCELLS, BCELLS), 0)
    column = lax.broadcasted_iota(jnp.int32, (BCELLS, BCELLS), 1)
    theta_ref[0] = jnp.sum(jnp.where(row == column, scaled, 0.0)) * (6.5 / BCELLS)


def precondition(split_ref, field_ref, out_ref):
    def body(step, carry):
        base = pl.multiple_of(step * (2 * BCELLS), 2 * BCELLS)
        halves = [pl.ds(base + half * BCELLS, BCELLS) for half in range(2)]
        field = jnp.concatenate([field_ref[half, :] for half in halves], axis=1)
        top = field.astype(jnp.bfloat16)
        rest = (field - top.astype(F32)).astype(jnp.bfloat16)
        stacked = jnp.concatenate([top, rest, top], axis=0)
        found = jnp.dot(split_ref[...], stacked, preferred_element_type=F32)
        out_ref[halves[0], :] = found[:, :LANES]
        out_ref[halves[1], :] = found[:, LANES:]
        return carry

    lax.fori_loop(0, CHUNKS // 2, body, 0)


def split_ends(field_ref, first_ref, last_ref):
    first_ref[...] = field_ref[pl.ds(0, CHUNKS * FACE, stride=BE), :]
    last_ref[...] = field_ref[pl.ds(BE - 1, CHUNKS * FACE, stride=BE), :]


def layer_tile(field_ref, ends, which, part, chunk):
    if which >= 4:
        row = chunk * FACE + part * SUB
        return ends[which - 4][row : row + SUB, :]
    row = (part * BE, (BE - 1) * FACE + part * BE, part * FACE, part * FACE + (BE - 1) * BE)[which]
    row = row + chunk * BCELLS
    return field_ref[row : row + SUB, :]


def pack(field_ref, ends, send_ref, odd, cross_ref, inside_ref):
    for cross, out_ref in ((True, cross_ref), (False, inside_ref)):
        for step in range(HMAX // LANES):
            at = slice(step * LANES, (step + 1) * LANES)
            low, high = send_ref[0:1, at], send_ref[1:2, at]
            code = jnp.where(odd, high, low) if cross else jnp.where(odd, low, high)
            code = jnp.broadcast_to(code, (SUB, LANES))
            lane = code & (LANES - 1)
            tile = code >> 7
            found = [jnp.zeros((SUB, LANES), F32) for _ in range(8)]
            for which in range(6):
                for source in range(CHUNKS):
                    here = tile == which * CHUNKS + source
                    for part in range(8):
                        values = layer_tile(field_ref, ends, which, part, source)
                        found[part] = jnp.where(here, pick(values, lane), found[part])
            for part in range(8):
                row = step * FACE + part * SUB
                out_ref[row : row + SUB, :] = found[part]


def put_layers(which, found, half, faces_ref, ends_ref):
    for part in range(8):
        if which < 4:
            base = (half * 4 + which) * FACE + part * SUB
            faces_ref[base : base + SUB, :] = found[part]
        else:
            base = half * BCELLS + part * FACE + (which - 4) * (BE - 1)
            ends_ref[pl.ds(base, SUB, stride=BE), :] = found[part]


def gather_layers(step, codes_ref, first_code, flip, count, source_tile, faces_ref, ends_ref):
    pending = None
    for half in range(PAIR):
        at = lanes((step * PAIR + half) * LANES)
        for which in range(6):
            code = jnp.broadcast_to(codes_ref[which : which + 1, at], (SUB, LANES))
            code = code - first_code(which)
            lane = code & (LANES - 1)
            tile = code >> 7
            if flip is not None:
                tile = tile ^ flip
            found = [jnp.zeros((SUB, LANES), F32) for _ in range(8)]
            for source in range(count):
                here = tile == source
                for part in range(8):
                    values = source_tile(which, part, source)
                    found[part] = jnp.where(here, pick(values, lane), found[part])
            if pending is not None:
                put_layers(*pending, faces_ref, ends_ref)
            pending = (which, found, half)
    put_layers(*pending, faces_ref, ends_ref)


def layer(faces_ref, half, which, part):
    base = (half * 4 + which) * FACE + part * SUB
    return faces_ref[base : base + SUB, :]


def local_kernel(known, theta_ref, codes_ref, diagonal_ref, field_ref, *refs):
    basis = refs[:known]
    gram_in = refs[known][...] if known > 1 else jnp.zeros((SUB, LANES), F32)
    out_ref, gram_ref, first_ref, last_ref, faces_ref, ends_ref, sums_ref = refs[-7:]
    split_ends(field_ref, first_ref, last_ref)
    ends = (first_ref, last_ref)
    cell = lax.broadcasted_iota(jnp.int32, (SUB, LANES), 0)
    theta = theta_ref[0]
    sums_ref[...] = jnp.zeros_like(sums_ref)

    def source_tile(which, part, source):
        return layer_tile(field_ref, ends, which ^ 1, part, source)

    def body(step, carry):
        gather_layers(
            step, codes_ref, lambda which: (which ^ 1) * BDEV, None, CHUNKS, source_tile,
            faces_ref, ends_ref,
        )
        sums = [jnp.zeros((SUB, LANES), F32) for _ in range(known)]
        for half in range(PAIR):
            start = pl.multiple_of((step * PAIR + half) * BCELLS, BCELLS)

            def block(i, j):
                return field_ref[pl.ds(start + (i * BE + j) * BE, SUB), :]

            for i in range(BE):
                for j in range(BE):
                    row = (i * BE + j) * BE
                    rows = pl.ds(start + row, SUB)
                    here = block(i, j)
                    edge = ends_ref[half * BCELLS + row : half * BCELLS + row + SUB, :]
                    beside = block(i - 1, j) if i > 0 else layer(faces_ref, half, 0, j)
                    beside = beside + (
                        block(i + 1, j) if i < BE - 1 else layer(faces_ref, half, 1, j)
                    )
                    beside = beside + (block(i, j - 1) if j > 0 else layer(faces_ref, half, 2, i))
                    beside = beside + (
                        block(i, j + 1) if j < BE - 1 else layer(faces_ref, half, 3, i)
                    )
                    beside = beside + jnp.where(cell == 0, edge, pltpu.roll(here, 1, 0))
                    beside = beside + jnp.where(cell == BE - 1, edge, pltpu.roll(here, BE - 1, 0))
                    newest = basis[-1][rows, :]
                    value = (6.0 + diagonal_ref[rows, :]) * here - beside
                    out_ref[rows, :] = value - theta * newest
                    for k, ref in enumerate(basis):
                        old = newest if k == known - 1 else ref[rows, :]
                        sums[k] = sums[k] + newest * old
        for k, part in enumerate(sums):
            sums_ref[k] += part
        return carry

    lax.fori_loop(0, CHUNKS // PAIR, body, 0)
    place_sums(sums_ref, known, gram_in, gram_ref, (known - 1) * known // 2)


def finish(odd, codes_ref, cross_ref, inside_ref, partial_ref, basis, out_ref, faces_ref, ends_ref, sums_ref):
    cell = lax.broadcasted_iota(jnp.int32, (SUB, LANES), 0)
    is_end = (cell == 0) | (cell == BE - 1)
    if basis:
        sums_ref[...] = jnp.zeros_like(sums_ref)

    def source_tile(which, part, source):
        from_ref = cross_ref if source < HMAX // LANES else inside_ref
        base = source % (HMAX // LANES) * FACE + part * SUB
        return from_ref[base : base + SUB, :]

    def body(step, carry):
        gather_layers(
            step, codes_ref, lambda which: REMOTE, odd * 2, 2 * HMAX // LANES, source_tile,
            faces_ref, ends_ref,
        )
        sums = [jnp.zeros((SUB, LANES), F32) for _ in range(len(basis) + 1)]
        for half in range(PAIR):
            start = pl.multiple_of((step * PAIR + half) * BCELLS, BCELLS)
            for i in range(BE):
                for j in range(BE):
                    row = (i * BE + j) * BE
                    rows = pl.ds(start + row, SUB)
                    edge = ends_ref[half * BCELLS + row : half * BCELLS + row + SUB, :]
                    value = partial_ref[rows, :] - jnp.where(is_end, edge, 0.0)
                    if i == 0:
                        value = value - layer(faces_ref, half, 0, j)
                    if i == BE - 1:
                        value = value - layer(faces_ref, half, 1, j)
                    if j == 0:
                        value = value - layer(faces_ref, half, 2, i)
                    if j == BE - 1:
                        value = value - layer(faces_ref, half, 3, i)
                    out_ref[rows, :] = value
                    if basis:
                        for k, ref in enumerate(basis):
                            sums[k] = sums[k] + value * ref[rows, :]
                        sums[-1] = sums[-1] + value * value
        if basis:
            for k, part in enumerate(sums):
                sums_ref[k] += part
        return carry

    lax.fori_loop(0, CHUNKS // PAIR, body, 0)


def place_sums(sums_ref, count, gram_in, gram_out_ref, first):
    lane = lax.broadcasted_iota(jnp.int32, (SUB, LANES), 1)
    row = gram_in
    for k in range(count):
        row = row + jnp.where(lane == first + k, jnp.sum(sums_ref[k]), 0.0)
    for start in range(0, gram_out_ref.shape[0], SUB):
        gram_out_ref[start : start + SUB, :] = row


def first_kernel(
    counts_ref, old_ref, cross_ref, inside_ref, split_ref, send_ref,
    before_ref, rhs_ref, field_ref, to_cross_ref, to_inside_ref,
    turned_ref, first_ref, last_ref,
):
    odd = counts_ref[3] == 1
    before = count_before(odd, cross_ref, inside_ref)
    before_ref[0] = before
    assemble(counts_ref, before, old_ref, cross_ref, inside_ref, rhs_ref, turned_ref)
    precondition(split_ref, rhs_ref, field_ref)
    split_ends(field_ref, first_ref, last_ref)
    pack(field_ref, (first_ref, last_ref), send_ref, odd, to_cross_ref, to_inside_ref)


def next_kernel(
    counts_ref, codes_ref, cross_ref, inside_ref, partial_ref, split_ref, send_ref,
    out_ref, next_ref, to_cross_ref, to_inside_ref,
    first_ref, last_ref, faces_ref, ends_ref,
):
    odd = counts_ref[3]
    finish(
        odd, codes_ref, cross_ref, inside_ref, partial_ref, (), out_ref, faces_ref, ends_ref, None
    )
    precondition(split_ref, out_ref, next_ref)
    split_ends(next_ref, first_ref, last_ref)
    pack(next_ref, (first_ref, last_ref), send_ref, odd == 1, to_cross_ref, to_inside_ref)


def end_kernel(counts_ref, codes_ref, cross_ref, inside_ref, partial_ref, gram_in_ref, *refs):
    basis = refs[: BASIS - 1]
    out_ref, gram_ref, faces_ref, ends_ref, sums_ref = refs[BASIS - 1 :]
    finish(
        counts_ref[3], codes_ref, cross_ref, inside_ref, partial_ref, basis, out_ref, faces_ref,
        ends_ref, sums_ref,
    )
    place_sums(sums_ref, BASIS, gram_in_ref[...], gram_ref, BASIS * (BASIS - 1) // 2)


def recurrence(gram, theta):
    def dot(left, right):
        total = None
        for a, x in enumerate(left):
            if x is None:
                continue
            part = None
            for b, y in enumerate(right):
                if y is not None:
                    term = gram[max(a, b)][min(a, b)] * y
                    part = term if part is None else part + term
            total = x * part if total is None else total + x * part
        return total

    def add(left, right):
        return [
            y if x is None else x if y is None else x + y for x, y in zip(left, right)
        ]

    def times(factor, vector):
        return [None if x is None else factor * x for x in vector]

    def apply(vector):
        return add([None] + vector[:-1], times(theta, vector))

    one = jnp.ones_like(theta)
    shadow = [one] + [None] * (BASIS - 1)
    residual = shadow
    direction = residual
    rho = gram[0][0]
    rho_next = rho
    total = [None] * BASIS
    along = alpha = omega = None
    for step in range(ITERS):
        if step > 0:
            beta = (rho_next / rho) * (alpha / omega)
            rho = rho_next
            direction = add(residual, times(beta, add(direction, times(-omega, along))))
        along = apply(direction)
        alpha = rho / dot(shadow, along)
        middle = add(residual, times(-alpha, along))
        image = apply(middle)
        omega = dot(image, middle) / dot(image, image)
        total = add(total, add(times(alpha, direction), times(omega, middle)))
        residual = add(middle, times(-omega, image))
        rho_next = dot(shadow, residual)
    return total, residual


def last_kernel(theta_ref, gathered_ref, *refs):
    basis = refs[:BASIS]
    fields = refs[BASIS : 2 * BASIS - 1]
    outs = refs[2 * BASIS - 1 : 2 * BASIS + 1]
    solution_ref, residual_ref, sems = refs[2 * BASIS + 1 :]
    row = jnp.sum(gathered_ref[...], axis=0, keepdims=True)
    lane = lax.broadcasted_iota(jnp.int32, (1, LANES), 1)

    def entry(k):
        return jnp.sum(jnp.where(lane == k, row, 0.0), axis=1, keepdims=True)

    gram = [[entry(a * (a + 1) // 2 + b) for b in range(a + 1)] for a in range(BASIS)]
    theta = jnp.full((1, 1), theta_ref[0])
    total, residual = recurrence(gram, theta)
    total = [None if x is None else jnp.broadcast_to(x, (SUB, LANES)) for x in total]
    residual = [jnp.broadcast_to(x, (SUB, LANES)) for x in residual]
    part = BCELLS // PARTS
    copies = []
    for block in range(PARTS):

        def body(step, carry, block=block):
            start = pl.multiple_of(block * part + step * SUB, SUB)
            for chunk in range(CHUNKS):
                rows = pl.ds(chunk * BCELLS + start, SUB)
                at = slice(chunk * LANES, (chunk + 1) * LANES)
                value = total[0] * fields[0][rows, :]
                for k in range(1, BASIS - 1):
                    value = value + total[k] * fields[k][rows, :]
                solution_ref[pl.ds(start, SUB), at] = value
                value = residual[0] * basis[0][rows, :]
                for k in range(1, BASIS):
                    value = value + residual[k] * basis[k][rows, :]
                residual_ref[pl.ds(start, SUB), at] = value
            return carry

        lax.fori_loop(0, part // SUB, body, 0, unroll=4)
        for k, ref in enumerate((solution_ref, residual_ref)):
            at = slice(block * part, (block + 1) * part)
            copies.append(
                pltpu.make_async_copy(ref.at[at, :], outs[k].at[at, :], sems.at[k, block])
            )
            copies[-1].start()
    for copy in copies:
        copy.wait()


def per_device(rhs_old, diagonal_old, new_owner, face_source, send_layers, block_inverse):
    def of(rows):
        return jax.ShapeDtypeStruct((rows, LANES), F32)

    field_type = of(CHUNKS * BCELLS)
    out_type = jax.ShapeDtypeStruct((BCELLS, BDEV), F32)
    halo_type = of(2 * FACE)
    split_type = jax.ShapeDtypeStruct((BCELLS, 3 * BCELLS), jnp.bfloat16)
    turned = pltpu.VMEM((2, 64, LANES), F32)
    end_layers = [pltpu.VMEM((CHUNKS * FACE, LANES), F32)] * 2
    layers = [pltpu.VMEM((PAIR * 4 * FACE, LANES), F32), pltpu.VMEM((PAIR * BCELLS, LANES), F32)]
    sums = pltpu.VMEM((BASIS, SUB, LANES), F32)

    rank = lax.axis_index(AXES).astype(jnp.int32).reshape(1)
    counts, cross, inside = call(
        front_kernel,
        (jax.ShapeDtypeStruct((4,), jnp.int32), of(2 * BCELLS + SUB), of(2 * BCELLS + SUB)),
        (rank, new_owner.reshape(CAP // LANES, LANES), rhs_old),
        [SMEM, HBM, HBM],
        (SMEM, VMEM, VMEM),
        [
            pltpu.VMEM((CAP // LANES, LANES), jnp.int32),
            pltpu.VMEM((BCELLS, MOVE), F32),
            pltpu.VMEM((BCELLS, 3 * LANES), F32),
            pltpu.SemaphoreType.DMA((3,)),
        ],
        limit=58,
    )
    rhs_cross = swapped(cross, True)
    rhs_inside = swapped(inside, False)
    cross, inside = call(
        cut_kernel,
        (of(2 * BCELLS), of(2 * BCELLS)),
        (counts, diagonal_old),
        [SMEM, VMEM],
        (VMEM, VMEM),
    )
    diagonal_cross = swapped(cross, True)
    diagonal_inside = swapped(inside, False)
    split, theta = call(
        prepare_kernel,
        (split_type, jax.ShapeDtypeStruct((1,), F32)),
        (block_inverse,),
        [VMEM],
        (VMEM, SMEM),
    )
    before, rhs, field, to_cross, to_inside = call(
        first_kernel,
        (jax.ShapeDtypeStruct((1,), jnp.int32),)
        + (field_type, field_type, halo_type, halo_type),
        (counts, rhs_old, rhs_cross, rhs_inside, split, send_layers),
        [SMEM] + [VMEM] * 5,
        (SMEM,) + (VMEM,) * 4,
        [turned] + end_layers,
        flops=10**9,
        bytes_accessed=8 * MIB,
    )
    diagonal = gram = None
    basis = [rhs]
    fields = [field]
    for known in range(1, BASIS):
        from_cross = swapped(to_cross, True)
        from_inside = swapped(to_inside, False)
        if diagonal is None:
            diagonal = call(
                diagonal_kernel,
                field_type,
                (counts, before, diagonal_old, diagonal_cross, diagonal_inside),
                [SMEM, SMEM] + [VMEM] * 3,
                VMEM,
                [turned],
                bytes_accessed=6 * MIB,
            )
        args = [theta, face_source, diagonal, field] + basis + ([gram] if known > 1 else [])
        partial, gram = call(
            functools.partial(local_kernel, known),
            (field_type, of(SUB)),
            tuple(args),
            [SMEM] + [VMEM] * (len(args) - 1),
            (VMEM, VMEM),
            end_layers + layers + [sums],
            flops=10**9,
            bytes_accessed=4 * MIB,
        )
        if known < BASIS - 1:
            value, field, to_cross, to_inside = call(
                next_kernel,
                (field_type, field_type, halo_type, halo_type),
                (counts, face_source, from_cross, from_inside, partial, split, send_layers),
                [SMEM] + [VMEM] * 6,
                (VMEM,) * 4,
                end_layers + layers,
                flops=10**9,
                bytes_accessed=12 * MIB,
            )
            fields.append(field)
        else:
            value, copies = call(
                end_kernel,
                (field_type, of(lax.axis_size(AXES))),
                (counts, face_source, from_cross, from_inside, partial, gram, *basis),
                [SMEM] + [VMEM] * (5 + len(basis)),
                (VMEM, VMEM),
                layers + [sums],
                limit=32,
                flops=10**9,
                bytes_accessed=12 * MIB,
            )
        basis.append(value)
    gathered = lax.all_to_all(copies, AXES, split_axis=0, concat_axis=0, tiled=True)
    return call(
        last_kernel,
        (out_type, out_type),
        (theta, gathered, *basis, *fields),
        [SMEM] + [VMEM] * (2 * BASIS),
        (HBM, HBM),
        [pltpu.VMEM((BCELLS, BDEV), F32)] * 2 + [pltpu.SemaphoreType.DMA((2, PARTS))],
        limit=32,
    )


def solution(mesh):
    return jax.shard_map(
        per_device,
        mesh=mesh,
        in_specs=(
            P(None, AXES),
            P(None, AXES),
            P(AXES),
            P(None, AXES),
            P(None, AXES),
            P(),
        ),
        out_specs=(P(None, AXES), P(None, AXES)),
        check_vma=False,
    )
```

```python
import functools

import jax
import jax.numpy as jnp
from jax import lax
from jax.experimental import pallas as pl
from jax.experimental.pallas import tpu as pltpu
from jax.sharding import PartitionSpec as P

BE = 8
BCELLS = 512
FACE = 64
BDEV = 1024
MOVE = 256
CAP = 1536
HMAX = 256
ITERS = 2
LANES = 128
SUB = 8
CHUNKS = BDEV // LANES
AXES = ("gx", "gy", "gz")
REMOTE = 6 * BDEV
BASIS = 2 * ITERS + 1
MIB = 1024 * 1024
PARTS = 8
PAIR = 2
FRONT = 52
PRODUCT = (0, 4, 5)
F32 = jnp.float32

VMEM = pl.BlockSpec(memory_space=pltpu.VMEM)
SMEM = pl.BlockSpec(memory_space=pltpu.SMEM)
HBM = pl.BlockSpec(memory_space=pltpu.HBM)


def swapped(value, cross):
    count = lax.axis_size(AXES)
    first = 1 if cross else 0
    pairs = [(low, low + 1) for low in range(first, count - 1, 2)]
    return lax.ppermute(value, AXES, pairs + [(high, low) for low, high in pairs])


def call(kernel, outs, args, in_specs, out_specs, scratch=(), limit=16, flops=0, bytes_accessed=0, aliases=None):
    if aliases is None:
        aliases = {}
    return pl.pallas_call(
        kernel,
        out_shape=outs,
        in_specs=in_specs,
        out_specs=out_specs,
        scratch_shapes=list(scratch),
        input_output_aliases=aliases,
        compiler_params=pltpu.CompilerParams(vmem_limit_bytes=limit * MIB),
        cost_estimate=pl.CostEstimate(
            flops=flops, bytes_accessed=bytes_accessed, transcendentals=0
        ),
    )(*args)


def lane_iota(rows=SUB):
    return lax.broadcasted_iota(jnp.int32, (rows, LANES), 1)


def lanes(start):
    return pl.ds(pl.multiple_of(start, LANES), LANES)


def pick(values, index):
    return jnp.take_along_axis(values, index, axis=1, mode="promise_in_bounds")


def cut_rows(start, low_ref, high_ref, odd, count, cross_ref, inside_ref):
    tile = start >> 7
    shift = start & (LANES - 1)
    rows = 128

    for step in range(BCELLS // rows):
        at = slice(step * rows, (step + 1) * rows)
        first = lane_iota(rows) < LANES - shift
        turned = []
        for part in range(3):
            source = jnp.minimum(tile + part, high_ref.shape[1] // LANES - 1) * LANES
            turned.append(pltpu.roll(high_ref[at, lanes(source)], (LANES - shift) & (LANES - 1), 1))
        for half in range(2):
            lower = low_ref[at, half * LANES : (half + 1) * LANES]
            upper = jnp.where(first, turned[half], turned[half + 1])
            to = slice(half * BCELLS + step * rows, half * BCELLS + (step + 1) * rows)
            cross_ref[to, :] = jnp.where(odd, upper, lower)
            inside_ref[to, :] = jnp.where(odd, lower, upper)
    if count is not None:
        row = jnp.full((SUB, LANES), count.astype(F32))
        cross_ref[2 * BCELLS : 2 * BCELLS + SUB, :] = row
        inside_ref[2 * BCELLS : 2 * BCELLS + SUB, :] = row


def front_kernel(
    rank_ref, owner_ref, old_ref, counts_ref, cross_ref, inside_ref, low_ref, high_ref, sems
):
    high_copy = pltpu.make_async_copy(
        old_ref.at[:, pl.ds(2 * MOVE, CAP - 2 * MOVE)], high_ref, sems.at[1]
    )
    high_copy.start()
    low_copy = pltpu.make_async_copy(old_ref.at[:, pl.ds(0, MOVE)], low_ref, sems.at[0])
    low_copy.start()
    rank = rank_ref[0]
    owner = owner_ref[...]
    filled = owner >= 0
    head = jnp.sum(((owner == rank - 1) & filled).astype(jnp.int32))
    stay = jnp.sum((owner == rank).astype(jnp.int32))
    tail = jnp.sum(((owner == rank + 1) & filled).astype(jnp.int32))
    odd = rank & 1
    row = lax.broadcasted_iota(jnp.int32, (SUB, LANES), 0)
    counts_ref[...] = jnp.where(
        row == 0, head, jnp.where(row == 1, stay, jnp.where(row == 2, tail, odd))
    )
    high_copy.wait()
    low_copy.wait()
    start = head + stay - 2 * MOVE
    cut_rows(start, low_ref, high_ref, odd == 1, tail, cross_ref, inside_ref)


def count_of(counts_ref, row):
    return jnp.max(counts_ref[row : row + 1, :])


def cut_kernel(counts_ref, old_ref, cross_ref, inside_ref):
    start = count_of(counts_ref, 0) + count_of(counts_ref, 1)
    odd = count_of(counts_ref, 3) == 1
    cut_rows(start, old_ref, old_ref, odd, None, cross_ref, inside_ref)


def count_before(odd, cross_ref, inside_ref):
    row = slice(2 * BCELLS, 2 * BCELLS + SUB)
    return jnp.max(jnp.where(odd, inside_ref[row, :], cross_ref[row, :])).astype(jnp.int32)


def assemble(counts_ref, before, old_ref, cross_ref, inside_ref, out_ref, turned_ref):
    head = count_of(counts_ref, 0)
    stay = count_of(counts_ref, 1)
    odd = count_of(counts_ref, 3) == 1
    own_start = head - before
    own_tile = own_start >> 7
    own_shift = own_start & (LANES - 1)
    up_start = -(before + stay)
    up_tile = up_start >> 7
    up_shift = up_start & (LANES - 1)
    rows = 64

    def body(step, carry):
        start = pl.multiple_of(step * rows, rows)
        at = pl.ds(start, rows)
        lane = lane_iota(rows)
        for part in range(2):
            half = pl.ds(part * BCELLS + start, rows)
            turned_ref[part] = pltpu.roll(
                jnp.where(odd, cross_ref[half, :], inside_ref[half, :]),
                (LANES - up_shift) & (LANES - 1),
                1,
            )
        last = None
        for chunk in range(CHUNKS + 1):
            source = jnp.clip(own_tile + chunk, 0, CAP // LANES - 1) * LANES
            now = pltpu.roll(
                old_ref[at, lanes(source)], (LANES - own_shift) & (LANES - 1), 1
            )
            if chunk > 0:
                place = chunk - 1
                column = lane + place * LANES
                own = jnp.where(lane < LANES - own_shift, last, now)
                low_half = turned_ref[jnp.clip(up_tile + place, 0, 1)]
                high_half = turned_ref[jnp.clip(up_tile + place + 1, 0, 1)]
                above = jnp.where(lane < LANES - up_shift, low_half, high_half)
                value = jnp.where(column < before + stay, own, above)
                if place < MOVE // LANES:
                    half = pl.ds(place * BCELLS + start, rows)
                    below = jnp.where(odd, inside_ref[half, :], cross_ref[half, :])
                    value = jnp.where(column < before, below, value)
                out_ref[pl.ds(place * BCELLS + start, rows), :] = value
            last = now
        return carry

    lax.fori_loop(0, BCELLS // rows, body, 0)


def diagonal_kernel(counts_ref, before_ref, old_ref, cross_ref, inside_ref, out_ref, turned_ref):
    assemble(counts_ref, before_ref[0], old_ref, cross_ref, inside_ref, out_ref, turned_ref)


def prepare_kernel(
    rank_ref, inverse_ref, codes_ref, send_ref, split_ref, theta_ref, sent_ref, taken_ref, local_ref
):
    select(rank_ref[0] & 1, codes_ref, send_ref, sent_ref, taken_ref, local_ref)
    inverse = inverse_ref[...]
    size = jnp.abs(inverse)
    by_row = jnp.max(jnp.sum(size, axis=1, keepdims=True), axis=0, keepdims=True)
    by_column = jnp.max(jnp.sum(size, axis=0, keepdims=True), axis=1, keepdims=True)
    bound = 14.5 * jnp.sqrt(by_row) * jnp.sqrt(by_column)
    scale = jnp.full((1, 1), 0.5, F32)
    for power in (64, 32, 16, 8, 4, 2, 1):
        large = bound >= 2.0**power
        bound = jnp.where(large, bound * 2.0**-power, bound)
        scale = jnp.where(large, scale * 2.0**-power, scale)
    for power in (64, 32, 16, 8, 4, 2, 1):
        small = bound < 2.0**-power
        bound = jnp.where(small, bound * 2.0**power, bound)
        scale = jnp.where(small, scale * 2.0**power, scale)
    scaled = inverse * scale
    high = scaled.astype(jnp.bfloat16)
    split_ref[:, 0:BCELLS] = high
    split_ref[:, BCELLS : 2 * BCELLS] = high
    split_ref[:, 2 * BCELLS : 3 * BCELLS] = (scaled - high.astype(F32)).astype(jnp.bfloat16)
    row = lax.broadcasted_iota(jnp.int32, (BCELLS, BCELLS), 0)
    column = lax.broadcasted_iota(jnp.int32, (BCELLS, BCELLS), 1)
    theta_ref[0] = jnp.sum(jnp.where(row == column, scaled, 0.0)) * (6.5 / BCELLS)


def precondition(split_ref, field_ref, out_ref, pair):
    base = pair * 2 * BCELLS
    field = jnp.concatenate(
        [field_ref[base + half * BCELLS : base + (half + 1) * BCELLS, :] for half in range(2)],
        axis=1,
    )
    top = field.astype(jnp.bfloat16)
    rest = (field - top.astype(F32)).astype(jnp.bfloat16)
    stacked = jnp.concatenate([top, rest, top], axis=0)
    found = jnp.dot(split_ref[...], stacked, preferred_element_type=F32)
    out_ref[base : base + BCELLS, :] = found[:, :LANES]
    out_ref[base + BCELLS : base + 2 * BCELLS, :] = found[:, LANES:]


def one_hot(code, out_ref, column):
    rows = 128
    width = code.shape[1]
    base = lax.broadcasted_iota(jnp.int32, (rows, width), 0).astype(jnp.int16)
    one = jnp.ones((rows, width), jnp.bfloat16)
    zero = jnp.zeros((rows, width), jnp.bfloat16)

    def body(step, carry):
        start = pl.multiple_of(step * rows, rows)
        here = base == jnp.broadcast_to((code - start).astype(jnp.int16), (rows, width))
        out_ref[pl.ds(start, rows), column : column + width] = jnp.where(here, one, zero)
        return carry

    lax.fori_loop(0, out_ref.shape[0] // rows, body, 0)


def select(odd, codes_ref, send_ref, sent_ref, taken_ref, local_ref):
    low, high = send_ref[0:1, :], send_ref[1:2, :]
    one_hot(jnp.where(odd == 1, high, low), sent_ref, 0)
    one_hot(jnp.where(odd == 1, low, high), sent_ref, HMAX)
    for which in range(6):
        code = codes_ref[which : which + 1, :]
        for half in range(2):
            part = code[:, half * BCELLS : (half + 1) * BCELLS]
            at = which * BDEV + half * BCELLS
            one_hot((part - REMOTE) ^ (odd * HMAX), taken_ref, at)
            if which in PRODUCT:
                at = PRODUCT.index(which) * BDEV + half * BCELLS
                one_hot(part - (which ^ 1) * BDEV, local_ref, at)


def halves(value):
    top = value.astype(jnp.bfloat16)
    return jnp.concatenate([top, (value - top.astype(F32)).astype(jnp.bfloat16)], axis=0)


def whole_layer(field_ref, which, chunk):
    start = chunk * BCELLS
    if which >= 4:
        return field_ref[pl.ds(start + (which - 4) * (BE - 1), FACE, stride=BE), :]
    if which < 2:
        row = start + which * (BE - 1) * FACE
        return field_ref[row : row + FACE, :]
    rows = [start + part * FACE + (which - 2) * (BE - 1) * BE for part in range(BE)]
    return jnp.concatenate([field_ref[row : row + SUB, :] for row in rows], axis=0)


def split_layers(field_ref, chunk, layers_ref):
    for which in range(6):
        at = (which * CHUNKS + chunk) * LANES
        layers_ref[:, at : at + LANES] = halves(whole_layer(field_ref, which, chunk))


def pack(layers_ref, sent_ref, cross_ref, inside_ref):
    for out_ref, start in ((cross_ref, 0), (inside_ref, HMAX)):
        found = jnp.dot(
            layers_ref[...], sent_ref[:, start : start + HMAX], preferred_element_type=F32
        )
        found = found[:FACE, :] + found[FACE:, :]
        out_ref[0:FACE, :] = found[:, :LANES]
        out_ref[FACE : 2 * FACE, :] = found[:, LANES:]


def layer_tile(field_ref, which, part, chunk):
    row = (part * BE, (BE - 1) * FACE + part * BE, part * FACE, part * FACE + (BE - 1) * BE)[which]
    row = row + chunk * BCELLS
    return field_ref[row : row + SUB, :]


def layer(faces_ref, half, which, part):
    base = (half * 6 + which) * FACE + part * SUB
    return faces_ref[base : base + SUB, :]


def gather_layers(step, codes_ref, field_ref, layers_ref, local_ref, faces_ref):
    for index, which in enumerate(PRODUCT):
        at = index * BDEV + step * (2 * LANES)
        start = (which ^ 1) * BDEV
        found = jnp.dot(
            layers_ref[:, start : start + BDEV],
            local_ref[:, pl.ds(pl.multiple_of(at, 2 * LANES), 2 * LANES)],
            preferred_element_type=F32,
        )
        found = found[:FACE, :] + found[FACE:, :]
        for half in range(PAIR):
            base = (half * 6 + which) * FACE
            faces_ref[base : base + FACE, :] = found[:, half * LANES : (half + 1) * LANES]
    for half in range(PAIR):
        at = lanes((step * PAIR + half) * LANES)
        for which in range(6):
            if which in PRODUCT:
                continue
            partner = which ^ 1
            code = jnp.broadcast_to(codes_ref[which : which + 1, at], (SUB, LANES))
            code = code - partner * BDEV
            lane = code & (LANES - 1)
            tile = code >> 7
            found = [jnp.zeros((SUB, LANES), F32) for _ in range(8)]
            for source in range(CHUNKS):
                here = tile == source
                for part in range(8):
                    values = layer_tile(field_ref, partner, part, source)
                    found[part] = jnp.where(here, pick(values, lane), found[part])
            for part in range(8):
                base = (half * 6 + which) * FACE + part * SUB
                faces_ref[base : base + SUB, :] = found[part]


def local_kernel(
    known, theta_ref, codes_ref, diagonal_ref, field_ref, layers_ref, local_ref, *refs
):
    basis = refs[:known]
    gram_in = refs[known][...] if known > 1 else jnp.zeros((SUB, LANES), F32)
    out_ref, gram_ref, faces_ref, beside_ref, sums_ref = refs[-5:]
    theta = theta_ref[0]
    sums_ref[...] = jnp.zeros_like(sums_ref)

    def body(step, carry):
        gather_layers(step, codes_ref, field_ref, layers_ref, local_ref, faces_ref)
        sums = [jnp.zeros((SUB, LANES), F32) for _ in range(known)]
        for half in range(PAIR):
            start = pl.multiple_of((step * PAIR + half) * BCELLS, BCELLS)

            def block(i, j):
                return field_ref[pl.ds(start + (i * BE + j) * BE, SUB), :]

            for i in range(BE):
                row = [layer(faces_ref, half, 4, i)]
                row += [field_ref[pl.ds(start + i * FACE + k, SUB, stride=BE), :] for k in range(BE)]
                row += [layer(faces_ref, half, 5, i)]
                for k in range(BE):
                    at = pl.ds(half * BCELLS + i * FACE + k, SUB, stride=BE)
                    beside_ref[at, :] = row[k] + row[k + 2]
            for i in range(BE):
                for j in range(BE):
                    row = (i * BE + j) * BE
                    rows = pl.ds(start + row, SUB)
                    here = block(i, j)
                    beside = beside_ref[half * BCELLS + row : half * BCELLS + row + SUB, :]
                    beside = beside + (block(i - 1, j) if i > 0 else layer(faces_ref, half, 0, j))
                    beside = beside + (
                        block(i + 1, j) if i < BE - 1 else layer(faces_ref, half, 1, j)
                    )
                    beside = beside + (block(i, j - 1) if j > 0 else layer(faces_ref, half, 2, i))
                    beside = beside + (
                        block(i, j + 1) if j < BE - 1 else layer(faces_ref, half, 3, i)
                    )
                    newest = basis[-1][rows, :]
                    value = (6.0 + diagonal_ref[rows, :]) * here - beside
                    out_ref[rows, :] = value - theta * newest
                    for k, ref in enumerate(basis):
                        old = newest if k == known - 1 else ref[rows, :]
                        sums[k] = sums[k] + newest * old
        for k, part in enumerate(sums):
            sums_ref[k] += part
        return carry

    lax.fori_loop(0, CHUNKS // PAIR, body, 0)
    place_sums(sums_ref, known, gram_in, gram_ref, (known - 1) * known // 2)


def receive(cross_ref, inside_ref):
    parts = [
        ref[part * FACE : (part + 1) * FACE, :]
        for ref in (cross_ref, inside_ref)
        for part in range(2)
    ]
    return halves(jnp.concatenate(parts, axis=1))


def finish(taken_ref, received, out_ref, pair):
    for which in range(6):
        at = which * BDEV + pair * 2 * LANES
        found = jnp.dot(received, taken_ref[:, at : at + 2 * LANES], preferred_element_type=F32)
        found = found[:FACE, :] + found[FACE:, :]
        for half in range(2):
            start = (pair * 2 + half) * BCELLS
            beside = found[:, half * LANES : (half + 1) * LANES]
            if which >= 4:
                rows = pl.ds(start + (which - 4) * (BE - 1), FACE, stride=BE)
                out_ref[rows, :] = out_ref[rows, :] - beside
            elif which < 2:
                row = start + which * (BE - 1) * FACE
                out_ref[row : row + FACE, :] = out_ref[row : row + FACE, :] - beside
            else:
                for part in range(BE):
                    row = start + part * FACE + (which - 2) * (BE - 1) * BE
                    out_ref[row : row + SUB, :] = (
                        out_ref[row : row + SUB, :] - beside[part * SUB : (part + 1) * SUB, :]
                    )


def place_sums(sums_ref, count, gram_in, gram_out_ref, first):
    lane = lax.broadcasted_iota(jnp.int32, (SUB, LANES), 1)
    row = gram_in
    for k in range(count):
        row = row + jnp.where(lane == first + k, jnp.sum(sums_ref[k]), 0.0)
    for start in range(0, gram_out_ref.shape[0], SUB):
        gram_out_ref[start : start + SUB, :] = row


def send(split_ref, value_ref, field_ref, layers_ref, sent_ref, cross_ref, inside_ref, before):
    for pair in range(CHUNKS // 2):
        before(pair)
        precondition(split_ref, value_ref, field_ref, pair)
        split_layers(field_ref, 2 * pair, layers_ref)
        split_layers(field_ref, 2 * pair + 1, layers_ref)
    pack(layers_ref, sent_ref, cross_ref, inside_ref)


def first_kernel(
    counts_ref, old_ref, cross_ref, inside_ref, split_ref, sent_ref,
    before_ref, rhs_ref, field_ref, layers_ref, to_cross_ref, to_inside_ref,
    turned_ref,
):
    odd = count_of(counts_ref, 3) == 1
    before = count_before(odd, cross_ref, inside_ref)
    before_ref[0] = before
    assemble(counts_ref, before, old_ref, cross_ref, inside_ref, rhs_ref, turned_ref)
    send(
        split_ref, rhs_ref, field_ref, layers_ref, sent_ref, to_cross_ref, to_inside_ref,
        lambda pair: None,
    )


def next_kernel(
    cross_ref, inside_ref, partial_ref, taken_ref, split_ref, sent_ref,
    out_ref, field_ref, layers_ref, to_cross_ref, to_inside_ref,
):
    del partial_ref
    received = receive(cross_ref, inside_ref)
    send(
        split_ref, out_ref, field_ref, layers_ref, sent_ref, to_cross_ref, to_inside_ref,
        lambda pair: finish(taken_ref, received, out_ref, pair),
    )


def end_kernel(cross_ref, inside_ref, partial_ref, taken_ref, gram_in_ref, *refs):
    del partial_ref
    basis = refs[: BASIS - 1]
    out_ref, gram_ref, sums_ref = refs[BASIS - 1 :]
    received = receive(cross_ref, inside_ref)
    for pair in range(CHUNKS // 2):
        finish(taken_ref, received, out_ref, pair)
    sums_ref[...] = jnp.zeros_like(sums_ref)

    def body(step, carry):
        start = pl.multiple_of(step * BCELLS, BCELLS)
        sums = [jnp.zeros((SUB, LANES), F32) for _ in range(BASIS)]
        for row in range(0, BCELLS, SUB):
            rows = pl.ds(start + row, SUB)
            value = out_ref[rows, :]
            for k, ref in enumerate(basis):
                sums[k] = sums[k] + value * ref[rows, :]
            sums[-1] = sums[-1] + value * value
        for k, part in enumerate(sums):
            sums_ref[k] += part
        return carry

    lax.fori_loop(0, CHUNKS, body, 0)
    place_sums(sums_ref, BASIS, gram_in_ref[...], gram_ref, BASIS * (BASIS - 1) // 2)


def recurrence(gram, theta):
    def dot(left, right):
        total = None
        for a, x in enumerate(left):
            if x is None:
                continue
            part = None
            for b, y in enumerate(right):
                if y is not None:
                    term = gram[max(a, b)][min(a, b)] * y
                    part = term if part is None else part + term
            total = x * part if total is None else total + x * part
        return total

    def add(left, right):
        return [
            y if x is None else x if y is None else x + y for x, y in zip(left, right)
        ]

    def times(factor, vector):
        return [None if x is None else factor * x for x in vector]

    def apply(vector):
        return add([None] + vector[:-1], times(theta, vector))

    one = jnp.ones_like(theta)
    shadow = [one] + [None] * (BASIS - 1)
    residual = shadow
    direction = residual
    rho = gram[0][0]
    rho_next = rho
    total = [None] * BASIS
    along = alpha = omega = None
    for step in range(ITERS):
        if step > 0:
            beta = (rho_next / rho) * (alpha / omega)
            rho = rho_next
            direction = add(residual, times(beta, add(direction, times(-omega, along))))
        along = apply(direction)
        alpha = rho / dot(shadow, along)
        middle = add(residual, times(-alpha, along))
        image = apply(middle)
        omega = dot(image, middle) / dot(image, image)
        total = add(total, add(times(alpha, direction), times(omega, middle)))
        residual = add(middle, times(-omega, image))
        rho_next = dot(shadow, residual)
    return total, residual


def last_kernel(theta_ref, gathered_ref, *refs):
    basis = refs[:BASIS]
    fields = refs[BASIS : 2 * BASIS - 1]
    outs = refs[2 * BASIS - 1 : 2 * BASIS + 1]
    solution_ref, residual_ref, sems = refs[2 * BASIS + 1 :]
    row = jnp.sum(gathered_ref[...], axis=0, keepdims=True)
    lane = lax.broadcasted_iota(jnp.int32, (1, LANES), 1)

    def entry(k):
        return jnp.sum(jnp.where(lane == k, row, 0.0), axis=1, keepdims=True)

    gram = [[entry(a * (a + 1) // 2 + b) for b in range(a + 1)] for a in range(BASIS)]
    theta = jnp.full((1, 1), theta_ref[0])
    total, residual = recurrence(gram, theta)
    total = [None if x is None else jnp.broadcast_to(x, (SUB, LANES)) for x in total]
    residual = [jnp.broadcast_to(x, (SUB, LANES)) for x in residual]
    part = BCELLS // PARTS
    copies = []
    for block in range(PARTS):

        def body(step, carry, block=block):
            start = pl.multiple_of(block * part + step * SUB, SUB)
            for chunk in range(CHUNKS):
                rows = pl.ds(chunk * BCELLS + start, SUB)
                at = slice(chunk * LANES, (chunk + 1) * LANES)
                value = total[0] * fields[0][rows, :]
                for k in range(1, BASIS - 1):
                    value = value + total[k] * fields[k][rows, :]
                solution_ref[pl.ds(start, SUB), at] = value
                value = residual[0] * basis[0][rows, :]
                for k in range(1, BASIS):
                    value = value + residual[k] * basis[k][rows, :]
                residual_ref[pl.ds(start, SUB), at] = value
            return carry

        lax.fori_loop(0, part // SUB, body, 0, unroll=4)
        for k, ref in enumerate((solution_ref, residual_ref)):
            at = slice(block * part, (block + 1) * part)
            copies.append(
                pltpu.make_async_copy(ref.at[at, :], outs[k].at[at, :], sems.at[k, block])
            )
            copies[-1].start()
    for copy in copies:
        copy.wait()


def per_device(rhs_old, diagonal_old, new_owner, face_source, send_layers, block_inverse):
    def of(rows):
        return jax.ShapeDtypeStruct((rows, LANES), F32)

    field_type = of(CHUNKS * BCELLS)
    out_type = jax.ShapeDtypeStruct((BCELLS, BDEV), F32)
    halo_type = of(2 * FACE)
    split_type = jax.ShapeDtypeStruct((BCELLS, 3 * BCELLS), jnp.bfloat16)
    turned = pltpu.VMEM((2, 64, LANES), F32)
    layers = [pltpu.VMEM((PAIR * 6 * FACE, LANES), F32), pltpu.VMEM((PAIR * BCELLS, LANES), F32)]
    packed_type = jax.ShapeDtypeStruct((2 * FACE, 6 * BDEV), jnp.bfloat16)
    sums = pltpu.VMEM((BASIS, SUB, LANES), F32)

    rank = lax.axis_index(AXES).astype(jnp.int32).reshape(1)
    counts, cross, inside = call(
        front_kernel,
        (
            jax.ShapeDtypeStruct((SUB, LANES), jnp.int32),
            of(2 * BCELLS + SUB),
            of(2 * BCELLS + SUB),
        ),
        (rank, new_owner.reshape(CAP // LANES, LANES), rhs_old),
        [SMEM, VMEM, HBM],
        (VMEM, VMEM, VMEM),
        [
            pltpu.VMEM((BCELLS, MOVE), F32),
            pltpu.VMEM((BCELLS, CAP - 2 * MOVE), F32),
            pltpu.SemaphoreType.DMA((2,)),
        ],
        limit=FRONT,
    )
    rhs_cross = swapped(cross, True)
    rhs_inside = swapped(inside, False)
    cross, inside = call(
        cut_kernel,
        (of(2 * BCELLS), of(2 * BCELLS)),
        (counts, diagonal_old),
        [VMEM, VMEM],
        (VMEM, VMEM),
    )
    diagonal_cross = swapped(cross, True)
    diagonal_inside = swapped(inside, False)
    split, theta, sent, taken, local = call(
        prepare_kernel,
        (
            split_type,
            jax.ShapeDtypeStruct((1,), F32),
            jax.ShapeDtypeStruct((6 * BDEV, 2 * HMAX), jnp.bfloat16),
            jax.ShapeDtypeStruct((2 * HMAX, 6 * BDEV), jnp.bfloat16),
            jax.ShapeDtypeStruct((BDEV, len(PRODUCT) * BDEV), jnp.bfloat16),
        ),
        (rank, block_inverse, face_source, send_layers),
        [SMEM] + [VMEM] * 3,
        (VMEM, SMEM, VMEM, VMEM, VMEM),
    )
    before, rhs, field, packed, to_cross, to_inside = call(
        first_kernel,
        (jax.ShapeDtypeStruct((1,), jnp.int32),)
        + (field_type, field_type, packed_type, halo_type, halo_type),
        (counts, rhs_old, rhs_cross, rhs_inside, split, sent),
        [VMEM] * 6,
        (SMEM,) + (VMEM,) * 5,
        [turned],
        flops=10**9,
        bytes_accessed=8 * MIB,
    )
    diagonal = gram = None
    basis = [rhs]
    fields = [field]
    for known in range(1, BASIS):
        from_cross = swapped(to_cross, True)
        from_inside = swapped(to_inside, False)
        if diagonal is None:
            diagonal = call(
                diagonal_kernel,
                field_type,
                (counts, before, diagonal_old, diagonal_cross, diagonal_inside),
                [VMEM, SMEM] + [VMEM] * 3,
                VMEM,
                [turned],
                bytes_accessed=6 * MIB,
            )
        args = [theta, face_source, diagonal, field, packed, local] + basis + ([gram] if known > 1 else [])
        partial, gram = call(
            functools.partial(local_kernel, known),
            (field_type, of(SUB)),
            tuple(args),
            [SMEM] + [VMEM] * (len(args) - 1),
            (VMEM, VMEM),
            layers + [sums],
            flops=10**9,
            bytes_accessed=4 * MIB,
        )
        if known < BASIS - 1:
            value, field, packed, to_cross, to_inside = call(
                next_kernel,
                (field_type, field_type, packed_type, halo_type, halo_type),
                (from_cross, from_inside, partial, taken, split, sent),
                [VMEM] * 6,
                (VMEM,) * 5,
                flops=10**9,
                bytes_accessed=12 * MIB,
                aliases={2: 0},
            )
            fields.append(field)
        else:
            value, copies = call(
                end_kernel,
                (field_type, of(lax.axis_size(AXES))),
                (from_cross, from_inside, partial, taken, gram, *basis),
                [VMEM] * (5 + len(basis)),
                (VMEM, VMEM),
                [sums],
                flops=10**9,
                bytes_accessed=12 * MIB,
                aliases={2: 0},
            )
        basis.append(value)
    gathered = lax.all_to_all(copies, AXES, split_axis=0, concat_axis=0, tiled=True)
    return call(
        last_kernel,
        (out_type, out_type),
        (theta, gathered, *basis, *fields),
        [SMEM] + [VMEM] * (2 * BASIS),
        (HBM, HBM),
        [pltpu.VMEM((BCELLS, BDEV), F32)] * 2 + [pltpu.SemaphoreType.DMA((2, PARTS))],
        limit=16,
    )


def solution(mesh):
    return jax.shard_map(
        per_device,
        mesh=mesh,
        in_specs=(
            P(None, AXES),
            P(None, AXES),
            P(AXES),
            P(None, AXES),
            P(None, AXES),
            P(),
        ),
        out_specs=(P(None, AXES), P(None, AXES)),
        check_vma=False,
    )
```

```python
import functools

import jax
import jax.numpy as jnp
from jax import lax
from jax.experimental import pallas as pl
from jax.experimental.pallas import tpu as pltpu
from jax.sharding import PartitionSpec as P

BE = 8
BCELLS = 512
FACE = 64
BDEV = 1024
MOVE = 256
CAP = 1536
HMAX = 256
ITERS = 2
LANES = 128
SUB = 8
CHUNKS = BDEV // LANES
AXES = ("gx", "gy", "gz")
REMOTE = 6 * BDEV
BASIS = 2 * ITERS + 1
MIB = 1024 * 1024
PARTS = 8
PAIR = 2
FRONT = 52
PRODUCT = (0, 4, 5)
SENT = (4, 5, 0, 3)
SPLIT = (1,) + SENT
F32 = jnp.float32

VMEM = pl.BlockSpec(memory_space=pltpu.VMEM)
SMEM = pl.BlockSpec(memory_space=pltpu.SMEM)
HBM = pl.BlockSpec(memory_space=pltpu.HBM)


def swapped(value, cross):
    count = lax.axis_size(AXES)
    first = 1 if cross else 0
    pairs = [(low, low + 1) for low in range(first, count - 1, 2)]
    return lax.ppermute(value, AXES, pairs + [(high, low) for low, high in pairs])


def call(kernel, outs, args, in_specs, out_specs, scratch=(), limit=16, flops=0, bytes_accessed=0, aliases=None):
    if aliases is None:
        aliases = {}
    return pl.pallas_call(
        kernel,
        out_shape=outs,
        in_specs=in_specs,
        out_specs=out_specs,
        scratch_shapes=list(scratch),
        input_output_aliases=aliases,
        compiler_params=pltpu.CompilerParams(vmem_limit_bytes=limit * MIB),
        cost_estimate=pl.CostEstimate(
            flops=flops, bytes_accessed=bytes_accessed, transcendentals=0
        ),
    )(*args)


def lane_iota(rows=SUB):
    return lax.broadcasted_iota(jnp.int32, (rows, LANES), 1)


def lanes(start):
    return pl.ds(pl.multiple_of(start, LANES), LANES)


def pick(values, index):
    return jnp.take_along_axis(values, index, axis=1, mode="promise_in_bounds")


def cut_rows(start, low_ref, high_ref, odd, count, cross_ref, inside_ref):
    tile = start >> 7
    shift = start & (LANES - 1)
    rows = 128

    for step in range(BCELLS // rows):
        at = slice(step * rows, (step + 1) * rows)
        first = lane_iota(rows) < LANES - shift
        turned = []
        for part in range(3):
            source = jnp.minimum(tile + part, high_ref.shape[1] // LANES - 1) * LANES
            turned.append(pltpu.roll(high_ref[at, lanes(source)], (LANES - shift) & (LANES - 1), 1))
        for half in range(2):
            lower = low_ref[at, half * LANES : (half + 1) * LANES]
            upper = jnp.where(first, turned[half], turned[half + 1])
            to = slice(half * BCELLS + step * rows, half * BCELLS + (step + 1) * rows)
            cross_ref[to, :] = jnp.where(odd, upper, lower)
            inside_ref[to, :] = jnp.where(odd, lower, upper)
    if count is not None:
        row = jnp.full((SUB, LANES), count.astype(F32))
        cross_ref[2 * BCELLS : 2 * BCELLS + SUB, :] = row
        inside_ref[2 * BCELLS : 2 * BCELLS + SUB, :] = row


def front_kernel(
    rank_ref, owner_ref, old_ref, counts_ref, cross_ref, inside_ref, low_ref, high_ref, sems
):
    high_copy = pltpu.make_async_copy(
        old_ref.at[:, pl.ds(2 * MOVE, CAP - 2 * MOVE)], high_ref, sems.at[1]
    )
    high_copy.start()
    low_copy = pltpu.make_async_copy(old_ref.at[:, pl.ds(0, MOVE)], low_ref, sems.at[0])
    low_copy.start()
    rank = rank_ref[0]
    owner = owner_ref[...]
    filled = owner >= 0
    head = jnp.sum(((owner == rank - 1) & filled).astype(jnp.int32))
    stay = jnp.sum((owner == rank).astype(jnp.int32))
    tail = jnp.sum(((owner == rank + 1) & filled).astype(jnp.int32))
    odd = rank & 1
    row = lax.broadcasted_iota(jnp.int32, (SUB, LANES), 0)
    counts_ref[...] = jnp.where(
        row == 0, head, jnp.where(row == 1, stay, jnp.where(row == 2, tail, odd))
    )
    high_copy.wait()
    low_copy.wait()
    start = head + stay - 2 * MOVE
    cut_rows(start, low_ref, high_ref, odd == 1, tail, cross_ref, inside_ref)


def count_of(counts_ref, row):
    return jnp.max(counts_ref[row : row + 1, :])


def cut_kernel(counts_ref, old_ref, cross_ref, inside_ref):
    start = count_of(counts_ref, 0) + count_of(counts_ref, 1)
    odd = count_of(counts_ref, 3) == 1
    cut_rows(start, old_ref, old_ref, odd, None, cross_ref, inside_ref)


def count_before(odd, cross_ref, inside_ref):
    row = slice(2 * BCELLS, 2 * BCELLS + SUB)
    return jnp.max(jnp.where(odd, inside_ref[row, :], cross_ref[row, :])).astype(jnp.int32)


def assemble(counts_ref, before, old_ref, cross_ref, inside_ref, out_ref, turned_ref):
    head = count_of(counts_ref, 0)
    stay = count_of(counts_ref, 1)
    odd = count_of(counts_ref, 3) == 1
    own_start = head - before
    own_tile = own_start >> 7
    own_shift = own_start & (LANES - 1)
    up_start = -(before + stay)
    up_tile = up_start >> 7
    up_shift = up_start & (LANES - 1)
    rows = 64

    def body(step, carry):
        start = pl.multiple_of(step * rows, rows)
        at = pl.ds(start, rows)
        lane = lane_iota(rows)
        for part in range(2):
            half = pl.ds(part * BCELLS + start, rows)
            turned_ref[part] = pltpu.roll(
                jnp.where(odd, cross_ref[half, :], inside_ref[half, :]),
                (LANES - up_shift) & (LANES - 1),
                1,
            )
        last = None
        for chunk in range(CHUNKS + 1):
            source = jnp.clip(own_tile + chunk, 0, CAP // LANES - 1) * LANES
            now = pltpu.roll(
                old_ref[at, lanes(source)], (LANES - own_shift) & (LANES - 1), 1
            )
            if chunk > 0:
                place = chunk - 1
                column = lane + place * LANES
                own = jnp.where(lane < LANES - own_shift, last, now)
                value = own
                if place >= 2 * MOVE // LANES:
                    low_half = turned_ref[jnp.clip(up_tile + place, 0, 1)]
                    high_half = turned_ref[jnp.clip(up_tile + place + 1, 0, 1)]
                    above = jnp.where(lane < LANES - up_shift, low_half, high_half)
                    value = jnp.where(column < before + stay, own, above)
                if place < MOVE // LANES:
                    half = pl.ds(place * BCELLS + start, rows)
                    below = jnp.where(odd, inside_ref[half, :], cross_ref[half, :])
                    value = jnp.where(column < before, below, value)
                out_ref[pl.ds(place * BCELLS + start, rows), :] = value
            last = now
        return carry

    lax.fori_loop(0, BCELLS // rows, body, 0)


def prepare_kernel(
    rank_ref, inverse_ref, codes_ref, send_ref, split_ref, theta_ref, sent_ref, taken_ref, local_ref
):
    select(rank_ref[0] & 1, codes_ref, send_ref, sent_ref, taken_ref, local_ref)
    inverse = inverse_ref[...]
    size = jnp.abs(inverse)
    by_row = jnp.max(jnp.sum(size, axis=1, keepdims=True), axis=0, keepdims=True)
    by_column = jnp.max(jnp.sum(size, axis=0, keepdims=True), axis=1, keepdims=True)
    bound = 14.5 * jnp.sqrt(by_row) * jnp.sqrt(by_column)
    scale = jnp.full((1, 1), 0.5, F32)
    for power in (64, 32, 16, 8, 4, 2, 1):
        large = bound >= 2.0**power
        bound = jnp.where(large, bound * 2.0**-power, bound)
        scale = jnp.where(large, scale * 2.0**-power, scale)
    for power in (64, 32, 16, 8, 4, 2, 1):
        small = bound < 2.0**-power
        bound = jnp.where(small, bound * 2.0**power, bound)
        scale = jnp.where(small, scale * 2.0**power, scale)
    scaled = inverse * scale
    high = scaled.astype(jnp.bfloat16)
    split_ref[:, 0:BCELLS] = high
    split_ref[:, BCELLS : 2 * BCELLS] = high
    split_ref[:, 2 * BCELLS : 3 * BCELLS] = (scaled - high.astype(F32)).astype(jnp.bfloat16)
    row = lax.broadcasted_iota(jnp.int32, (BCELLS, BCELLS), 0)
    column = lax.broadcasted_iota(jnp.int32, (BCELLS, BCELLS), 1)
    theta_ref[0] = jnp.sum(jnp.where(row == column, scaled, 0.0)) * (6.5 / BCELLS)


def precondition(split_ref, field_ref, out_ref, pair):
    base = pair * 2 * BCELLS
    field = jnp.concatenate(
        [field_ref[base + half * BCELLS : base + (half + 1) * BCELLS, :] for half in range(2)],
        axis=1,
    )
    top = field.astype(jnp.bfloat16)
    rest = (field - top.astype(F32)).astype(jnp.bfloat16)
    stacked = jnp.concatenate([top, rest, top], axis=0)
    found = jnp.dot(split_ref[...], stacked, preferred_element_type=F32)
    out_ref[base : base + BCELLS, :] = found[:, :LANES]
    out_ref[base + BCELLS : base + 2 * BCELLS, :] = found[:, LANES:]


def one_hot(code, out_ref, row, count, column):
    rows = 512
    width = code.shape[1]
    base = lax.broadcasted_iota(jnp.int32, (rows, width), 0).astype(jnp.int16)
    one = jnp.ones((rows, width), jnp.bfloat16)
    zero = jnp.zeros((rows, width), jnp.bfloat16)
    for start in range(0, count, rows):
        here = base == jnp.broadcast_to((code - start).astype(jnp.int16), (rows, width))
        out_ref[row + start : row + start + rows, column : column + width] = jnp.where(
            here, one, zero
        )


def select(odd, codes_ref, send_ref, sent_ref, taken_ref, local_ref):
    low, high = send_ref[0:1, :], send_ref[1:2, :]
    for index, which in enumerate(SENT):
        for column, code in (
            (0, jnp.where(odd == 1, high, low)), (HMAX, jnp.where(odd == 1, low, high))
        ):
            one_hot(code - which * BDEV, sent_ref, index * BDEV, BDEV, column)
    for index, which in enumerate(PRODUCT):
        for half in range(2):
            code = codes_ref[which : which + 1, half * BCELLS : (half + 1) * BCELLS]
            at = index * BDEV + half * BCELLS
            one_hot((code - REMOTE) ^ (odd * HMAX), taken_ref, 0, 2 * HMAX, at)
            one_hot(code - (which ^ 1) * BDEV, local_ref, 0, BDEV, at)


def halves(value):
    top = value.astype(jnp.bfloat16)
    return jnp.concatenate([top, (value - top.astype(F32)).astype(jnp.bfloat16)], axis=0)


def whole_layer(field_ref, which, chunk):
    start = chunk * BCELLS
    if which >= 4:
        return field_ref[pl.ds(start + (which - 4) * (BE - 1), FACE, stride=BE), :]
    if which < 2:
        row = start + which * (BE - 1) * FACE
        return field_ref[row : row + FACE, :]
    rows = [start + part * FACE + (which - 2) * (BE - 1) * BE for part in range(BE)]
    return jnp.concatenate([field_ref[row : row + SUB, :] for row in rows], axis=0)


def split_layers(field_ref, chunk, layers_ref):
    for index, which in enumerate(SPLIT):
        at = (index * CHUNKS + chunk) * LANES
        layers_ref[:, at : at + LANES] = halves(whole_layer(field_ref, which, chunk))


def pack(field_ref, layers_ref, sent_ref, send_ref, odd, cross_ref, inside_ref):
    low, high = send_ref[0:1, :], send_ref[1:2, :]
    for out_ref, start, codes in (
        (cross_ref, 0, jnp.where(odd, high, low)), (inside_ref, HMAX, jnp.where(odd, low, high))
    ):
        product = jnp.dot(
            layers_ref[:, BDEV:], sent_ref[:, start : start + HMAX], preferred_element_type=F32
        )
        product = product[:FACE, :] + product[FACE:, :]
        for step in range(2):
            code = jnp.broadcast_to(codes[:, step * LANES : (step + 1) * LANES], (SUB, LANES))
            lane = code & (LANES - 1)
            tile = code >> 7
            found = [
                product[part * SUB : (part + 1) * SUB, step * LANES : (step + 1) * LANES]
                for part in range(8)
            ]
            for which in range(6):
                if which in SENT:
                    continue
                for source in range(CHUNKS):
                    here = tile == which * CHUNKS + source
                    for part in range(8):
                        values = layer_tile(field_ref, which, part, source)
                        found[part] = jnp.where(here, pick(values, lane), found[part])
            for part in range(8):
                row = step * FACE + part * SUB
                out_ref[row : row + SUB, :] = found[part]


def layer_tile(field_ref, which, part, chunk):
    row = (part * BE, (BE - 1) * FACE + part * BE, part * FACE, part * FACE + (BE - 1) * BE)[which]
    row = row + chunk * BCELLS
    return field_ref[row : row + SUB, :]


def layer(faces_ref, half, which, part):
    base = (half * 6 + which) * FACE + part * SUB
    return faces_ref[base : base + SUB, :]


def gather_layers(step, codes_ref, field_ref, layers_ref, local_ref, faces_ref):
    for index, which in enumerate(PRODUCT):
        at = index * BDEV + step * (2 * LANES)
        start = SPLIT.index(which ^ 1) * BDEV
        found = jnp.dot(
            layers_ref[:, start : start + BDEV],
            local_ref[:, pl.ds(pl.multiple_of(at, 2 * LANES), 2 * LANES)],
            preferred_element_type=F32,
        )
        found = found[:FACE, :] + found[FACE:, :]
        for half in range(PAIR):
            base = (half * 6 + which) * FACE
            faces_ref[base : base + FACE, :] = found[:, half * LANES : (half + 1) * LANES]
    for half in range(PAIR):
        at = lanes((step * PAIR + half) * LANES)
        for which in range(6):
            if which in PRODUCT:
                continue
            partner = which ^ 1
            code = jnp.broadcast_to(codes_ref[which : which + 1, at], (SUB, LANES))
            code = code - partner * BDEV
            lane = code & (LANES - 1)
            tile = code >> 7
            found = [jnp.zeros((SUB, LANES), F32) for _ in range(8)]
            for source in range(CHUNKS):
                here = tile == source
                for part in range(8):
                    values = layer_tile(field_ref, partner, part, source)
                    found[part] = jnp.where(here, pick(values, lane), found[part])
            for part in range(8):
                base = (half * 6 + which) * FACE + part * SUB
                faces_ref[base : base + SUB, :] = found[part]


def local_kernel(known, theta_ref, codes_ref, field_ref, layers_ref, local_ref, *refs):
    basis = refs[:known]
    faces_ref, beside_ref, sums_ref = refs[-3:]
    if known > 1:
        diagonal_ref, gram_in_ref, out_ref, gram_ref = refs[known:-3]
        gram_in = gram_in_ref[...]
    else:
        counts_ref, before_ref, old_ref, cross_ref, inside_ref, out_ref, gram_ref, diagonal_ref = (
            refs[1:9]
        )
        turned_ref = refs[9]
        gram_in = jnp.zeros((SUB, LANES), F32)
        assemble(
            counts_ref, before_ref[0], old_ref, cross_ref, inside_ref, diagonal_ref, turned_ref
        )
    theta = theta_ref[0]
    sums_ref[...] = jnp.zeros_like(sums_ref)

    def body(step, carry):
        gather_layers(step, codes_ref, field_ref, layers_ref, local_ref, faces_ref)
        sums = [jnp.zeros((SUB, LANES), F32) for _ in range(known)]
        for half in range(PAIR):
            start = pl.multiple_of((step * PAIR + half) * BCELLS, BCELLS)

            def block(i, j):
                return field_ref[pl.ds(start + (i * BE + j) * BE, SUB), :]

            for i in range(BE):
                row = [layer(faces_ref, half, 4, i)]
                row += [field_ref[pl.ds(start + i * FACE + k, SUB, stride=BE), :] for k in range(BE)]
                row += [layer(faces_ref, half, 5, i)]
                for k in range(BE):
                    at = pl.ds(half * BCELLS + i * FACE + k, SUB, stride=BE)
                    beside_ref[at, :] = row[k] + row[k + 2]
            for i in range(BE):
                for j in range(BE):
                    row = (i * BE + j) * BE
                    rows = pl.ds(start + row, SUB)
                    here = block(i, j)
                    beside = beside_ref[half * BCELLS + row : half * BCELLS + row + SUB, :]
                    beside = beside + (block(i - 1, j) if i > 0 else layer(faces_ref, half, 0, j))
                    beside = beside + (
                        block(i + 1, j) if i < BE - 1 else layer(faces_ref, half, 1, j)
                    )
                    beside = beside + (block(i, j - 1) if j > 0 else layer(faces_ref, half, 2, i))
                    beside = beside + (
                        block(i, j + 1) if j < BE - 1 else layer(faces_ref, half, 3, i)
                    )
                    newest = basis[-1][rows, :]
                    value = (6.0 + diagonal_ref[rows, :]) * here - beside
                    out_ref[rows, :] = value - theta * newest
                    for k, ref in enumerate(basis):
                        old = newest if k == known - 1 else ref[rows, :]
                        sums[k] = sums[k] + newest * old
        for k, part in enumerate(sums):
            sums_ref[k] += part
        return carry

    lax.fori_loop(0, CHUNKS // PAIR, body, 0)
    place_sums(sums_ref, known, gram_in, gram_ref, (known - 1) * known // 2)


def receive(cross_ref, inside_ref):
    parts = [
        ref[part * FACE : (part + 1) * FACE, :]
        for ref in (cross_ref, inside_ref)
        for part in range(2)
    ]
    return halves(jnp.concatenate(parts, axis=1))


def finish(odd, codes_ref, taken_ref, received, cross_ref, inside_ref, out_ref, pair):
    for which in range(6):
        if which in PRODUCT:
            at = PRODUCT.index(which) * BDEV + pair * 2 * LANES
            product = jnp.dot(
                received, taken_ref[:, at : at + 2 * LANES], preferred_element_type=F32
            )
            product = product[:FACE, :] + product[FACE:, :]
        for half in range(2):
            chunk = pair * 2 + half
            start = chunk * BCELLS
            if which in PRODUCT:
                beside = product[:, half * LANES : (half + 1) * LANES]
            else:
                code = codes_ref[which : which + 1, chunk * LANES : (chunk + 1) * LANES] - REMOTE
                code = jnp.broadcast_to(code, (SUB, LANES))
                lane = code & (LANES - 1)
                tile = (code >> 7) ^ (odd * 2)
                found = [jnp.zeros((SUB, LANES), F32) for _ in range(8)]
                for source in range(2 * HMAX // LANES):
                    here = tile == source
                    from_ref = cross_ref if source < HMAX // LANES else inside_ref
                    base = source % (HMAX // LANES) * FACE
                    for part in range(8):
                        values = from_ref[base + part * SUB : base + (part + 1) * SUB, :]
                        found[part] = jnp.where(here, pick(values, lane), found[part])
                beside = jnp.concatenate(found, axis=0)
            if which >= 4:
                rows = pl.ds(start + (which - 4) * (BE - 1), FACE, stride=BE)
                out_ref[rows, :] = out_ref[rows, :] - beside
            elif which < 2:
                row = start + which * (BE - 1) * FACE
                out_ref[row : row + FACE, :] = out_ref[row : row + FACE, :] - beside
            else:
                for part in range(BE):
                    row = start + part * FACE + (which - 2) * (BE - 1) * BE
                    out_ref[row : row + SUB, :] = (
                        out_ref[row : row + SUB, :] - beside[part * SUB : (part + 1) * SUB, :]
                    )


def place_sums(sums_ref, count, gram_in, gram_out_ref, first):
    lane = lax.broadcasted_iota(jnp.int32, (SUB, LANES), 1)
    row = gram_in
    for k in range(count):
        row = row + jnp.where(lane == first + k, jnp.sum(sums_ref[k]), 0.0)
    for start in range(0, gram_out_ref.shape[0], SUB):
        gram_out_ref[start : start + SUB, :] = row


def send(
    split_ref, value_ref, field_ref, layers_ref, sent_ref, send_ref, odd, cross_ref, inside_ref,
    before,
):
    for pair in range(CHUNKS // 2):
        before(pair)
        precondition(split_ref, value_ref, field_ref, pair)
        split_layers(field_ref, 2 * pair, layers_ref)
        split_layers(field_ref, 2 * pair + 1, layers_ref)
    pack(field_ref, layers_ref, sent_ref, send_ref, odd, cross_ref, inside_ref)


def first_kernel(
    counts_ref, old_ref, cross_ref, inside_ref, split_ref, sent_ref, send_ref,
    before_ref, rhs_ref, field_ref, layers_ref, to_cross_ref, to_inside_ref,
    turned_ref,
):
    odd = count_of(counts_ref, 3) == 1
    before = count_before(odd, cross_ref, inside_ref)
    before_ref[0] = before
    assemble(counts_ref, before, old_ref, cross_ref, inside_ref, rhs_ref, turned_ref)
    send(
        split_ref, rhs_ref, field_ref, layers_ref, sent_ref, send_ref, odd, to_cross_ref,
        to_inside_ref, lambda pair: None,
    )


def next_kernel(
    rank_ref, codes_ref, send_ref, cross_ref, inside_ref, partial_ref, taken_ref, split_ref,
    sent_ref,
    out_ref, field_ref, layers_ref, to_cross_ref, to_inside_ref,
):
    del partial_ref
    odd = rank_ref[0] & 1
    received = receive(cross_ref, inside_ref)

    def before(pair):
        finish(odd, codes_ref, taken_ref, received, cross_ref, inside_ref, out_ref, pair)

    send(
        split_ref, out_ref, field_ref, layers_ref, sent_ref, send_ref, odd == 1, to_cross_ref,
        to_inside_ref, before,
    )


def end_kernel(
    rank_ref, codes_ref, cross_ref, inside_ref, partial_ref, taken_ref, gram_in_ref, *refs
):
    del partial_ref
    basis = refs[: BASIS - 1]
    out_ref, gram_ref, sums_ref = refs[BASIS - 1 :]
    odd = rank_ref[0] & 1
    received = receive(cross_ref, inside_ref)
    sums = [jnp.zeros((SUB, LANES), F32) for _ in range(BASIS)]
    for pair in range(CHUNKS // 2):
        finish(odd, codes_ref, taken_ref, received, cross_ref, inside_ref, out_ref, pair)
        for row in range(pair * 2 * BCELLS, (pair + 1) * 2 * BCELLS, SUB):
            rows = slice(row, row + SUB)
            value = out_ref[rows, :]
            for k, ref in enumerate(basis):
                sums[k] = sums[k] + value * ref[rows, :]
            sums[-1] = sums[-1] + value * value
    for k, part in enumerate(sums):
        sums_ref[k] = part
    place_sums(sums_ref, BASIS, gram_in_ref[...], gram_ref, BASIS * (BASIS - 1) // 2)


def recurrence(gram, theta):
    def dot(left, right):
        total = None
        for a, x in enumerate(left):
            if x is None:
                continue
            part = None
            for b, y in enumerate(right):
                if y is not None:
                    term = gram[max(a, b)][min(a, b)] * y
                    part = term if part is None else part + term
            total = x * part if total is None else total + x * part
        return total

    def add(left, right):
        return [
            y if x is None else x if y is None else x + y for x, y in zip(left, right)
        ]

    def times(factor, vector):
        return [None if x is None else factor * x for x in vector]

    def apply(vector):
        return add([None] + vector[:-1], times(theta, vector))

    one = jnp.ones_like(theta)
    shadow = [one] + [None] * (BASIS - 1)
    residual = shadow
    direction = residual
    rho = gram[0][0]
    rho_next = rho
    total = [None] * BASIS
    along = alpha = omega = None
    for step in range(ITERS):
        if step > 0:
            beta = (rho_next / rho) * (alpha / omega)
            rho = rho_next
            direction = add(residual, times(beta, add(direction, times(-omega, along))))
        along = apply(direction)
        alpha = rho / dot(shadow, along)
        middle = add(residual, times(-alpha, along))
        image = apply(middle)
        omega = dot(image, middle) / dot(image, image)
        total = add(total, add(times(alpha, direction), times(omega, middle)))
        residual = add(middle, times(-omega, image))
        rho_next = dot(shadow, residual)
    return total, residual


def last_kernel(theta_ref, gathered_ref, *refs):
    basis = refs[:BASIS]
    fields = refs[BASIS : 2 * BASIS - 1]
    outs = refs[2 * BASIS - 1 : 2 * BASIS + 1]
    solution_ref, residual_ref, sems = refs[2 * BASIS + 1 :]
    row = jnp.sum(gathered_ref[...], axis=0, keepdims=True)
    lane = lax.broadcasted_iota(jnp.int32, (1, LANES), 1)

    def entry(k):
        return jnp.sum(jnp.where(lane == k, row, 0.0), axis=1, keepdims=True)

    gram = [[entry(a * (a + 1) // 2 + b) for b in range(a + 1)] for a in range(BASIS)]
    theta = jnp.full((1, 1), theta_ref[0])
    total, residual = recurrence(gram, theta)
    total = [None if x is None else jnp.broadcast_to(x, (SUB, LANES)) for x in total]
    residual = [jnp.broadcast_to(x, (SUB, LANES)) for x in residual]
    part = BCELLS // PARTS
    copies = []
    for block in range(PARTS):

        def body(step, carry, block=block):
            start = pl.multiple_of(block * part + step * SUB, SUB)
            for chunk in range(CHUNKS):
                rows = pl.ds(chunk * BCELLS + start, SUB)
                at = slice(chunk * LANES, (chunk + 1) * LANES)
                value = total[0] * fields[0][rows, :]
                for k in range(1, BASIS - 1):
                    value = value + total[k] * fields[k][rows, :]
                solution_ref[pl.ds(start, SUB), at] = value
                value = residual[0] * basis[0][rows, :]
                for k in range(1, BASIS):
                    value = value + residual[k] * basis[k][rows, :]
                residual_ref[pl.ds(start, SUB), at] = value
            return carry

        lax.fori_loop(0, part // SUB, body, 0, unroll=4)
        for k, ref in enumerate((solution_ref, residual_ref)):
            at = slice(block * part, (block + 1) * part)
            copies.append(
                pltpu.make_async_copy(ref.at[at, :], outs[k].at[at, :], sems.at[k, block])
            )
            copies[-1].start()
    for copy in copies:
        copy.wait()


def per_device(rhs_old, diagonal_old, new_owner, face_source, send_layers, block_inverse):
    def of(rows):
        return jax.ShapeDtypeStruct((rows, LANES), F32)

    field_type = of(CHUNKS * BCELLS)
    out_type = jax.ShapeDtypeStruct((BCELLS, BDEV), F32)
    halo_type = of(2 * FACE)
    split_type = jax.ShapeDtypeStruct((BCELLS, 3 * BCELLS), jnp.bfloat16)
    turned = pltpu.VMEM((2, 64, LANES), F32)
    layers = [pltpu.VMEM((PAIR * 6 * FACE, LANES), F32), pltpu.VMEM((PAIR * BCELLS, LANES), F32)]
    packed_type = jax.ShapeDtypeStruct((2 * FACE, len(SPLIT) * BDEV), jnp.bfloat16)
    sums = pltpu.VMEM((BASIS, SUB, LANES), F32)

    rank = lax.axis_index(AXES).astype(jnp.int32).reshape(1)
    counts, cross, inside = call(
        front_kernel,
        (
            jax.ShapeDtypeStruct((SUB, LANES), jnp.int32),
            of(2 * BCELLS + SUB),
            of(2 * BCELLS + SUB),
        ),
        (rank, new_owner.reshape(CAP // LANES, LANES), rhs_old),
        [SMEM, VMEM, HBM],
        (VMEM, VMEM, VMEM),
        [
            pltpu.VMEM((BCELLS, MOVE), F32),
            pltpu.VMEM((BCELLS, CAP - 2 * MOVE), F32),
            pltpu.SemaphoreType.DMA((2,)),
        ],
        limit=FRONT,
    )
    rhs_cross = swapped(cross, True)
    rhs_inside = swapped(inside, False)
    cross, inside = call(
        cut_kernel,
        (of(2 * BCELLS), of(2 * BCELLS)),
        (counts, diagonal_old),
        [VMEM, VMEM],
        (VMEM, VMEM),
    )
    diagonal_cross = swapped(cross, True)
    diagonal_inside = swapped(inside, False)
    split, theta, sent, taken, local = call(
        prepare_kernel,
        (
            split_type,
            jax.ShapeDtypeStruct((1,), F32),
            jax.ShapeDtypeStruct((len(SENT) * BDEV, 2 * HMAX), jnp.bfloat16),
            jax.ShapeDtypeStruct((2 * HMAX, len(PRODUCT) * BDEV), jnp.bfloat16),
            jax.ShapeDtypeStruct((BDEV, len(PRODUCT) * BDEV), jnp.bfloat16),
        ),
        (rank, block_inverse, face_source, send_layers),
        [SMEM] + [VMEM] * 3,
        (VMEM, SMEM, VMEM, VMEM, VMEM),
    )
    before, rhs, field, packed, to_cross, to_inside = call(
        first_kernel,
        (jax.ShapeDtypeStruct((1,), jnp.int32),)
        + (field_type, field_type, packed_type, halo_type, halo_type),
        (counts, rhs_old, rhs_cross, rhs_inside, split, sent, send_layers),
        [VMEM] * 7,
        (SMEM,) + (VMEM,) * 5,
        [turned],
        flops=10**9,
        bytes_accessed=8 * MIB,
    )
    diagonal = gram = None
    basis = [rhs]
    fields = [field]
    for known in range(1, BASIS):
        from_cross = swapped(to_cross, True)
        from_inside = swapped(to_inside, False)
        args = [theta, face_source, field, packed, local] + basis
        outs = [field_type, of(SUB)]
        specs = [SMEM] + [VMEM] * (len(args) - 1)
        if known > 1:
            args += [diagonal, gram]
            specs += [VMEM, VMEM]
            scratch = layers + [sums]
        else:
            args += [counts, before, diagonal_old, diagonal_cross, diagonal_inside]
            specs += [VMEM, SMEM] + [VMEM] * 3
            outs.append(field_type)
            scratch = [turned] + layers + [sums]
        found = call(
            functools.partial(local_kernel, known),
            tuple(outs),
            tuple(args),
            specs,
            (VMEM,) * len(outs),
            scratch,
            flops=10**9,
            bytes_accessed=4 * MIB,
        )
        partial, gram = found[:2]
        if known == 1:
            diagonal = found[2]
        if known < BASIS - 1:
            value, field, packed, to_cross, to_inside = call(
                next_kernel,
                (field_type, field_type, packed_type, halo_type, halo_type),
                (
                    rank, face_source, send_layers, from_cross, from_inside, partial, taken,
                    split, sent,
                ),
                [SMEM] + [VMEM] * 8,
                (VMEM,) * 5,
                flops=10**9,
                bytes_accessed=12 * MIB,
                aliases={5: 0},
            )
            fields.append(field)
        else:
            value, copies = call(
                end_kernel,
                (field_type, of(lax.axis_size(AXES))),
                (rank, face_source, from_cross, from_inside, partial, taken, gram, *basis),
                [SMEM] + [VMEM] * (6 + len(basis)),
                (VMEM, VMEM),
                [sums],
                flops=10**9,
                bytes_accessed=12 * MIB,
                aliases={4: 0},
            )
        basis.append(value)
    gathered = lax.all_to_all(copies, AXES, split_axis=0, concat_axis=0, tiled=True)
    return call(
        last_kernel,
        (out_type, out_type),
        (theta, gathered, *basis, *fields),
        [SMEM] + [VMEM] * (2 * BASIS),
        (HBM, HBM),
        [pltpu.VMEM((BCELLS, BDEV), F32)] * 2 + [pltpu.SemaphoreType.DMA((2, PARTS))],
        limit=16,
    )


def solution(mesh):
    return jax.shard_map(
        per_device,
        mesh=mesh,
        in_specs=(
            P(None, AXES),
            P(None, AXES),
            P(AXES),
            P(None, AXES),
            P(None, AXES),
            P(),
        ),
        out_specs=(P(None, AXES), P(None, AXES)),
        check_vma=False,
    )
```

```python
import functools

import jax
import jax.numpy as jnp
from jax import lax
from jax.experimental import pallas as pl
from jax.experimental.pallas import tpu as pltpu
from jax.sharding import PartitionSpec as P

BE = 8
BCELLS = 512
FACE = 64
BDEV = 1024
MOVE = 256
CAP = 1536
HMAX = 256
ITERS = 2
LANES = 128
SUB = 8
CHUNKS = BDEV // LANES
AXES = ("gx", "gy", "gz")
REMOTE = 6 * BDEV
BASIS = 2 * ITERS + 1
MIB = 1024 * 1024
PARTS = 8
PAIR = 2
FRONT = 52
PRODUCT = (0, 4, 5)
SENT = (4, 5, 0, 3)
SPLIT = (1,) + SENT
F32 = jnp.float32

VMEM = pl.BlockSpec(memory_space=pltpu.VMEM)
SMEM = pl.BlockSpec(memory_space=pltpu.SMEM)
HBM = pl.BlockSpec(memory_space=pltpu.HBM)


def swapped(value, cross):
    count = lax.axis_size(AXES)
    first = 1 if cross else 0
    pairs = [(low, low + 1) for low in range(first, count - 1, 2)]
    return lax.ppermute(value, AXES, pairs + [(high, low) for low, high in pairs])


def call(kernel, outs, args, in_specs, out_specs, scratch=(), limit=16, flops=0, bytes_accessed=0, aliases=None):
    if aliases is None:
        aliases = {}
    return pl.pallas_call(
        kernel,
        out_shape=outs,
        in_specs=in_specs,
        out_specs=out_specs,
        scratch_shapes=list(scratch),
        input_output_aliases=aliases,
        compiler_params=pltpu.CompilerParams(vmem_limit_bytes=limit * MIB),
        cost_estimate=pl.CostEstimate(
            flops=flops, bytes_accessed=bytes_accessed, transcendentals=0
        ),
    )(*args)


def lane_iota(rows=SUB):
    return lax.broadcasted_iota(jnp.int32, (rows, LANES), 1)


def lanes(start):
    return pl.ds(pl.multiple_of(start, LANES), LANES)


def pick(values, index):
    return jnp.take_along_axis(values, index, axis=1, mode="promise_in_bounds")


def cut_rows(start, low_ref, high_ref, odd, count, cross_ref, inside_ref):
    tile = start >> 7
    shift = start & (LANES - 1)
    rows = 128

    for step in range(BCELLS // rows):
        at = slice(step * rows, (step + 1) * rows)
        first = lane_iota(rows) < LANES - shift
        turned = []
        for part in range(3):
            source = jnp.minimum(tile + part, high_ref.shape[1] // LANES - 1) * LANES
            turned.append(pltpu.roll(high_ref[at, lanes(source)], (LANES - shift) & (LANES - 1), 1))
        for half in range(2):
            lower = low_ref[at, half * LANES : (half + 1) * LANES]
            upper = jnp.where(first, turned[half], turned[half + 1])
            to = slice(half * BCELLS + step * rows, half * BCELLS + (step + 1) * rows)
            cross_ref[to, :] = jnp.where(odd, upper, lower)
            inside_ref[to, :] = jnp.where(odd, lower, upper)
    if count is not None:
        row = jnp.full((SUB, LANES), count.astype(F32))
        cross_ref[2 * BCELLS : 2 * BCELLS + SUB, :] = row
        inside_ref[2 * BCELLS : 2 * BCELLS + SUB, :] = row


def front_kernel(
    rank_ref, owner_ref, old_ref, counts_ref, cross_ref, inside_ref, low_ref, high_ref, sems
):
    high_copy = pltpu.make_async_copy(
        old_ref.at[:, pl.ds(2 * MOVE, CAP - 2 * MOVE)], high_ref, sems.at[1]
    )
    high_copy.start()
    low_copy = pltpu.make_async_copy(old_ref.at[:, pl.ds(0, MOVE)], low_ref, sems.at[0])
    low_copy.start()
    rank = rank_ref[0]
    owner = owner_ref[...]
    filled = owner >= 0
    head = jnp.sum(((owner == rank - 1) & filled).astype(jnp.int32))
    stay = jnp.sum((owner == rank).astype(jnp.int32))
    tail = jnp.sum(((owner == rank + 1) & filled).astype(jnp.int32))
    odd = rank & 1
    row = lax.broadcasted_iota(jnp.int32, (SUB, LANES), 0)
    counts_ref[...] = jnp.where(
        row == 0, head, jnp.where(row == 1, stay, jnp.where(row == 2, tail, odd))
    )
    high_copy.wait()
    low_copy.wait()
    start = head + stay - 2 * MOVE
    cut_rows(start, low_ref, high_ref, odd == 1, tail, cross_ref, inside_ref)


def count_of(counts_ref, row):
    return jnp.max(counts_ref[row : row + 1, :])


def cut_kernel(counts_ref, old_ref, cross_ref, inside_ref):
    start = count_of(counts_ref, 0) + count_of(counts_ref, 1)
    odd = count_of(counts_ref, 3) == 1
    cut_rows(start, old_ref, old_ref, odd, None, cross_ref, inside_ref)


def count_before(odd, cross_ref, inside_ref):
    row = slice(2 * BCELLS, 2 * BCELLS + SUB)
    return jnp.max(jnp.where(odd, inside_ref[row, :], cross_ref[row, :])).astype(jnp.int32)


def assemble(counts_ref, before, old_ref, cross_ref, inside_ref, out_ref, turned_ref):
    head = count_of(counts_ref, 0)
    stay = count_of(counts_ref, 1)
    odd = count_of(counts_ref, 3) == 1
    own_start = head - before
    own_tile = own_start >> 7
    own_shift = own_start & (LANES - 1)
    up_start = -(before + stay)
    up_tile = up_start >> 7
    up_shift = up_start & (LANES - 1)
    rows = 64
    lane = lane_iota(rows)
    for start in range(0, BCELLS, rows):
        for part in range(2):
            half = slice(part * BCELLS + start, part * BCELLS + start + rows)
            turned_ref[part, start : start + rows, :] = pltpu.roll(
                jnp.where(odd, cross_ref[half, :], inside_ref[half, :]),
                (LANES - up_shift) & (LANES - 1),
                1,
            )
    for start in range(0, BCELLS, rows):
        at = slice(start, start + rows)
        last = None
        for chunk in range(CHUNKS + 1):
            source = jnp.clip(own_tile + chunk, 0, CAP // LANES - 1) * LANES
            now = pltpu.roll(
                old_ref[at, lanes(source)], (LANES - own_shift) & (LANES - 1), 1
            )
            if chunk > 0:
                place = chunk - 1
                column = lane + place * LANES
                value = jnp.where(lane < LANES - own_shift, last, now)
                if place >= 2 * MOVE // LANES:
                    low_half = turned_ref[jnp.clip(up_tile + place, 0, 1), at, :]
                    high_half = turned_ref[jnp.clip(up_tile + place + 1, 0, 1), at, :]
                    above = jnp.where(lane < LANES - up_shift, low_half, high_half)
                    value = jnp.where(column < before + stay, value, above)
                if place < MOVE // LANES:
                    half = slice(place * BCELLS + start, place * BCELLS + start + rows)
                    below = jnp.where(odd, inside_ref[half, :], cross_ref[half, :])
                    value = jnp.where(column < before, below, value)
                out_ref[place * BCELLS + start : place * BCELLS + start + rows, :] = value
            last = now


def prepare_kernel(
    rank_ref, inverse_ref, codes_ref, send_ref, split_ref, theta_ref, sent_ref, taken_ref, local_ref
):
    select(rank_ref[0] & 1, codes_ref, send_ref, sent_ref, taken_ref, local_ref)
    inverse = inverse_ref[...]
    size = jnp.abs(inverse)
    by_row = jnp.max(jnp.sum(size, axis=1, keepdims=True), axis=0, keepdims=True)
    by_column = jnp.max(jnp.sum(size, axis=0, keepdims=True), axis=1, keepdims=True)
    bound = 14.5 * jnp.sqrt(by_row) * jnp.sqrt(by_column)
    scale = jnp.full((1, 1), 0.5, F32)
    for power in (64, 32, 16, 8, 4, 2, 1):
        large = bound >= 2.0**power
        bound = jnp.where(large, bound * 2.0**-power, bound)
        scale = jnp.where(large, scale * 2.0**-power, scale)
    for power in (64, 32, 16, 8, 4, 2, 1):
        small = bound < 2.0**-power
        bound = jnp.where(small, bound * 2.0**power, bound)
        scale = jnp.where(small, scale * 2.0**power, scale)
    scaled = inverse * scale
    high = scaled.astype(jnp.bfloat16)
    split_ref[:, 0:BCELLS] = high
    split_ref[:, BCELLS : 2 * BCELLS] = high
    split_ref[:, 2 * BCELLS : 3 * BCELLS] = (scaled - high.astype(F32)).astype(jnp.bfloat16)
    row = lax.broadcasted_iota(jnp.int32, (BCELLS, BCELLS), 0)
    column = lax.broadcasted_iota(jnp.int32, (BCELLS, BCELLS), 1)
    theta_ref[0] = jnp.sum(jnp.where(row == column, scaled, 0.0)) * (6.5 / BCELLS)


def precondition(split_ref, field_ref, out_ref, pair):
    base = pair * 2 * BCELLS
    field = jnp.concatenate(
        [field_ref[base + half * BCELLS : base + (half + 1) * BCELLS, :] for half in range(2)],
        axis=1,
    )
    top = field.astype(jnp.bfloat16)
    rest = (field - top.astype(F32)).astype(jnp.bfloat16)
    stacked = jnp.concatenate([top, rest, top], axis=0)
    found = jnp.dot(split_ref[...], stacked, preferred_element_type=F32)
    out_ref[base : base + BCELLS, :] = found[:, :LANES]
    out_ref[base + BCELLS : base + 2 * BCELLS, :] = found[:, LANES:]


def one_hot(code, out_ref, row, count, column):
    rows = 512
    width = code.shape[1]
    base = lax.broadcasted_iota(jnp.int32, (rows, width), 0).astype(jnp.int16)
    one = jnp.ones((rows, width), jnp.bfloat16)
    zero = jnp.zeros((rows, width), jnp.bfloat16)
    for start in range(0, count, rows):
        here = base == jnp.broadcast_to((code - start).astype(jnp.int16), (rows, width))
        out_ref[row + start : row + start + rows, column : column + width] = jnp.where(
            here, one, zero
        )


def select(odd, codes_ref, send_ref, sent_ref, taken_ref, local_ref):
    low, high = send_ref[0:1, :], send_ref[1:2, :]
    for index, which in enumerate(SENT):
        for column, code in (
            (0, jnp.where(odd == 1, high, low)), (HMAX, jnp.where(odd == 1, low, high))
        ):
            one_hot(code - which * BDEV, sent_ref, index * BDEV, BDEV, column)
    for index, which in enumerate(PRODUCT):
        for half in range(2):
            code = codes_ref[which : which + 1, half * BCELLS : (half + 1) * BCELLS]
            at = index * BDEV + half * BCELLS
            one_hot((code - REMOTE) ^ (odd * HMAX), taken_ref, 0, 2 * HMAX, at)
            one_hot(code - (which ^ 1) * BDEV, local_ref, 0, BDEV, at)


def halves(value):
    top = value.astype(jnp.bfloat16)
    return jnp.concatenate([top, (value - top.astype(F32)).astype(jnp.bfloat16)], axis=0)


def whole_layer(field_ref, which, chunk):
    start = chunk * BCELLS
    if which >= 4:
        return field_ref[pl.ds(start + (which - 4) * (BE - 1), FACE, stride=BE), :]
    if which < 2:
        row = start + which * (BE - 1) * FACE
        return field_ref[row : row + FACE, :]
    rows = [start + part * FACE + (which - 2) * (BE - 1) * BE for part in range(BE)]
    return jnp.concatenate([field_ref[row : row + SUB, :] for row in rows], axis=0)


def split_layers(field_ref, chunk, layers_ref):
    for index, which in enumerate(SPLIT):
        at = (index * CHUNKS + chunk) * LANES
        layers_ref[:, at : at + LANES] = halves(whole_layer(field_ref, which, chunk))


def pack(field_ref, layers_ref, sent_ref, send_ref, odd, cross_ref, inside_ref):
    low, high = send_ref[0:1, :], send_ref[1:2, :]
    for out_ref, start, codes in (
        (cross_ref, 0, jnp.where(odd, high, low)), (inside_ref, HMAX, jnp.where(odd, low, high))
    ):
        product = jnp.dot(
            layers_ref[:, BDEV:], sent_ref[:, start : start + HMAX], preferred_element_type=F32
        )
        product = product[:FACE, :] + product[FACE:, :]
        for step in range(2):
            code = jnp.broadcast_to(codes[:, step * LANES : (step + 1) * LANES], (SUB, LANES))
            lane = code & (LANES - 1)
            tile = code >> 7
            found = [
                product[part * SUB : (part + 1) * SUB, step * LANES : (step + 1) * LANES]
                for part in range(8)
            ]
            for which in range(6):
                if which in SENT:
                    continue
                for source in range(CHUNKS):
                    here = tile == which * CHUNKS + source
                    for part in range(8):
                        values = layer_tile(field_ref, which, part, source)
                        found[part] = jnp.where(here, pick(values, lane), found[part])
            for part in range(8):
                row = step * FACE + part * SUB
                out_ref[row : row + SUB, :] = found[part]


def layer_tile(field_ref, which, part, chunk):
    row = (part * BE, (BE - 1) * FACE + part * BE, part * FACE, part * FACE + (BE - 1) * BE)[which]
    row = row + chunk * BCELLS
    return field_ref[row : row + SUB, :]


def layer(faces_ref, half, which, part):
    base = (half * 6 + which) * FACE + part * SUB
    return faces_ref[base : base + SUB, :]


def gather_layers(step, codes_ref, field_ref, layers_ref, local_ref, faces_ref):
    for index, which in enumerate(PRODUCT):
        at = index * BDEV + step * (2 * LANES)
        start = SPLIT.index(which ^ 1) * BDEV
        found = jnp.dot(
            layers_ref[:, start : start + BDEV],
            local_ref[:, pl.ds(pl.multiple_of(at, 2 * LANES), 2 * LANES)],
            preferred_element_type=F32,
        )
        found = found[:FACE, :] + found[FACE:, :]
        for half in range(PAIR):
            base = (half * 6 + which) * FACE
            faces_ref[base : base + FACE, :] = found[:, half * LANES : (half + 1) * LANES]
    for half in range(PAIR):
        at = lanes((step * PAIR + half) * LANES)
        for which in range(6):
            if which in PRODUCT:
                continue
            partner = which ^ 1
            code = jnp.broadcast_to(codes_ref[which : which + 1, at], (SUB, LANES))
            code = code - partner * BDEV
            lane = code & (LANES - 1)
            tile = code >> 7
            found = [jnp.zeros((SUB, LANES), F32) for _ in range(8)]
            for source in range(CHUNKS):
                here = tile == source
                for part in range(8):
                    values = layer_tile(field_ref, partner, part, source)
                    found[part] = jnp.where(here, pick(values, lane), found[part])
            for part in range(8):
                base = (half * 6 + which) * FACE + part * SUB
                faces_ref[base : base + SUB, :] = found[part]


def local_kernel(known, theta_ref, codes_ref, field_ref, layers_ref, local_ref, *refs):
    basis = refs[:known]
    faces_ref, beside_ref, sums_ref = refs[-3:]
    if known > 1:
        diagonal_ref, gram_in_ref, out_ref, gram_ref = refs[known:-3]
        gram_in = gram_in_ref[...]
    else:
        counts_ref, before_ref, old_ref, cross_ref, inside_ref, out_ref, gram_ref, diagonal_ref = (
            refs[1:9]
        )
        turned_ref = refs[9]
        gram_in = jnp.zeros((SUB, LANES), F32)
        assemble(
            counts_ref, before_ref[0], old_ref, cross_ref, inside_ref, diagonal_ref, turned_ref
        )
    theta = theta_ref[0]
    sums_ref[...] = jnp.zeros_like(sums_ref)

    def body(step, carry):
        gather_layers(step, codes_ref, field_ref, layers_ref, local_ref, faces_ref)
        sums = [jnp.zeros((SUB, LANES), F32) for _ in range(known)]
        for half in range(PAIR):
            start = pl.multiple_of((step * PAIR + half) * BCELLS, BCELLS)

            def block(i, j):
                return field_ref[pl.ds(start + (i * BE + j) * BE, SUB), :]

            for i in range(BE):
                row = [layer(faces_ref, half, 4, i)]
                row += [field_ref[pl.ds(start + i * FACE + k, SUB, stride=BE), :] for k in range(BE)]
                row += [layer(faces_ref, half, 5, i)]
                for k in range(BE):
                    at = pl.ds(half * BCELLS + i * FACE + k, SUB, stride=BE)
                    beside_ref[at, :] = row[k] + row[k + 2]
            for i in range(BE):
                for j in range(BE):
                    row = (i * BE + j) * BE
                    rows = pl.ds(start + row, SUB)
                    here = block(i, j)
                    beside = beside_ref[half * BCELLS + row : half * BCELLS + row + SUB, :]
                    beside = beside + (block(i - 1, j) if i > 0 else layer(faces_ref, half, 0, j))
                    beside = beside + (
                        block(i + 1, j) if i < BE - 1 else layer(faces_ref, half, 1, j)
                    )
                    beside = beside + (block(i, j - 1) if j > 0 else layer(faces_ref, half, 2, i))
                    beside = beside + (
                        block(i, j + 1) if j < BE - 1 else layer(faces_ref, half, 3, i)
                    )
                    newest = basis[-1][rows, :]
                    value = (6.0 + diagonal_ref[rows, :]) * here - beside
                    out_ref[rows, :] = value - theta * newest
                    for k, ref in enumerate(basis):
                        old = newest if k == known - 1 else ref[rows, :]
                        sums[k] = sums[k] + newest * old
        for k, part in enumerate(sums):
            sums_ref[k] += part
        return carry

    lax.fori_loop(0, CHUNKS // PAIR, body, 0)
    place_sums(sums_ref, known, gram_in, gram_ref, (known - 1) * known // 2)


def receive(cross_ref, inside_ref):
    parts = [
        ref[part * FACE : (part + 1) * FACE, :]
        for ref in (cross_ref, inside_ref)
        for part in range(2)
    ]
    return halves(jnp.concatenate(parts, axis=1))


def finish(odd, codes_ref, taken_ref, received, cross_ref, inside_ref, out_ref, pair):
    for which in range(6):
        if which in PRODUCT:
            at = PRODUCT.index(which) * BDEV + pair * 2 * LANES
            product = jnp.dot(
                received, taken_ref[:, at : at + 2 * LANES], preferred_element_type=F32
            )
            product = product[:FACE, :] + product[FACE:, :]
        for half in range(2):
            chunk = pair * 2 + half
            start = chunk * BCELLS
            if which in PRODUCT:
                beside = product[:, half * LANES : (half + 1) * LANES]
            else:
                code = codes_ref[which : which + 1, chunk * LANES : (chunk + 1) * LANES] - REMOTE
                code = jnp.broadcast_to(code, (SUB, LANES))
                lane = code & (LANES - 1)
                tile = (code >> 7) ^ (odd * 2)
                found = [jnp.zeros((SUB, LANES), F32) for _ in range(8)]
                for source in range(2 * HMAX // LANES):
                    here = tile == source
                    from_ref = cross_ref if source < HMAX // LANES else inside_ref
                    base = source % (HMAX // LANES) * FACE
                    for part in range(8):
                        values = from_ref[base + part * SUB : base + (part + 1) * SUB, :]
                        found[part] = jnp.where(here, pick(values, lane), found[part])
                beside = jnp.concatenate(found, axis=0)
            if which >= 4:
                rows = pl.ds(start + (which - 4) * (BE - 1), FACE, stride=BE)
                out_ref[rows, :] = out_ref[rows, :] - beside
            elif which < 2:
                row = start + which * (BE - 1) * FACE
                out_ref[row : row + FACE, :] = out_ref[row : row + FACE, :] - beside
            else:
                for part in range(BE):
                    row = start + part * FACE + (which - 2) * (BE - 1) * BE
                    out_ref[row : row + SUB, :] = (
                        out_ref[row : row + SUB, :] - beside[part * SUB : (part + 1) * SUB, :]
                    )


def place_sums(sums_ref, count, gram_in, gram_out_ref, first):
    lane = lax.broadcasted_iota(jnp.int32, (SUB, LANES), 1)
    row = gram_in
    for k in range(count):
        row = row + jnp.where(lane == first + k, jnp.sum(sums_ref[k]), 0.0)
    for start in range(0, gram_out_ref.shape[0], SUB):
        gram_out_ref[start : start + SUB, :] = row


def send(
    split_ref, value_ref, field_ref, layers_ref, sent_ref, send_ref, odd, cross_ref, inside_ref,
    before,
):
    for pair in range(CHUNKS // 2):
        before(pair)
        precondition(split_ref, value_ref, field_ref, pair)
        split_layers(field_ref, 2 * pair, layers_ref)
        split_layers(field_ref, 2 * pair + 1, layers_ref)
    pack(field_ref, layers_ref, sent_ref, send_ref, odd, cross_ref, inside_ref)


def first_kernel(
    counts_ref, old_ref, cross_ref, inside_ref, split_ref, sent_ref, send_ref,
    before_ref, rhs_ref, field_ref, layers_ref, to_cross_ref, to_inside_ref,
    turned_ref,
):
    odd = count_of(counts_ref, 3) == 1
    before = count_before(odd, cross_ref, inside_ref)
    before_ref[0] = before
    assemble(counts_ref, before, old_ref, cross_ref, inside_ref, rhs_ref, turned_ref)
    send(
        split_ref, rhs_ref, field_ref, layers_ref, sent_ref, send_ref, odd, to_cross_ref,
        to_inside_ref, lambda pair: None,
    )


def next_kernel(
    rank_ref, codes_ref, send_ref, cross_ref, inside_ref, partial_ref, taken_ref, split_ref,
    sent_ref,
    out_ref, field_ref, layers_ref, to_cross_ref, to_inside_ref,
):
    del partial_ref
    odd = rank_ref[0] & 1
    received = receive(cross_ref, inside_ref)

    def before(pair):
        finish(odd, codes_ref, taken_ref, received, cross_ref, inside_ref, out_ref, pair)

    send(
        split_ref, out_ref, field_ref, layers_ref, sent_ref, send_ref, odd == 1, to_cross_ref,
        to_inside_ref, before,
    )


def end_kernel(
    rank_ref, codes_ref, cross_ref, inside_ref, partial_ref, taken_ref, gram_in_ref, *refs
):
    del partial_ref
    basis = refs[: BASIS - 1]
    out_ref, gram_ref, sums_ref = refs[BASIS - 1 :]
    odd = rank_ref[0] & 1
    received = receive(cross_ref, inside_ref)
    sums = [jnp.zeros((SUB, LANES), F32) for _ in range(BASIS)]
    for pair in range(CHUNKS // 2):
        finish(odd, codes_ref, taken_ref, received, cross_ref, inside_ref, out_ref, pair)
        for row in range(pair * 2 * BCELLS, (pair + 1) * 2 * BCELLS, SUB):
            rows = slice(row, row + SUB)
            value = out_ref[rows, :]
            for k, ref in enumerate(basis):
                sums[k] = sums[k] + value * ref[rows, :]
            sums[-1] = sums[-1] + value * value
    for k, part in enumerate(sums):
        sums_ref[k] = part
    place_sums(sums_ref, BASIS, gram_in_ref[...], gram_ref, BASIS * (BASIS - 1) // 2)


def recurrence(gram, theta):
    def dot(left, right):
        total = None
        for a, x in enumerate(left):
            if x is None:
                continue
            part = None
            for b, y in enumerate(right):
                if y is not None:
                    term = gram[max(a, b)][min(a, b)] * y
                    part = term if part is None else part + term
            total = x * part if total is None else total + x * part
        return total

    def add(left, right):
        return [
            y if x is None else x if y is None else x + y for x, y in zip(left, right)
        ]

    def times(factor, vector):
        return [None if x is None else factor * x for x in vector]

    def apply(vector):
        return add([None] + vector[:-1], times(theta, vector))

    one = jnp.ones_like(theta)
    shadow = [one] + [None] * (BASIS - 1)
    residual = shadow
    direction = residual
    rho = gram[0][0]
    rho_next = rho
    total = [None] * BASIS
    along = alpha = omega = None
    for step in range(ITERS):
        if step > 0:
            beta = (rho_next / rho) * (alpha / omega)
            rho = rho_next
            direction = add(residual, times(beta, add(direction, times(-omega, along))))
        along = apply(direction)
        alpha = rho / dot(shadow, along)
        middle = add(residual, times(-alpha, along))
        image = apply(middle)
        omega = dot(image, middle) / dot(image, image)
        total = add(total, add(times(alpha, direction), times(omega, middle)))
        residual = add(middle, times(-omega, image))
        rho_next = dot(shadow, residual)
    return total, residual


def last_kernel(theta_ref, gathered_ref, *refs):
    basis = refs[:BASIS]
    fields = refs[BASIS : 2 * BASIS - 1]
    outs = refs[2 * BASIS - 1 : 2 * BASIS + 1]
    solution_ref, residual_ref, sems = refs[2 * BASIS + 1 :]
    row = jnp.sum(gathered_ref[...], axis=0, keepdims=True)
    lane = lax.broadcasted_iota(jnp.int32, (1, LANES), 1)

    def entry(k):
        return jnp.sum(jnp.where(lane == k, row, 0.0), axis=1, keepdims=True)

    gram = [[entry(a * (a + 1) // 2 + b) for b in range(a + 1)] for a in range(BASIS)]
    theta = jnp.full((1, 1), theta_ref[0])
    total, residual = recurrence(gram, theta)
    total = [None if x is None else jnp.broadcast_to(x, (SUB, LANES)) for x in total]
    residual = [jnp.broadcast_to(x, (SUB, LANES)) for x in residual]
    part = BCELLS // PARTS
    copies = []
    for block in range(PARTS):

        def body(step, carry, block=block):
            start = pl.multiple_of(block * part + step * SUB, SUB)
            for chunk in range(CHUNKS):
                rows = pl.ds(chunk * BCELLS + start, SUB)
                at = slice(chunk * LANES, (chunk + 1) * LANES)
                value = total[0] * fields[0][rows, :]
                for k in range(1, BASIS - 1):
                    value = value + total[k] * fields[k][rows, :]
                solution_ref[pl.ds(start, SUB), at] = value
                value = residual[0] * basis[0][rows, :]
                for k in range(1, BASIS):
                    value = value + residual[k] * basis[k][rows, :]
                residual_ref[pl.ds(start, SUB), at] = value
            return carry

        lax.fori_loop(0, part // SUB, body, 0, unroll=4)
        for k, ref in enumerate((solution_ref, residual_ref)):
            at = slice(block * part, (block + 1) * part)
            copies.append(
                pltpu.make_async_copy(ref.at[at, :], outs[k].at[at, :], sems.at[k, block])
            )
            copies[-1].start()
    for copy in copies:
        copy.wait()


def per_device(rhs_old, diagonal_old, new_owner, face_source, send_layers, block_inverse):
    def of(rows):
        return jax.ShapeDtypeStruct((rows, LANES), F32)

    field_type = of(CHUNKS * BCELLS)
    out_type = jax.ShapeDtypeStruct((BCELLS, BDEV), F32)
    halo_type = of(2 * FACE)
    split_type = jax.ShapeDtypeStruct((BCELLS, 3 * BCELLS), jnp.bfloat16)
    turned = pltpu.VMEM((2, BCELLS, LANES), F32)
    layers = [pltpu.VMEM((PAIR * 6 * FACE, LANES), F32), pltpu.VMEM((PAIR * BCELLS, LANES), F32)]
    packed_type = jax.ShapeDtypeStruct((2 * FACE, len(SPLIT) * BDEV), jnp.bfloat16)
    sums = pltpu.VMEM((BASIS, SUB, LANES), F32)

    rank = lax.axis_index(AXES).astype(jnp.int32).reshape(1)
    counts, cross, inside = call(
        front_kernel,
        (
            jax.ShapeDtypeStruct((SUB, LANES), jnp.int32),
            of(2 * BCELLS + SUB),
            of(2 * BCELLS + SUB),
        ),
        (rank, new_owner.reshape(CAP // LANES, LANES), rhs_old),
        [SMEM, VMEM, HBM],
        (VMEM, VMEM, VMEM),
        [
            pltpu.VMEM((BCELLS, MOVE), F32),
            pltpu.VMEM((BCELLS, CAP - 2 * MOVE), F32),
            pltpu.SemaphoreType.DMA((2,)),
        ],
        limit=FRONT,
    )
    rhs_cross = swapped(cross, True)
    rhs_inside = swapped(inside, False)
    cross, inside = call(
        cut_kernel,
        (of(2 * BCELLS), of(2 * BCELLS)),
        (counts, diagonal_old),
        [VMEM, VMEM],
        (VMEM, VMEM),
    )
    diagonal_cross = swapped(cross, True)
    diagonal_inside = swapped(inside, False)
    split, theta, sent, taken, local = call(
        prepare_kernel,
        (
            split_type,
            jax.ShapeDtypeStruct((1,), F32),
            jax.ShapeDtypeStruct((len(SENT) * BDEV, 2 * HMAX), jnp.bfloat16),
            jax.ShapeDtypeStruct((2 * HMAX, len(PRODUCT) * BDEV), jnp.bfloat16),
            jax.ShapeDtypeStruct((BDEV, len(PRODUCT) * BDEV), jnp.bfloat16),
        ),
        (rank, block_inverse, face_source, send_layers),
        [SMEM] + [VMEM] * 3,
        (VMEM, SMEM, VMEM, VMEM, VMEM),
    )
    before, rhs, field, packed, to_cross, to_inside = call(
        first_kernel,
        (jax.ShapeDtypeStruct((1,), jnp.int32),)
        + (field_type, field_type, packed_type, halo_type, halo_type),
        (counts, rhs_old, rhs_cross, rhs_inside, split, sent, send_layers),
        [VMEM] * 7,
        (SMEM,) + (VMEM,) * 5,
        [turned],
        flops=10**9,
        bytes_accessed=8 * MIB,
    )
    diagonal = gram = None
    basis = [rhs]
    fields = [field]
    for known in range(1, BASIS):
        from_cross = swapped(to_cross, True)
        from_inside = swapped(to_inside, False)
        args = [theta, face_source, field, packed, local] + basis
        outs = [field_type, of(SUB)]
        specs = [SMEM] + [VMEM] * (len(args) - 1)
        if known > 1:
            args += [diagonal, gram]
            specs += [VMEM, VMEM]
            scratch = layers + [sums]
        else:
            args += [counts, before, diagonal_old, diagonal_cross, diagonal_inside]
            specs += [VMEM, SMEM] + [VMEM] * 3
            outs.append(field_type)
            scratch = [turned] + layers + [sums]
        found = call(
            functools.partial(local_kernel, known),
            tuple(outs),
            tuple(args),
            specs,
            (VMEM,) * len(outs),
            scratch,
            flops=10**9,
            bytes_accessed=4 * MIB,
        )
        partial, gram = found[:2]
        if known == 1:
            diagonal = found[2]
        if known < BASIS - 1:
            value, field, packed, to_cross, to_inside = call(
                next_kernel,
                (field_type, field_type, packed_type, halo_type, halo_type),
                (
                    rank, face_source, send_layers, from_cross, from_inside, partial, taken,
                    split, sent,
                ),
                [SMEM] + [VMEM] * 8,
                (VMEM,) * 5,
                flops=10**9,
                bytes_accessed=12 * MIB,
                aliases={5: 0},
            )
            fields.append(field)
        else:
            value, copies = call(
                end_kernel,
                (field_type, of(lax.axis_size(AXES))),
                (rank, face_source, from_cross, from_inside, partial, taken, gram, *basis),
                [SMEM] + [VMEM] * (6 + len(basis)),
                (VMEM, VMEM),
                [sums],
                flops=10**9,
                bytes_accessed=12 * MIB,
                aliases={4: 0},
            )
        basis.append(value)
    gathered = lax.all_to_all(copies, AXES, split_axis=0, concat_axis=0, tiled=True)
    return call(
        last_kernel,
        (out_type, out_type),
        (theta, gathered, *basis, *fields),
        [SMEM] + [VMEM] * (2 * BASIS),
        (HBM, HBM),
        [pltpu.VMEM((BCELLS, BDEV), F32)] * 2 + [pltpu.SemaphoreType.DMA((2, PARTS))],
        limit=16,
    )


def solution(mesh):
    return jax.shard_map(
        per_device,
        mesh=mesh,
        in_specs=(
            P(None, AXES),
            P(None, AXES),
            P(AXES),
            P(None, AXES),
            P(None, AXES),
            P(),
        ),
        out_specs=(P(None, AXES), P(None, AXES)),
        check_vma=False,
    )
```

```python
import functools

import jax
import jax.numpy as jnp
from jax import lax
from jax.experimental import pallas as pl
from jax.experimental.pallas import tpu as pltpu
from jax.sharding import PartitionSpec as P

BE = 8
BCELLS = 512
FACE = 64
BDEV = 1024
MOVE = 256
CAP = 1536
HMAX = 256
ITERS = 2
LANES = 128
SUB = 8
CHUNKS = BDEV // LANES
AXES = ("gx", "gy", "gz")
REMOTE = 6 * BDEV
BASIS = 2 * ITERS + 1
MIB = 1024 * 1024
PARTS = 8
FRONT = 52
PRODUCT = (0, 4, 5)
SENT = (4, 5, 0, 3)
SPLIT = (1,) + SENT
F32 = jnp.float32

VMEM = pl.BlockSpec(memory_space=pltpu.VMEM)
SMEM = pl.BlockSpec(memory_space=pltpu.SMEM)
HBM = pl.BlockSpec(memory_space=pltpu.HBM)


def swapped(value, cross):
    count = lax.axis_size(AXES)
    first = 1 if cross else 0
    pairs = [(low, low + 1) for low in range(first, count - 1, 2)]
    return lax.ppermute(value, AXES, pairs + [(high, low) for low, high in pairs])


def call(kernel, outs, args, in_specs, out_specs, scratch=(), limit=16, flops=0, bytes_accessed=0, aliases=None):
    if aliases is None:
        aliases = {}
    return pl.pallas_call(
        kernel,
        out_shape=outs,
        in_specs=in_specs,
        out_specs=out_specs,
        scratch_shapes=list(scratch),
        input_output_aliases=aliases,
        compiler_params=pltpu.CompilerParams(vmem_limit_bytes=limit * MIB),
        cost_estimate=pl.CostEstimate(
            flops=flops, bytes_accessed=bytes_accessed, transcendentals=0
        ),
    )(*args)


def lane_iota(rows=SUB):
    return lax.broadcasted_iota(jnp.int32, (rows, LANES), 1)


def lanes(start):
    return pl.ds(pl.multiple_of(start, LANES), LANES)


def pick(values, index):
    return jnp.take_along_axis(values, index, axis=1, mode="promise_in_bounds")


def cut_rows(start, low_ref, high_ref, odd, count, cross_ref, inside_ref):
    tile = start >> 7
    shift = start & (LANES - 1)
    rows = 128

    for step in range(BCELLS // rows):
        at = slice(step * rows, (step + 1) * rows)
        first = lane_iota(rows) < LANES - shift
        turned = []
        for part in range(3):
            source = jnp.minimum(tile + part, high_ref.shape[1] // LANES - 1) * LANES
            turned.append(pltpu.roll(high_ref[at, lanes(source)], (LANES - shift) & (LANES - 1), 1))
        for half in range(2):
            lower = low_ref[at, half * LANES : (half + 1) * LANES]
            upper = jnp.where(first, turned[half], turned[half + 1])
            to = slice(half * BCELLS + step * rows, half * BCELLS + (step + 1) * rows)
            cross_ref[to, :] = jnp.where(odd, upper, lower)
            inside_ref[to, :] = jnp.where(odd, lower, upper)
    if count is not None:
        row = jnp.full((SUB, LANES), count.astype(F32))
        cross_ref[2 * BCELLS : 2 * BCELLS + SUB, :] = row
        inside_ref[2 * BCELLS : 2 * BCELLS + SUB, :] = row


def front_kernel(
    rank_ref, owner_ref, old_ref, counts_ref, cross_ref, inside_ref, low_ref, high_ref, sems
):
    high_copy = pltpu.make_async_copy(
        old_ref.at[:, pl.ds(2 * MOVE, CAP - 2 * MOVE)], high_ref, sems.at[1]
    )
    high_copy.start()
    low_copy = pltpu.make_async_copy(old_ref.at[:, pl.ds(0, MOVE)], low_ref, sems.at[0])
    low_copy.start()
    rank = rank_ref[0]
    owner = owner_ref[...]
    filled = owner >= 0
    head = jnp.sum(((owner == rank - 1) & filled).astype(jnp.int32))
    stay = jnp.sum((owner == rank).astype(jnp.int32))
    tail = jnp.sum(((owner == rank + 1) & filled).astype(jnp.int32))
    odd = rank & 1
    row = lax.broadcasted_iota(jnp.int32, (SUB, LANES), 0)
    counts_ref[...] = jnp.where(
        row == 0, head, jnp.where(row == 1, stay, jnp.where(row == 2, tail, odd))
    )
    high_copy.wait()
    low_copy.wait()
    start = head + stay - 2 * MOVE
    cut_rows(start, low_ref, high_ref, odd == 1, tail, cross_ref, inside_ref)


def count_of(counts_ref, row):
    return jnp.max(counts_ref[row : row + 1, :])


def cut_kernel(counts_ref, old_ref, cross_ref, inside_ref):
    start = count_of(counts_ref, 0) + count_of(counts_ref, 1)
    odd = count_of(counts_ref, 3) == 1
    cut_rows(start, old_ref, old_ref, odd, None, cross_ref, inside_ref)


def count_before(odd, cross_ref, inside_ref):
    row = slice(2 * BCELLS, 2 * BCELLS + SUB)
    return jnp.max(jnp.where(odd, inside_ref[row, :], cross_ref[row, :])).astype(jnp.int32)


def assemble(counts_ref, before, old_ref, cross_ref, inside_ref, out_ref, turned_ref):
    head = count_of(counts_ref, 0)
    stay = count_of(counts_ref, 1)
    odd = count_of(counts_ref, 3) == 1
    own_start = head - before
    own_tile = own_start >> 7
    own_shift = own_start & (LANES - 1)
    up_start = -(before + stay)
    up_tile = up_start >> 7
    up_shift = up_start & (LANES - 1)
    rows = 64
    lane = lane_iota(rows)
    for start in range(0, BCELLS, rows):
        for part in range(2):
            half = slice(part * BCELLS + start, part * BCELLS + start + rows)
            turned_ref[part, start : start + rows, :] = pltpu.roll(
                jnp.where(odd, cross_ref[half, :], inside_ref[half, :]),
                (LANES - up_shift) & (LANES - 1),
                1,
            )
    for start in range(0, BCELLS, rows):
        at = slice(start, start + rows)
        last = None
        for chunk in range(CHUNKS + 1):
            source = jnp.clip(own_tile + chunk, 0, CAP // LANES - 1) * LANES
            now = pltpu.roll(
                old_ref[at, lanes(source)], (LANES - own_shift) & (LANES - 1), 1
            )
            if chunk > 0:
                place = chunk - 1
                column = lane + place * LANES
                value = jnp.where(lane < LANES - own_shift, last, now)
                if place >= 2 * MOVE // LANES:
                    low_half = turned_ref[jnp.clip(up_tile + place, 0, 1), at, :]
                    high_half = turned_ref[jnp.clip(up_tile + place + 1, 0, 1), at, :]
                    above = jnp.where(lane < LANES - up_shift, low_half, high_half)
                    value = jnp.where(column < before + stay, value, above)
                if place < MOVE // LANES:
                    half = slice(place * BCELLS + start, place * BCELLS + start + rows)
                    below = jnp.where(odd, inside_ref[half, :], cross_ref[half, :])
                    value = jnp.where(column < before, below, value)
                out_ref[place * BCELLS + start : place * BCELLS + start + rows, :] = value
            last = now


def prepare_kernel(
    rank_ref, inverse_ref, codes_ref, send_ref, split_ref, theta_ref, sent_ref, taken_ref, local_ref
):
    select(rank_ref[0] & 1, codes_ref, send_ref, sent_ref, taken_ref, local_ref)
    inverse = inverse_ref[...]
    size = jnp.abs(inverse)
    by_row = jnp.max(jnp.sum(size, axis=1, keepdims=True), axis=0, keepdims=True)
    by_column = jnp.max(jnp.sum(size, axis=0, keepdims=True), axis=1, keepdims=True)
    bound = 14.5 * jnp.sqrt(by_row) * jnp.sqrt(by_column)
    scale = jnp.full((1, 1), 0.5, F32)
    for power in (64, 32, 16, 8, 4, 2, 1):
        large = bound >= 2.0**power
        bound = jnp.where(large, bound * 2.0**-power, bound)
        scale = jnp.where(large, scale * 2.0**-power, scale)
    for power in (64, 32, 16, 8, 4, 2, 1):
        small = bound < 2.0**-power
        bound = jnp.where(small, bound * 2.0**power, bound)
        scale = jnp.where(small, scale * 2.0**power, scale)
    scaled = inverse * scale
    high = scaled.astype(jnp.bfloat16)
    split_ref[:, 0:BCELLS] = high
    split_ref[:, BCELLS : 2 * BCELLS] = high
    split_ref[:, 2 * BCELLS : 3 * BCELLS] = (scaled - high.astype(F32)).astype(jnp.bfloat16)
    row = lax.broadcasted_iota(jnp.int32, (BCELLS, BCELLS), 0)
    column = lax.broadcasted_iota(jnp.int32, (BCELLS, BCELLS), 1)
    theta_ref[0] = jnp.sum(jnp.where(row == column, scaled, 0.0)) * (6.5 / BCELLS)


def precondition(split_ref, field_ref, out_ref, pair):
    base = pair * 2 * BCELLS
    field = jnp.concatenate(
        [field_ref[base + half * BCELLS : base + (half + 1) * BCELLS, :] for half in range(2)],
        axis=1,
    )
    top = field.astype(jnp.bfloat16)
    rest = (field - top.astype(F32)).astype(jnp.bfloat16)
    stacked = jnp.concatenate([top, rest, top], axis=0)
    found = jnp.dot(split_ref[...], stacked, preferred_element_type=F32)
    out_ref[base : base + BCELLS, :] = found[:, :LANES]
    out_ref[base + BCELLS : base + 2 * BCELLS, :] = found[:, LANES:]


def one_hot(code, out_ref, row, count, column):
    rows = 512
    width = code.shape[1]
    base = lax.broadcasted_iota(jnp.int32, (rows, width), 0).astype(jnp.int16)
    one = jnp.ones((rows, width), jnp.bfloat16)
    zero = jnp.zeros((rows, width), jnp.bfloat16)
    for start in range(0, count, rows):
        here = base == jnp.broadcast_to((code - start).astype(jnp.int16), (rows, width))
        out_ref[row + start : row + start + rows, column : column + width] = jnp.where(
            here, one, zero
        )


def select(odd, codes_ref, send_ref, sent_ref, taken_ref, local_ref):
    low, high = send_ref[0:1, :], send_ref[1:2, :]
    for index, which in enumerate(SENT):
        for column, code in (
            (0, jnp.where(odd == 1, high, low)), (HMAX, jnp.where(odd == 1, low, high))
        ):
            one_hot(code - which * BDEV, sent_ref, index * BDEV, BDEV, column)
    for index, which in enumerate(PRODUCT):
        for half in range(2):
            code = codes_ref[which : which + 1, half * BCELLS : (half + 1) * BCELLS]
            at = index * BDEV + half * BCELLS
            one_hot((code - REMOTE) ^ (odd * HMAX), taken_ref, 0, 2 * HMAX, at)
            one_hot(code - (which ^ 1) * BDEV, local_ref, 0, BDEV, at)


def halves(value):
    top = value.astype(jnp.bfloat16)
    return jnp.concatenate([top, (value - top.astype(F32)).astype(jnp.bfloat16)], axis=0)


def whole_layer(field_ref, which, chunk):
    start = chunk * BCELLS
    if which >= 4:
        return field_ref[pl.ds(start + (which - 4) * (BE - 1), FACE, stride=BE), :]
    if which < 2:
        row = start + which * (BE - 1) * FACE
        return field_ref[row : row + FACE, :]
    rows = [start + part * FACE + (which - 2) * (BE - 1) * BE for part in range(BE)]
    return jnp.concatenate([field_ref[row : row + SUB, :] for row in rows], axis=0)


def split_layers(field_ref, chunk, layers_ref):
    for index, which in enumerate(SPLIT):
        at = (index * CHUNKS + chunk) * LANES
        layers_ref[:, at : at + LANES] = halves(whole_layer(field_ref, which, chunk))


def pack(field_ref, layers_ref, sent_ref, send_ref, odd, cross_ref, inside_ref):
    low, high = send_ref[0:1, :], send_ref[1:2, :]
    for out_ref, start, codes in (
        (cross_ref, 0, jnp.where(odd, high, low)), (inside_ref, HMAX, jnp.where(odd, low, high))
    ):
        product = jnp.dot(
            layers_ref[:, BDEV:], sent_ref[:, start : start + HMAX], preferred_element_type=F32
        )
        product = product[:FACE, :] + product[FACE:, :]
        for step in range(2):
            code = jnp.broadcast_to(codes[:, step * LANES : (step + 1) * LANES], (SUB, LANES))
            lane = code & (LANES - 1)
            tile = code >> 7
            found = [
                product[part * SUB : (part + 1) * SUB, step * LANES : (step + 1) * LANES]
                for part in range(8)
            ]
            for which in range(6):
                if which in SENT:
                    continue
                for source in range(CHUNKS):
                    here = tile == which * CHUNKS + source
                    for part in range(8):
                        values = layer_tile(field_ref, which, part, source)
                        found[part] = jnp.where(here, pick(values, lane), found[part])
            for part in range(8):
                row = step * FACE + part * SUB
                out_ref[row : row + SUB, :] = found[part]


def layer_tile(field_ref, which, part, chunk):
    row = (part * BE, (BE - 1) * FACE + part * BE, part * FACE, part * FACE + (BE - 1) * BE)[which]
    row = row + chunk * BCELLS
    return field_ref[row : row + SUB, :]


def layer(faces_ref, chunk, which, part):
    base = (chunk * 6 + which) * FACE + part * SUB
    return faces_ref[base : base + SUB, :]


def gather_layers(pair, codes_ref, field_ref, layers_ref, local_ref, faces_ref):
    for index, which in enumerate(PRODUCT):
        at = index * BDEV + pair * (2 * LANES)
        start = SPLIT.index(which ^ 1) * BDEV
        found = jnp.dot(
            layers_ref[:, start : start + BDEV],
            local_ref[:, at : at + 2 * LANES],
            preferred_element_type=F32,
        )
        found = found[:FACE, :] + found[FACE:, :]
        for half in range(2):
            base = ((2 * pair + half) * 6 + which) * FACE
            faces_ref[base : base + FACE, :] = found[:, half * LANES : (half + 1) * LANES]
    for chunk in (2 * pair, 2 * pair + 1):
        at = slice(chunk * LANES, (chunk + 1) * LANES)
        for which in range(6):
            if which in PRODUCT:
                continue
            partner = which ^ 1
            code = jnp.broadcast_to(codes_ref[which : which + 1, at], (SUB, LANES))
            code = code - partner * BDEV
            lane = code & (LANES - 1)
            tile = code >> 7
            found = [jnp.zeros((SUB, LANES), F32) for _ in range(8)]
            for source in range(CHUNKS):
                here = tile == source
                for part in range(8):
                    values = layer_tile(field_ref, partner, part, source)
                    found[part] = jnp.where(here, pick(values, lane), found[part])
            for part in range(8):
                base = (chunk * 6 + which) * FACE + part * SUB
                faces_ref[base : base + SUB, :] = found[part]


def local_kernel(known, theta_ref, codes_ref, field_ref, layers_ref, local_ref, *refs):
    basis = refs[:known]
    faces_ref, beside_ref, sums_ref = refs[-3:]
    if known > 1:
        diagonal_ref, gram_in_ref, out_ref, gram_ref = refs[known:-3]
        gram_in = gram_in_ref[...]
    else:
        counts_ref, before_ref, old_ref, cross_ref, inside_ref, out_ref, gram_ref, diagonal_ref = (
            refs[1:9]
        )
        turned_ref = refs[9]
        gram_in = jnp.zeros((SUB, LANES), F32)
        assemble(
            counts_ref, before_ref[0], old_ref, cross_ref, inside_ref, diagonal_ref, turned_ref
        )
    theta = theta_ref[0]
    sums = [jnp.zeros((SUB, LANES), F32) for _ in range(known)]

    def stencil(chunk):
        start = chunk * BCELLS

        def block(i, j):
            row = start + (i * BE + j) * BE
            return field_ref[row : row + SUB, :]

        for i in range(BE):
            row = [layer(faces_ref, chunk, 4, i)]
            row += [field_ref[pl.ds(start + i * FACE + k, SUB, stride=BE), :] for k in range(BE)]
            row += [layer(faces_ref, chunk, 5, i)]
            for k in range(BE):
                beside_ref[pl.ds(start + i * FACE + k, SUB, stride=BE), :] = row[k] + row[k + 2]
        for i in range(BE):
            for j in range(BE):
                rows = slice(start + (i * BE + j) * BE, start + (i * BE + j + 1) * BE)
                beside = beside_ref[rows, :]
                beside = beside + (block(i - 1, j) if i > 0 else layer(faces_ref, chunk, 0, j))
                beside = beside + (
                    block(i + 1, j) if i < BE - 1 else layer(faces_ref, chunk, 1, j)
                )
                beside = beside + (block(i, j - 1) if j > 0 else layer(faces_ref, chunk, 2, i))
                beside = beside + (
                    block(i, j + 1) if j < BE - 1 else layer(faces_ref, chunk, 3, i)
                )
                newest = basis[-1][rows, :]
                value = (6.0 + diagonal_ref[rows, :]) * block(i, j) - beside
                out_ref[rows, :] = value - theta * newest
                for k, ref in enumerate(basis):
                    old = newest if k == known - 1 else ref[rows, :]
                    sums[k] = sums[k] + newest * old

    gather_layers(0, codes_ref, field_ref, layers_ref, local_ref, faces_ref)
    for pair in range(CHUNKS // 2):
        if pair + 1 < CHUNKS // 2:
            gather_layers(pair + 1, codes_ref, field_ref, layers_ref, local_ref, faces_ref)
        stencil(2 * pair)
        stencil(2 * pair + 1)
    for k, part in enumerate(sums):
        sums_ref[k] = part
    place_sums(sums_ref, known, gram_in, gram_ref, (known - 1) * known // 2)


def receive(cross_ref, inside_ref):
    parts = [
        ref[part * FACE : (part + 1) * FACE, :]
        for ref in (cross_ref, inside_ref)
        for part in range(2)
    ]
    return halves(jnp.concatenate(parts, axis=1))


def finish(odd, codes_ref, taken_ref, received, cross_ref, inside_ref, out_ref, pair):
    for which in range(6):
        if which in PRODUCT:
            at = PRODUCT.index(which) * BDEV + pair * 2 * LANES
            product = jnp.dot(
                received, taken_ref[:, at : at + 2 * LANES], preferred_element_type=F32
            )
            product = product[:FACE, :] + product[FACE:, :]
        for half in range(2):
            chunk = pair * 2 + half
            start = chunk * BCELLS
            if which in PRODUCT:
                beside = product[:, half * LANES : (half + 1) * LANES]
            else:
                code = codes_ref[which : which + 1, chunk * LANES : (chunk + 1) * LANES] - REMOTE
                code = jnp.broadcast_to(code, (SUB, LANES))
                lane = code & (LANES - 1)
                tile = (code >> 7) ^ (odd * 2)
                found = [jnp.zeros((SUB, LANES), F32) for _ in range(8)]
                for source in range(2 * HMAX // LANES):
                    here = tile == source
                    from_ref = cross_ref if source < HMAX // LANES else inside_ref
                    base = source % (HMAX // LANES) * FACE
                    for part in range(8):
                        values = from_ref[base + part * SUB : base + (part + 1) * SUB, :]
                        found[part] = jnp.where(here, pick(values, lane), found[part])
                beside = jnp.concatenate(found, axis=0)
            if which >= 4:
                rows = pl.ds(start + (which - 4) * (BE - 1), FACE, stride=BE)
                out_ref[rows, :] = out_ref[rows, :] - beside
            elif which < 2:
                row = start + which * (BE - 1) * FACE
                out_ref[row : row + FACE, :] = out_ref[row : row + FACE, :] - beside
            else:
                for part in range(BE):
                    row = start + part * FACE + (which - 2) * (BE - 1) * BE
                    out_ref[row : row + SUB, :] = (
                        out_ref[row : row + SUB, :] - beside[part * SUB : (part + 1) * SUB, :]
                    )


def place_sums(sums_ref, count, gram_in, gram_out_ref, first):
    lane = lax.broadcasted_iota(jnp.int32, (SUB, LANES), 1)
    row = gram_in
    for k in range(count):
        row = row + jnp.where(lane == first + k, jnp.sum(sums_ref[k]), 0.0)
    for start in range(0, gram_out_ref.shape[0], SUB):
        gram_out_ref[start : start + SUB, :] = row


def send(
    split_ref, value_ref, field_ref, layers_ref, sent_ref, send_ref, odd, cross_ref, inside_ref,
    before,
):
    for pair in range(CHUNKS // 2):
        before(pair)
        precondition(split_ref, value_ref, field_ref, pair)
        split_layers(field_ref, 2 * pair, layers_ref)
        split_layers(field_ref, 2 * pair + 1, layers_ref)
    pack(field_ref, layers_ref, sent_ref, send_ref, odd, cross_ref, inside_ref)


def first_kernel(
    counts_ref, old_ref, cross_ref, inside_ref, split_ref, sent_ref, send_ref,
    before_ref, rhs_ref, field_ref, layers_ref, to_cross_ref, to_inside_ref,
    turned_ref,
):
    odd = count_of(counts_ref, 3) == 1
    before = count_before(odd, cross_ref, inside_ref)
    before_ref[0] = before
    assemble(counts_ref, before, old_ref, cross_ref, inside_ref, rhs_ref, turned_ref)
    send(
        split_ref, rhs_ref, field_ref, layers_ref, sent_ref, send_ref, odd, to_cross_ref,
        to_inside_ref, lambda pair: None,
    )


def next_kernel(
    rank_ref, codes_ref, send_ref, cross_ref, inside_ref, partial_ref, taken_ref, split_ref,
    sent_ref,
    out_ref, field_ref, layers_ref, to_cross_ref, to_inside_ref,
):
    del partial_ref
    odd = rank_ref[0] & 1
    received = receive(cross_ref, inside_ref)

    def before(pair):
        finish(odd, codes_ref, taken_ref, received, cross_ref, inside_ref, out_ref, pair)

    send(
        split_ref, out_ref, field_ref, layers_ref, sent_ref, send_ref, odd == 1, to_cross_ref,
        to_inside_ref, before,
    )


def end_kernel(
    rank_ref, codes_ref, cross_ref, inside_ref, partial_ref, taken_ref, gram_in_ref, *refs
):
    del partial_ref
    basis = refs[: BASIS - 1]
    out_ref, gram_ref, sums_ref = refs[BASIS - 1 :]
    odd = rank_ref[0] & 1
    received = receive(cross_ref, inside_ref)
    sums = [jnp.zeros((SUB, LANES), F32) for _ in range(BASIS)]
    for pair in range(CHUNKS // 2):
        finish(odd, codes_ref, taken_ref, received, cross_ref, inside_ref, out_ref, pair)
        for row in range(pair * 2 * BCELLS, (pair + 1) * 2 * BCELLS, SUB):
            rows = slice(row, row + SUB)
            value = out_ref[rows, :]
            for k, ref in enumerate(basis):
                sums[k] = sums[k] + value * ref[rows, :]
            sums[-1] = sums[-1] + value * value
    for k, part in enumerate(sums):
        sums_ref[k] = part
    place_sums(sums_ref, BASIS, gram_in_ref[...], gram_ref, BASIS * (BASIS - 1) // 2)


def recurrence(gram, theta):
    def dot(left, right):
        total = None
        for a, x in enumerate(left):
            if x is None:
                continue
            part = None
            for b, y in enumerate(right):
                if y is not None:
                    term = gram[max(a, b)][min(a, b)] * y
                    part = term if part is None else part + term
            total = x * part if total is None else total + x * part
        return total

    def add(left, right):
        return [
            y if x is None else x if y is None else x + y for x, y in zip(left, right)
        ]

    def times(factor, vector):
        return [None if x is None else factor * x for x in vector]

    def apply(vector):
        return add([None] + vector[:-1], times(theta, vector))

    one = jnp.ones_like(theta)
    shadow = [one] + [None] * (BASIS - 1)
    residual = shadow
    direction = residual
    rho = gram[0][0]
    rho_next = rho
    total = [None] * BASIS
    along = alpha = omega = None
    for step in range(ITERS):
        if step > 0:
            beta = (rho_next / rho) * (alpha / omega)
            rho = rho_next
            direction = add(residual, times(beta, add(direction, times(-omega, along))))
        along = apply(direction)
        alpha = rho / dot(shadow, along)
        middle = add(residual, times(-alpha, along))
        image = apply(middle)
        omega = dot(image, middle) / dot(image, image)
        total = add(total, add(times(alpha, direction), times(omega, middle)))
        residual = add(middle, times(-omega, image))
        rho_next = dot(shadow, residual)
    return total, residual


def last_kernel(theta_ref, gathered_ref, *refs):
    basis = refs[:BASIS]
    fields = refs[BASIS : 2 * BASIS - 1]
    outs = refs[2 * BASIS - 1 : 2 * BASIS + 1]
    solution_ref, residual_ref, sems = refs[2 * BASIS + 1 :]
    row = jnp.sum(gathered_ref[...], axis=0, keepdims=True)
    lane = lax.broadcasted_iota(jnp.int32, (1, LANES), 1)

    def entry(k):
        return jnp.sum(jnp.where(lane == k, row, 0.0), axis=1, keepdims=True)

    gram = [[entry(a * (a + 1) // 2 + b) for b in range(a + 1)] for a in range(BASIS)]
    theta = jnp.full((1, 1), theta_ref[0])
    total, residual = recurrence(gram, theta)
    total = [None if x is None else jnp.broadcast_to(x, (SUB, LANES)) for x in total]
    residual = [jnp.broadcast_to(x, (SUB, LANES)) for x in residual]
    part = BCELLS // PARTS
    copies = []
    for block in range(PARTS):

        def body(step, carry, block=block):
            start = pl.multiple_of(block * part + step * SUB, SUB)
            for chunk in range(CHUNKS):
                rows = pl.ds(chunk * BCELLS + start, SUB)
                at = slice(chunk * LANES, (chunk + 1) * LANES)
                value = total[0] * fields[0][rows, :]
                for k in range(1, BASIS - 1):
                    value = value + total[k] * fields[k][rows, :]
                solution_ref[pl.ds(start, SUB), at] = value
                value = residual[0] * basis[0][rows, :]
                for k in range(1, BASIS):
                    value = value + residual[k] * basis[k][rows, :]
                residual_ref[pl.ds(start, SUB), at] = value
            return carry

        lax.fori_loop(0, part // SUB, body, 0, unroll=4)
        for k, ref in enumerate((solution_ref, residual_ref)):
            at = slice(block * part, (block + 1) * part)
            copies.append(
                pltpu.make_async_copy(ref.at[at, :], outs[k].at[at, :], sems.at[k, block])
            )
            copies[-1].start()
    for copy in copies:
        copy.wait()


def per_device(rhs_old, diagonal_old, new_owner, face_source, send_layers, block_inverse):
    def of(rows):
        return jax.ShapeDtypeStruct((rows, LANES), F32)

    field_type = of(CHUNKS * BCELLS)
    out_type = jax.ShapeDtypeStruct((BCELLS, BDEV), F32)
    halo_type = of(2 * FACE)
    split_type = jax.ShapeDtypeStruct((BCELLS, 3 * BCELLS), jnp.bfloat16)
    turned = pltpu.VMEM((2, BCELLS, LANES), F32)
    layers = [
        pltpu.VMEM((CHUNKS * 6 * FACE, LANES), F32),
        pltpu.VMEM((CHUNKS * BCELLS, LANES), F32),
    ]
    packed_type = jax.ShapeDtypeStruct((2 * FACE, len(SPLIT) * BDEV), jnp.bfloat16)
    sums = pltpu.VMEM((BASIS, SUB, LANES), F32)

    rank = lax.axis_index(AXES).astype(jnp.int32).reshape(1)
    counts, cross, inside = call(
        front_kernel,
        (
            jax.ShapeDtypeStruct((SUB, LANES), jnp.int32),
            of(2 * BCELLS + SUB),
            of(2 * BCELLS + SUB),
        ),
        (rank, new_owner.reshape(CAP // LANES, LANES), rhs_old),
        [SMEM, VMEM, HBM],
        (VMEM, VMEM, VMEM),
        [
            pltpu.VMEM((BCELLS, MOVE), F32),
            pltpu.VMEM((BCELLS, CAP - 2 * MOVE), F32),
            pltpu.SemaphoreType.DMA((2,)),
        ],
        limit=FRONT,
    )
    rhs_cross = swapped(cross, True)
    rhs_inside = swapped(inside, False)
    cross, inside = call(
        cut_kernel,
        (of(2 * BCELLS), of(2 * BCELLS)),
        (counts, diagonal_old),
        [VMEM, VMEM],
        (VMEM, VMEM),
    )
    diagonal_cross = swapped(cross, True)
    diagonal_inside = swapped(inside, False)
    split, theta, sent, taken, local = call(
        prepare_kernel,
        (
            split_type,
            jax.ShapeDtypeStruct((1,), F32),
            jax.ShapeDtypeStruct((len(SENT) * BDEV, 2 * HMAX), jnp.bfloat16),
            jax.ShapeDtypeStruct((2 * HMAX, len(PRODUCT) * BDEV), jnp.bfloat16),
            jax.ShapeDtypeStruct((BDEV, len(PRODUCT) * BDEV), jnp.bfloat16),
        ),
        (rank, block_inverse, face_source, send_layers),
        [SMEM] + [VMEM] * 3,
        (VMEM, SMEM, VMEM, VMEM, VMEM),
    )
    before, rhs, field, packed, to_cross, to_inside = call(
        first_kernel,
        (jax.ShapeDtypeStruct((1,), jnp.int32),)
        + (field_type, field_type, packed_type, halo_type, halo_type),
        (counts, rhs_old, rhs_cross, rhs_inside, split, sent, send_layers),
        [VMEM] * 7,
        (SMEM,) + (VMEM,) * 5,
        [turned],
        flops=10**9,
        bytes_accessed=8 * MIB,
    )
    diagonal = gram = None
    basis = [rhs]
    fields = [field]
    for known in range(1, BASIS):
        from_cross = swapped(to_cross, True)
        from_inside = swapped(to_inside, False)
        args = [theta, face_source, field, packed, local] + basis
        outs = [field_type, of(SUB)]
        specs = [SMEM] + [VMEM] * (len(args) - 1)
        if known > 1:
            args += [diagonal, gram]
            specs += [VMEM, VMEM]
            scratch = layers + [sums]
        else:
            args += [counts, before, diagonal_old, diagonal_cross, diagonal_inside]
            specs += [VMEM, SMEM] + [VMEM] * 3
            outs.append(field_type)
            scratch = [turned] + layers + [sums]
        found = call(
            functools.partial(local_kernel, known),
            tuple(outs),
            tuple(args),
            specs,
            (VMEM,) * len(outs),
            scratch,
            flops=10**9,
            bytes_accessed=4 * MIB,
        )
        partial, gram = found[:2]
        if known == 1:
            diagonal = found[2]
        if known < BASIS - 1:
            value, field, packed, to_cross, to_inside = call(
                next_kernel,
                (field_type, field_type, packed_type, halo_type, halo_type),
                (
                    rank, face_source, send_layers, from_cross, from_inside, partial, taken,
                    split, sent,
                ),
                [SMEM] + [VMEM] * 8,
                (VMEM,) * 5,
                flops=10**9,
                bytes_accessed=12 * MIB,
                aliases={5: 0},
            )
            fields.append(field)
        else:
            value, copies = call(
                end_kernel,
                (field_type, of(lax.axis_size(AXES))),
                (rank, face_source, from_cross, from_inside, partial, taken, gram, *basis),
                [SMEM] + [VMEM] * (6 + len(basis)),
                (VMEM, VMEM),
                [sums],
                flops=10**9,
                bytes_accessed=12 * MIB,
                aliases={4: 0},
            )
        basis.append(value)
    gathered = lax.all_to_all(copies, AXES, split_axis=0, concat_axis=0, tiled=True)
    return call(
        last_kernel,
        (out_type, out_type),
        (theta, gathered, *basis, *fields),
        [SMEM] + [VMEM] * (2 * BASIS),
        (HBM, HBM),
        [pltpu.VMEM((BCELLS, BDEV), F32)] * 2 + [pltpu.SemaphoreType.DMA((2, PARTS))],
        limit=16,
    )


def solution(mesh):
    return jax.shard_map(
        per_device,
        mesh=mesh,
        in_specs=(
            P(None, AXES),
            P(None, AXES),
            P(AXES),
            P(None, AXES),
            P(None, AXES),
            P(),
        ),
        out_specs=(P(None, AXES), P(None, AXES)),
        check_vma=False,
    )
```

```python
import functools

import jax
import jax.numpy as jnp
from jax import lax
from jax.experimental import pallas as pl
from jax.experimental.pallas import tpu as pltpu
from jax.sharding import PartitionSpec as P

BE = 8
BCELLS = 512
FACE = 64
BDEV = 1024
MOVE = 256
CAP = 1536
HMAX = 256
ITERS = 2
LANES = 128
SUB = 8
CHUNKS = BDEV // LANES
AXES = ("gx", "gy", "gz")
REMOTE = 6 * BDEV
BASIS = 2 * ITERS + 1
MIB = 1024 * 1024
PARTS = 8
FRONT = 52
PRODUCT = (0, 4, 5)
SENT = (4, 5, 0, 3)
SPLIT = (1,) + SENT
F32 = jnp.float32

VMEM = pl.BlockSpec(memory_space=pltpu.VMEM)
SMEM = pl.BlockSpec(memory_space=pltpu.SMEM)
HBM = pl.BlockSpec(memory_space=pltpu.HBM)


def swapped(value, cross):
    count = lax.axis_size(AXES)
    first = 1 if cross else 0
    pairs = [(low, low + 1) for low in range(first, count - 1, 2)]
    return lax.ppermute(value, AXES, pairs + [(high, low) for low, high in pairs])


def call(kernel, outs, args, in_specs, out_specs, scratch=(), limit=16, flops=0, bytes_accessed=0, aliases=None):
    if aliases is None:
        aliases = {}
    return pl.pallas_call(
        kernel,
        out_shape=outs,
        in_specs=in_specs,
        out_specs=out_specs,
        scratch_shapes=list(scratch),
        input_output_aliases=aliases,
        compiler_params=pltpu.CompilerParams(vmem_limit_bytes=limit * MIB),
        cost_estimate=pl.CostEstimate(
            flops=flops, bytes_accessed=bytes_accessed, transcendentals=0
        ),
    )(*args)


def lane_iota(rows=SUB):
    return lax.broadcasted_iota(jnp.int32, (rows, LANES), 1)


def lanes(start):
    return pl.ds(pl.multiple_of(start, LANES), LANES)


def pick(values, index):
    return jnp.take_along_axis(values, index, axis=1, mode="promise_in_bounds")


def cut_rows(start, low_ref, high_ref, odd, count, cross_ref, inside_ref):
    tile = start >> 7
    shift = start & (LANES - 1)
    rows = 128

    for step in range(BCELLS // rows):
        at = slice(step * rows, (step + 1) * rows)
        first = lane_iota(rows) < LANES - shift
        turned = []
        for part in range(3):
            source = jnp.minimum(tile + part, high_ref.shape[1] // LANES - 1) * LANES
            turned.append(pltpu.roll(high_ref[at, lanes(source)], (LANES - shift) & (LANES - 1), 1))
        for half in range(2):
            lower = low_ref[at, half * LANES : (half + 1) * LANES]
            upper = jnp.where(first, turned[half], turned[half + 1])
            to = slice(half * BCELLS + step * rows, half * BCELLS + (step + 1) * rows)
            cross_ref[to, :] = jnp.where(odd, upper, lower)
            inside_ref[to, :] = jnp.where(odd, lower, upper)
    if count is not None:
        row = jnp.full((SUB, LANES), count.astype(F32))
        cross_ref[2 * BCELLS : 2 * BCELLS + SUB, :] = row
        inside_ref[2 * BCELLS : 2 * BCELLS + SUB, :] = row


def front_kernel(
    rank_ref, owner_ref, old_ref, counts_ref, cross_ref, inside_ref, low_ref, high_ref, sems
):
    high_copy = pltpu.make_async_copy(
        old_ref.at[:, pl.ds(2 * MOVE, CAP - 2 * MOVE)], high_ref, sems.at[1]
    )
    high_copy.start()
    low_copy = pltpu.make_async_copy(old_ref.at[:, pl.ds(0, MOVE)], low_ref, sems.at[0])
    low_copy.start()
    rank = rank_ref[0]
    owner = owner_ref[...]
    filled = owner >= 0
    head = jnp.sum(((owner == rank - 1) & filled).astype(jnp.int32))
    stay = jnp.sum((owner == rank).astype(jnp.int32))
    tail = jnp.sum(((owner == rank + 1) & filled).astype(jnp.int32))
    odd = rank & 1
    row = lax.broadcasted_iota(jnp.int32, (SUB, LANES), 0)
    counts_ref[...] = jnp.where(
        row == 0, head, jnp.where(row == 1, stay, jnp.where(row == 2, tail, odd))
    )
    high_copy.wait()
    low_copy.wait()
    start = head + stay - 2 * MOVE
    cut_rows(start, low_ref, high_ref, odd == 1, tail, cross_ref, inside_ref)


def count_of(counts_ref, row):
    return jnp.max(counts_ref[row : row + 1, :])


def cut_kernel(counts_ref, old_ref, cross_ref, inside_ref):
    start = count_of(counts_ref, 0) + count_of(counts_ref, 1)
    odd = count_of(counts_ref, 3) == 1
    cut_rows(start, old_ref, old_ref, odd, None, cross_ref, inside_ref)


def count_before(odd, cross_ref, inside_ref):
    row = slice(2 * BCELLS, 2 * BCELLS + SUB)
    return jnp.max(jnp.where(odd, inside_ref[row, :], cross_ref[row, :])).astype(jnp.int32)


def assemble(counts_ref, before, old_ref, cross_ref, inside_ref, out_ref, turned_ref):
    head = count_of(counts_ref, 0)
    stay = count_of(counts_ref, 1)
    odd = count_of(counts_ref, 3) == 1
    own_start = head - before
    own_tile = own_start >> 7
    own_shift = own_start & (LANES - 1)
    up_start = -(before + stay)
    up_tile = up_start >> 7
    up_shift = up_start & (LANES - 1)
    rows = 64
    lane = lane_iota(rows)
    for start in range(0, BCELLS, rows):
        for part in range(2):
            half = slice(part * BCELLS + start, part * BCELLS + start + rows)
            turned_ref[part, start : start + rows, :] = pltpu.roll(
                jnp.where(odd, cross_ref[half, :], inside_ref[half, :]),
                (LANES - up_shift) & (LANES - 1),
                1,
            )
    for start in range(0, BCELLS, rows):
        at = slice(start, start + rows)
        last = None
        for chunk in range(CHUNKS + 1):
            source = jnp.clip(own_tile + chunk, 0, CAP // LANES - 1) * LANES
            now = pltpu.roll(
                old_ref[at, lanes(source)], (LANES - own_shift) & (LANES - 1), 1
            )
            if chunk > 0:
                place = chunk - 1
                column = lane + place * LANES
                value = jnp.where(lane < LANES - own_shift, last, now)
                if place >= 2 * MOVE // LANES:
                    low_half = turned_ref[jnp.clip(up_tile + place, 0, 1), at, :]
                    high_half = turned_ref[jnp.clip(up_tile + place + 1, 0, 1), at, :]
                    above = jnp.where(lane < LANES - up_shift, low_half, high_half)
                    value = jnp.where(column < before + stay, value, above)
                if place < MOVE // LANES:
                    half = slice(place * BCELLS + start, place * BCELLS + start + rows)
                    below = jnp.where(odd, inside_ref[half, :], cross_ref[half, :])
                    value = jnp.where(column < before, below, value)
                out_ref[place * BCELLS + start : place * BCELLS + start + rows, :] = value
            last = now


def prepare_kernel(
    rank_ref, inverse_ref, codes_ref, send_ref, split_ref, theta_ref, sent_ref, taken_ref, local_ref
):
    select(rank_ref[0] & 1, codes_ref, send_ref, sent_ref, taken_ref, local_ref)
    inverse = inverse_ref[...]
    size = jnp.abs(inverse)
    by_row = jnp.max(jnp.sum(size, axis=1, keepdims=True), axis=0, keepdims=True)
    by_column = jnp.max(jnp.sum(size, axis=0, keepdims=True), axis=1, keepdims=True)
    bound = 14.5 * jnp.sqrt(by_row) * jnp.sqrt(by_column)
    scale = jnp.full((1, 1), 0.5, F32)
    for power in (64, 32, 16, 8, 4, 2, 1):
        large = bound >= 2.0**power
        bound = jnp.where(large, bound * 2.0**-power, bound)
        scale = jnp.where(large, scale * 2.0**-power, scale)
    for power in (64, 32, 16, 8, 4, 2, 1):
        small = bound < 2.0**-power
        bound = jnp.where(small, bound * 2.0**power, bound)
        scale = jnp.where(small, scale * 2.0**power, scale)
    scaled = inverse * scale
    high = scaled.astype(jnp.bfloat16)
    split_ref[:, 0:BCELLS] = high
    split_ref[:, BCELLS : 2 * BCELLS] = high
    split_ref[:, 2 * BCELLS : 3 * BCELLS] = (scaled - high.astype(F32)).astype(jnp.bfloat16)
    row = lax.broadcasted_iota(jnp.int32, (BCELLS, BCELLS), 0)
    column = lax.broadcasted_iota(jnp.int32, (BCELLS, BCELLS), 1)
    theta = jnp.sum(jnp.where(row == column, scaled, 0.0)) * (6.5 / BCELLS)
    theta_ref[...] = jnp.full((SUB, LANES), theta)


def precondition(split_ref, field_ref, out_ref, pair):
    base = pair * 2 * BCELLS
    field = jnp.concatenate(
        [field_ref[base + half * BCELLS : base + (half + 1) * BCELLS, :] for half in range(2)],
        axis=1,
    )
    top = field.astype(jnp.bfloat16)
    rest = (field - top.astype(F32)).astype(jnp.bfloat16)
    stacked = jnp.concatenate([top, rest, top], axis=0)
    found = jnp.dot(split_ref[...], stacked, preferred_element_type=F32)
    out_ref[base : base + BCELLS, :] = found[:, :LANES]
    out_ref[base + BCELLS : base + 2 * BCELLS, :] = found[:, LANES:]


def one_hot(code, out_ref, row, count, column):
    rows = 512
    width = code.shape[1]
    base = lax.broadcasted_iota(jnp.int32, (rows, width), 0).astype(jnp.int16)
    one = jnp.ones((rows, width), jnp.bfloat16)
    zero = jnp.zeros((rows, width), jnp.bfloat16)
    for start in range(0, count, rows):
        here = base == jnp.broadcast_to((code - start).astype(jnp.int16), (rows, width))
        out_ref[row + start : row + start + rows, column : column + width] = jnp.where(
            here, one, zero
        )


def select(odd, codes_ref, send_ref, sent_ref, taken_ref, local_ref):
    low, high = send_ref[0:1, :], send_ref[1:2, :]
    for index, which in enumerate(SENT):
        for column, code in (
            (0, jnp.where(odd == 1, high, low)), (HMAX, jnp.where(odd == 1, low, high))
        ):
            one_hot(code - which * BDEV, sent_ref, index * BDEV, BDEV, column)
    for index, which in enumerate(PRODUCT):
        for half in range(2):
            code = codes_ref[which : which + 1, half * BCELLS : (half + 1) * BCELLS]
            at = index * BDEV + half * BCELLS
            one_hot((code - REMOTE) ^ (odd * HMAX), taken_ref, 0, 2 * HMAX, at)
            one_hot(code - (which ^ 1) * BDEV, local_ref, 0, BDEV, at)


def halves(value):
    top = value.astype(jnp.bfloat16)
    return jnp.concatenate([top, (value - top.astype(F32)).astype(jnp.bfloat16)], axis=0)


def whole_layer(field_ref, which, chunk):
    start = chunk * BCELLS
    if which >= 4:
        return field_ref[pl.ds(start + (which - 4) * (BE - 1), FACE, stride=BE), :]
    if which < 2:
        row = start + which * (BE - 1) * FACE
        return field_ref[row : row + FACE, :]
    rows = [start + part * FACE + (which - 2) * (BE - 1) * BE for part in range(BE)]
    return jnp.concatenate([field_ref[row : row + SUB, :] for row in rows], axis=0)


def split_layers(field_ref, chunk, layers_ref):
    for index, which in enumerate(SPLIT):
        at = (index * CHUNKS + chunk) * LANES
        layers_ref[:, at : at + LANES] = halves(whole_layer(field_ref, which, chunk))


def pack(field_ref, layers_ref, sent_ref, send_ref, odd, cross_ref, inside_ref):
    low, high = send_ref[0:1, :], send_ref[1:2, :]
    odd = jnp.concatenate([odd, odd], axis=1) == 1
    for out_ref, start, codes in (
        (cross_ref, 0, jnp.where(odd, high, low)), (inside_ref, HMAX, jnp.where(odd, low, high))
    ):
        product = jnp.dot(
            layers_ref[:, BDEV:], sent_ref[:, start : start + HMAX], preferred_element_type=F32
        )
        product = product[:FACE, :] + product[FACE:, :]
        for step in range(2):
            code = jnp.broadcast_to(codes[:, step * LANES : (step + 1) * LANES], (SUB, LANES))
            lane = code & (LANES - 1)
            tile = code >> 7
            found = [
                product[part * SUB : (part + 1) * SUB, step * LANES : (step + 1) * LANES]
                for part in range(8)
            ]
            for which in range(6):
                if which in SENT:
                    continue
                for source in range(CHUNKS):
                    here = tile == which * CHUNKS + source
                    for part in range(8):
                        values = layer_tile(field_ref, which, part, source)
                        found[part] = jnp.where(here, pick(values, lane), found[part])
            for part in range(8):
                row = step * FACE + part * SUB
                out_ref[row : row + SUB, :] = found[part]


def layer_tile(field_ref, which, part, chunk):
    row = (part * BE, (BE - 1) * FACE + part * BE, part * FACE, part * FACE + (BE - 1) * BE)[which]
    row = row + chunk * BCELLS
    return field_ref[row : row + SUB, :]


def layer(faces_ref, chunk, which, part):
    base = (chunk * 6 + which) * FACE + part * SUB
    return faces_ref[base : base + SUB, :]


def gather_layers(pair, codes_ref, field_ref, layers_ref, local_ref, faces_ref):
    for index, which in enumerate(PRODUCT):
        at = index * BDEV + pair * (2 * LANES)
        start = SPLIT.index(which ^ 1) * BDEV
        found = jnp.dot(
            layers_ref[:, start : start + BDEV],
            local_ref[:, at : at + 2 * LANES],
            preferred_element_type=F32,
        )
        found = found[:FACE, :] + found[FACE:, :]
        for half in range(2):
            base = ((2 * pair + half) * 6 + which) * FACE
            faces_ref[base : base + FACE, :] = found[:, half * LANES : (half + 1) * LANES]
    for chunk in (2 * pair, 2 * pair + 1):
        at = slice(chunk * LANES, (chunk + 1) * LANES)
        for which in range(6):
            if which in PRODUCT:
                continue
            partner = which ^ 1
            code = jnp.broadcast_to(codes_ref[which : which + 1, at], (SUB, LANES))
            code = code - partner * BDEV
            lane = code & (LANES - 1)
            tile = code >> 7
            found = [jnp.zeros((SUB, LANES), F32) for _ in range(8)]
            for source in range(CHUNKS):
                here = tile == source
                for part in range(8):
                    values = layer_tile(field_ref, partner, part, source)
                    found[part] = jnp.where(here, pick(values, lane), found[part])
            for part in range(8):
                base = (chunk * 6 + which) * FACE + part * SUB
                faces_ref[base : base + SUB, :] = found[part]


def local_kernel(known, theta_ref, codes_ref, field_ref, layers_ref, local_ref, *refs):
    basis = refs[:known]
    faces_ref, beside_ref, sums_ref = refs[-3:]
    if known > 1:
        diagonal_ref, gram_in_ref, out_ref, gram_ref = refs[known:-3]
        gram_in = gram_in_ref[...]
    else:
        counts_ref, before_ref, old_ref, cross_ref, inside_ref, out_ref, gram_ref, diagonal_ref = (
            refs[1:9]
        )
        turned_ref = refs[9]
        gram_in = jnp.zeros((SUB, LANES), F32)
        assemble(
            counts_ref, count_of(before_ref, 0), old_ref, cross_ref, inside_ref, diagonal_ref, turned_ref
        )
    theta = theta_ref[...]
    sums = [jnp.zeros((SUB, LANES), F32) for _ in range(known)]

    def stencil(chunk):
        start = chunk * BCELLS

        def block(i, j):
            row = start + (i * BE + j) * BE
            return field_ref[row : row + SUB, :]

        for i in range(BE):
            row = [layer(faces_ref, chunk, 4, i)]
            row += [field_ref[pl.ds(start + i * FACE + k, SUB, stride=BE), :] for k in range(BE)]
            row += [layer(faces_ref, chunk, 5, i)]
            for k in range(BE):
                beside_ref[pl.ds(start + i * FACE + k, SUB, stride=BE), :] = row[k] + row[k + 2]
        for i in range(BE):
            for j in range(BE):
                rows = slice(start + (i * BE + j) * BE, start + (i * BE + j + 1) * BE)
                beside = beside_ref[rows, :]
                beside = beside + (block(i - 1, j) if i > 0 else layer(faces_ref, chunk, 0, j))
                beside = beside + (
                    block(i + 1, j) if i < BE - 1 else layer(faces_ref, chunk, 1, j)
                )
                beside = beside + (block(i, j - 1) if j > 0 else layer(faces_ref, chunk, 2, i))
                beside = beside + (
                    block(i, j + 1) if j < BE - 1 else layer(faces_ref, chunk, 3, i)
                )
                newest = basis[-1][rows, :]
                value = (6.0 + diagonal_ref[rows, :]) * block(i, j) - beside
                out_ref[rows, :] = value - theta * newest
                for k, ref in enumerate(basis):
                    old = newest if k == known - 1 else ref[rows, :]
                    sums[k] = sums[k] + newest * old

    gather_layers(0, codes_ref, field_ref, layers_ref, local_ref, faces_ref)
    for pair in range(CHUNKS // 2):
        if pair + 1 < CHUNKS // 2:
            gather_layers(pair + 1, codes_ref, field_ref, layers_ref, local_ref, faces_ref)
        stencil(2 * pair)
        stencil(2 * pair + 1)
    for k, part in enumerate(sums):
        sums_ref[k] = part
    place_sums(sums_ref, known, gram_in, gram_ref, (known - 1) * known // 2)


def receive(cross_ref, inside_ref):
    parts = [
        ref[part * FACE : (part + 1) * FACE, :]
        for ref in (cross_ref, inside_ref)
        for part in range(2)
    ]
    return halves(jnp.concatenate(parts, axis=1))


def finish(odd, codes_ref, taken_ref, received, cross_ref, inside_ref, out_ref, pair):
    for which in range(6):
        if which in PRODUCT:
            at = PRODUCT.index(which) * BDEV + pair * 2 * LANES
            product = jnp.dot(
                received, taken_ref[:, at : at + 2 * LANES], preferred_element_type=F32
            )
            product = product[:FACE, :] + product[FACE:, :]
        for half in range(2):
            chunk = pair * 2 + half
            start = chunk * BCELLS
            if which in PRODUCT:
                beside = product[:, half * LANES : (half + 1) * LANES]
            else:
                code = codes_ref[which : which + 1, chunk * LANES : (chunk + 1) * LANES] - REMOTE
                lane = jnp.broadcast_to(code & (LANES - 1), (SUB, LANES))
                tile = jnp.broadcast_to((code >> 7) ^ (odd * 2), (SUB, LANES))
                found = [jnp.zeros((SUB, LANES), F32) for _ in range(8)]
                for source in range(2 * HMAX // LANES):
                    here = tile == source
                    from_ref = cross_ref if source < HMAX // LANES else inside_ref
                    base = source % (HMAX // LANES) * FACE
                    for part in range(8):
                        values = from_ref[base + part * SUB : base + (part + 1) * SUB, :]
                        found[part] = jnp.where(here, pick(values, lane), found[part])
                beside = jnp.concatenate(found, axis=0)
            if which >= 4:
                rows = pl.ds(start + (which - 4) * (BE - 1), FACE, stride=BE)
                out_ref[rows, :] = out_ref[rows, :] - beside
            elif which < 2:
                row = start + which * (BE - 1) * FACE
                out_ref[row : row + FACE, :] = out_ref[row : row + FACE, :] - beside
            else:
                for part in range(BE):
                    row = start + part * FACE + (which - 2) * (BE - 1) * BE
                    out_ref[row : row + SUB, :] = (
                        out_ref[row : row + SUB, :] - beside[part * SUB : (part + 1) * SUB, :]
                    )


def place_sums(sums_ref, count, gram_in, gram_out_ref, first):
    lane = lax.broadcasted_iota(jnp.int32, (SUB, LANES), 1)
    row = gram_in
    for k in range(count):
        row = row + jnp.where(lane == first + k, jnp.sum(sums_ref[k]), 0.0)
    for start in range(0, gram_out_ref.shape[0], SUB):
        gram_out_ref[start : start + SUB, :] = row


def send(
    split_ref, value_ref, field_ref, layers_ref, sent_ref, send_ref, odd, cross_ref, inside_ref,
    before,
):
    for pair in range(CHUNKS // 2):
        before(pair)
        precondition(split_ref, value_ref, field_ref, pair)
        split_layers(field_ref, 2 * pair, layers_ref)
        split_layers(field_ref, 2 * pair + 1, layers_ref)
    pack(field_ref, layers_ref, sent_ref, send_ref, odd, cross_ref, inside_ref)


def first_kernel(
    counts_ref, old_ref, cross_ref, inside_ref, split_ref, sent_ref, send_ref,
    before_ref, rhs_ref, field_ref, layers_ref, to_cross_ref, to_inside_ref,
    turned_ref,
):
    odd = count_of(counts_ref, 3) == 1
    before = count_before(odd, cross_ref, inside_ref)
    before_ref[...] = jnp.full((SUB, LANES), before)
    assemble(counts_ref, before, old_ref, cross_ref, inside_ref, rhs_ref, turned_ref)
    send(
        split_ref, rhs_ref, field_ref, layers_ref, sent_ref, send_ref, counts_ref[3:4, :],
        to_cross_ref, to_inside_ref, lambda pair: None,
    )


def next_kernel(
    counts_ref, codes_ref, send_ref, cross_ref, inside_ref, partial_ref, taken_ref, split_ref,
    sent_ref,
    out_ref, field_ref, layers_ref, to_cross_ref, to_inside_ref,
):
    del partial_ref
    odd = counts_ref[3:4, :]
    received = receive(cross_ref, inside_ref)

    def before(pair):
        finish(odd, codes_ref, taken_ref, received, cross_ref, inside_ref, out_ref, pair)

    send(
        split_ref, out_ref, field_ref, layers_ref, sent_ref, send_ref, odd, to_cross_ref,
        to_inside_ref, before,
    )


def end_kernel(
    counts_ref, codes_ref, cross_ref, inside_ref, partial_ref, taken_ref, gram_in_ref, *refs
):
    del partial_ref
    basis = refs[: BASIS - 1]
    out_ref, gram_ref, sums_ref = refs[BASIS - 1 :]
    odd = counts_ref[3:4, :]
    received = receive(cross_ref, inside_ref)
    sums = [jnp.zeros((SUB, LANES), F32) for _ in range(BASIS)]
    for pair in range(CHUNKS // 2):
        finish(odd, codes_ref, taken_ref, received, cross_ref, inside_ref, out_ref, pair)
        for row in range(pair * 2 * BCELLS, (pair + 1) * 2 * BCELLS, SUB):
            rows = slice(row, row + SUB)
            value = out_ref[rows, :]
            for k, ref in enumerate(basis):
                sums[k] = sums[k] + value * ref[rows, :]
            sums[-1] = sums[-1] + value * value
    for k, part in enumerate(sums):
        sums_ref[k] = part
    place_sums(sums_ref, BASIS, gram_in_ref[...], gram_ref, BASIS * (BASIS - 1) // 2)


def recurrence(gram, theta):
    def dot(left, right):
        total = None
        for a, x in enumerate(left):
            if x is None:
                continue
            part = None
            for b, y in enumerate(right):
                if y is not None:
                    term = gram[max(a, b)][min(a, b)] * y
                    part = term if part is None else part + term
            total = x * part if total is None else total + x * part
        return total

    def add(left, right):
        return [
            y if x is None else x if y is None else x + y for x, y in zip(left, right)
        ]

    def times(factor, vector):
        return [None if x is None else factor * x for x in vector]

    def apply(vector):
        return add([None] + vector[:-1], times(theta, vector))

    one = jnp.ones_like(theta)
    shadow = [one] + [None] * (BASIS - 1)
    residual = shadow
    direction = residual
    rho = gram[0][0]
    rho_next = rho
    total = [None] * BASIS
    along = alpha = omega = None
    for step in range(ITERS):
        if step > 0:
            beta = (rho_next / rho) * (alpha / omega)
            rho = rho_next
            direction = add(residual, times(beta, add(direction, times(-omega, along))))
        along = apply(direction)
        alpha = rho / dot(shadow, along)
        middle = add(residual, times(-alpha, along))
        image = apply(middle)
        omega = dot(image, middle) / dot(image, image)
        total = add(total, add(times(alpha, direction), times(omega, middle)))
        residual = add(middle, times(-omega, image))
        rho_next = dot(shadow, residual)
    return total, residual


def last_kernel(theta_ref, gathered_ref, *refs):
    basis = refs[:BASIS]
    fields = refs[BASIS : 2 * BASIS - 1]
    outs = refs[2 * BASIS - 1 : 2 * BASIS + 1]
    solution_ref, residual_ref, sems = refs[2 * BASIS + 1 :]
    row = jnp.sum(gathered_ref[...], axis=0, keepdims=True)
    lane = lax.broadcasted_iota(jnp.int32, (1, LANES), 1)

    def entry(k):
        return jnp.sum(jnp.where(lane == k, row, 0.0), axis=1, keepdims=True)

    gram = [[entry(a * (a + 1) // 2 + b) for b in range(a + 1)] for a in range(BASIS)]
    theta = theta_ref[0:1, 0:1]
    total, residual = recurrence(gram, theta)
    total = [None if x is None else jnp.broadcast_to(x, (SUB, LANES)) for x in total]
    residual = [jnp.broadcast_to(x, (SUB, LANES)) for x in residual]
    part = BCELLS // PARTS
    copies = []
    for block in range(PARTS):

        def body(step, carry, block=block):
            start = pl.multiple_of(block * part + step * SUB, SUB)
            for chunk in range(CHUNKS):
                rows = pl.ds(chunk * BCELLS + start, SUB)
                at = slice(chunk * LANES, (chunk + 1) * LANES)
                value = total[0] * fields[0][rows, :]
                for k in range(1, BASIS - 1):
                    value = value + total[k] * fields[k][rows, :]
                solution_ref[pl.ds(start, SUB), at] = value
                value = residual[0] * basis[0][rows, :]
                for k in range(1, BASIS):
                    value = value + residual[k] * basis[k][rows, :]
                residual_ref[pl.ds(start, SUB), at] = value
            return carry

        lax.fori_loop(0, part // SUB, body, 0, unroll=4)
        for k, ref in enumerate((solution_ref, residual_ref)):
            at = slice(block * part, (block + 1) * part)
            copies.append(
                pltpu.make_async_copy(ref.at[at, :], outs[k].at[at, :], sems.at[k, block])
            )
            copies[-1].start()
    for copy in copies:
        copy.wait()


def per_device(rhs_old, diagonal_old, new_owner, face_source, send_layers, block_inverse):
    def of(rows):
        return jax.ShapeDtypeStruct((rows, LANES), F32)

    field_type = of(CHUNKS * BCELLS)
    out_type = jax.ShapeDtypeStruct((BCELLS, BDEV), F32)
    halo_type = of(2 * FACE)
    split_type = jax.ShapeDtypeStruct((BCELLS, 3 * BCELLS), jnp.bfloat16)
    turned = pltpu.VMEM((2, BCELLS, LANES), F32)
    layers = [
        pltpu.VMEM((CHUNKS * 6 * FACE, LANES), F32),
        pltpu.VMEM((CHUNKS * BCELLS, LANES), F32),
    ]
    packed_type = jax.ShapeDtypeStruct((2 * FACE, len(SPLIT) * BDEV), jnp.bfloat16)
    sums = pltpu.VMEM((BASIS, SUB, LANES), F32)

    rank = lax.axis_index(AXES).astype(jnp.int32).reshape(1)
    counts, cross, inside = call(
        front_kernel,
        (
            jax.ShapeDtypeStruct((SUB, LANES), jnp.int32),
            of(2 * BCELLS + SUB),
            of(2 * BCELLS + SUB),
        ),
        (rank, new_owner.reshape(CAP // LANES, LANES), rhs_old),
        [SMEM, VMEM, HBM],
        (VMEM, VMEM, VMEM),
        [
            pltpu.VMEM((BCELLS, MOVE), F32),
            pltpu.VMEM((BCELLS, CAP - 2 * MOVE), F32),
            pltpu.SemaphoreType.DMA((2,)),
        ],
        limit=FRONT,
    )
    rhs_cross = swapped(cross, True)
    rhs_inside = swapped(inside, False)
    cross, inside = call(
        cut_kernel,
        (of(2 * BCELLS), of(2 * BCELLS)),
        (counts, diagonal_old),
        [VMEM, VMEM],
        (VMEM, VMEM),
    )
    diagonal_cross = swapped(cross, True)
    diagonal_inside = swapped(inside, False)
    split, theta, sent, taken, local = call(
        prepare_kernel,
        (
            split_type,
            of(SUB),
            jax.ShapeDtypeStruct((len(SENT) * BDEV, 2 * HMAX), jnp.bfloat16),
            jax.ShapeDtypeStruct((2 * HMAX, len(PRODUCT) * BDEV), jnp.bfloat16),
            jax.ShapeDtypeStruct((BDEV, len(PRODUCT) * BDEV), jnp.bfloat16),
        ),
        (rank, block_inverse, face_source, send_layers),
        [SMEM] + [VMEM] * 3,
        (VMEM,) * 5,
    )
    before, rhs, field, packed, to_cross, to_inside = call(
        first_kernel,
        (jax.ShapeDtypeStruct((SUB, LANES), jnp.int32),)
        + (field_type, field_type, packed_type, halo_type, halo_type),
        (counts, rhs_old, rhs_cross, rhs_inside, split, sent, send_layers),
        [VMEM] * 7,
        (VMEM,) * 6,
        [turned],
        flops=10**9,
        bytes_accessed=8 * MIB,
    )
    diagonal = gram = None
    basis = [rhs]
    fields = [field]
    for known in range(1, BASIS):
        from_cross = swapped(to_cross, True)
        from_inside = swapped(to_inside, False)
        args = [theta, face_source, field, packed, local] + basis
        outs = [field_type, of(SUB)]
        if known > 1:
            args += [diagonal, gram]
            scratch = layers + [sums]
        else:
            args += [counts, before, diagonal_old, diagonal_cross, diagonal_inside]
            outs.append(field_type)
            scratch = [turned] + layers + [sums]
        found = call(
            functools.partial(local_kernel, known),
            tuple(outs),
            tuple(args),
            [VMEM] * len(args),
            (VMEM,) * len(outs),
            scratch,
            flops=10**9,
            bytes_accessed=4 * MIB,
        )
        partial, gram = found[:2]
        if known == 1:
            diagonal = found[2]
        if known < BASIS - 1:
            value, field, packed, to_cross, to_inside = call(
                next_kernel,
                (field_type, field_type, packed_type, halo_type, halo_type),
                (
                    counts, face_source, send_layers, from_cross, from_inside, partial, taken,
                    split, sent,
                ),
                [VMEM] * 9,
                (VMEM,) * 5,
                flops=10**9,
                bytes_accessed=12 * MIB,
                aliases={5: 0},
            )
            fields.append(field)
        else:
            value, copies = call(
                end_kernel,
                (field_type, of(lax.axis_size(AXES))),
                (counts, face_source, from_cross, from_inside, partial, taken, gram, *basis),
                [VMEM] * (7 + len(basis)),
                (VMEM, VMEM),
                [sums],
                flops=10**9,
                bytes_accessed=12 * MIB,
                aliases={4: 0},
            )
        basis.append(value)
    gathered = lax.all_to_all(copies, AXES, split_axis=0, concat_axis=0, tiled=True)
    return call(
        last_kernel,
        (out_type, out_type),
        (theta, gathered, *basis, *fields),
        [VMEM] * (2 * BASIS + 1),
        (HBM, HBM),
        [pltpu.VMEM((BCELLS, BDEV), F32)] * 2 + [pltpu.SemaphoreType.DMA((2, PARTS))],
        limit=16,
    )


def solution(mesh):
    return jax.shard_map(
        per_device,
        mesh=mesh,
        in_specs=(
            P(None, AXES),
            P(None, AXES),
            P(AXES),
            P(None, AXES),
            P(None, AXES),
            P(),
        ),
        out_specs=(P(None, AXES), P(None, AXES)),
        check_vma=False,
    )
```

```python
import functools

import jax
import jax.numpy as jnp
from jax import lax
from jax.experimental import pallas as pl
from jax.experimental.pallas import tpu as pltpu
from jax.sharding import PartitionSpec as P

BE = 8
BCELLS = 512
FACE = 64
BDEV = 1024
MOVE = 256
CAP = 1536
HMAX = 256
ITERS = 2
LANES = 128
SUB = 8
CHUNKS = BDEV // LANES
AXES = ("gx", "gy", "gz")
REMOTE = 6 * BDEV
BASIS = 2 * ITERS + 1
MIB = 1024 * 1024
PARTS = 8
FRONT = 52
PRODUCT = (0, 4, 5)
SENT = (4, 5, 0, 3)
SPLIT = (1,) + SENT
SHELL = [(i, j) for i in range(BE) for j in range(BE) if i in (0, BE - 1) or j in (0, BE - 1)]
CORE = [(i, j) for i in range(BE) for j in range(BE) if (i, j) not in SHELL]
SHELL_ROWS = len(SHELL) * BE
F32 = jnp.float32

VMEM = pl.BlockSpec(memory_space=pltpu.VMEM)
SMEM = pl.BlockSpec(memory_space=pltpu.SMEM)
HBM = pl.BlockSpec(memory_space=pltpu.HBM)


def swapped(value, cross):
    count = lax.axis_size(AXES)
    first = 1 if cross else 0
    pairs = [(low, low + 1) for low in range(first, count - 1, 2)]
    return lax.ppermute(value, AXES, pairs + [(high, low) for low, high in pairs])


def call(kernel, outs, args, in_specs, out_specs, scratch=(), limit=16, flops=0, bytes_accessed=0, aliases=None):
    if aliases is None:
        aliases = {}
    return pl.pallas_call(
        kernel,
        out_shape=outs,
        in_specs=in_specs,
        out_specs=out_specs,
        scratch_shapes=list(scratch),
        input_output_aliases=aliases,
        compiler_params=pltpu.CompilerParams(vmem_limit_bytes=limit * MIB),
        cost_estimate=pl.CostEstimate(
            flops=flops, bytes_accessed=bytes_accessed, transcendentals=0
        ),
    )(*args)


def lane_iota(rows=SUB):
    return lax.broadcasted_iota(jnp.int32, (rows, LANES), 1)


def lanes(start):
    return pl.ds(pl.multiple_of(start, LANES), LANES)


def pick(values, index):
    return jnp.take_along_axis(values, index, axis=1, mode="promise_in_bounds")


def cut_rows(start, low_ref, high_ref, odd, count, cross_ref, inside_ref):
    tile = start >> 7
    shift = start & (LANES - 1)
    rows = 128

    for step in range(BCELLS // rows):
        at = slice(step * rows, (step + 1) * rows)
        first = lane_iota(rows) < LANES - shift
        turned = []
        for part in range(3):
            source = jnp.minimum(tile + part, high_ref.shape[1] // LANES - 1) * LANES
            turned.append(pltpu.roll(high_ref[at, lanes(source)], (LANES - shift) & (LANES - 1), 1))
        for half in range(2):
            lower = low_ref[at, half * LANES : (half + 1) * LANES]
            upper = jnp.where(first, turned[half], turned[half + 1])
            to = slice(half * BCELLS + step * rows, half * BCELLS + (step + 1) * rows)
            cross_ref[to, :] = jnp.where(odd, upper, lower)
            inside_ref[to, :] = jnp.where(odd, lower, upper)
    if count is not None:
        row = jnp.full((SUB, LANES), count.astype(F32))
        cross_ref[2 * BCELLS : 2 * BCELLS + SUB, :] = row
        inside_ref[2 * BCELLS : 2 * BCELLS + SUB, :] = row


def front_kernel(
    rank_ref, owner_ref, old_ref, counts_ref, cross_ref, inside_ref, low_ref, high_ref, sems
):
    high_copy = pltpu.make_async_copy(
        old_ref.at[:, pl.ds(2 * MOVE, CAP - 2 * MOVE)], high_ref, sems.at[1]
    )
    high_copy.start()
    low_copy = pltpu.make_async_copy(old_ref.at[:, pl.ds(0, MOVE)], low_ref, sems.at[0])
    low_copy.start()
    rank = rank_ref[0]
    owner = owner_ref[...]
    filled = owner >= 0
    head = jnp.sum(((owner == rank - 1) & filled).astype(jnp.int32))
    stay = jnp.sum((owner == rank).astype(jnp.int32))
    tail = jnp.sum(((owner == rank + 1) & filled).astype(jnp.int32))
    odd = rank & 1
    row = lax.broadcasted_iota(jnp.int32, (SUB, LANES), 0)
    counts_ref[...] = jnp.where(
        row == 0, head, jnp.where(row == 1, stay, jnp.where(row == 2, tail, odd))
    )
    high_copy.wait()
    low_copy.wait()
    start = head + stay - 2 * MOVE
    cut_rows(start, low_ref, high_ref, odd == 1, tail, cross_ref, inside_ref)


def count_of(counts_ref, row):
    return jnp.max(counts_ref[row : row + 1, :])


def cut_kernel(counts_ref, old_ref, cross_ref, inside_ref):
    start = count_of(counts_ref, 0) + count_of(counts_ref, 1)
    odd = count_of(counts_ref, 3) == 1
    cut_rows(start, old_ref, old_ref, odd, None, cross_ref, inside_ref)


def count_before(odd, cross_ref, inside_ref):
    row = slice(2 * BCELLS, 2 * BCELLS + SUB)
    return jnp.max(jnp.where(odd, inside_ref[row, :], cross_ref[row, :])).astype(jnp.int32)


def assemble(counts_ref, before, old_ref, cross_ref, inside_ref, out_ref, turned_ref):
    head = count_of(counts_ref, 0)
    stay = count_of(counts_ref, 1)
    odd = count_of(counts_ref, 3) == 1
    own_start = head - before
    own_tile = own_start >> 7
    own_shift = own_start & (LANES - 1)
    up_start = -(before + stay)
    up_tile = up_start >> 7
    up_shift = up_start & (LANES - 1)
    rows = 64
    lane = lane_iota(rows)
    for start in range(0, BCELLS, rows):
        for part in range(2):
            half = slice(part * BCELLS + start, part * BCELLS + start + rows)
            turned_ref[part, start : start + rows, :] = pltpu.roll(
                jnp.where(odd, cross_ref[half, :], inside_ref[half, :]),
                (LANES - up_shift) & (LANES - 1),
                1,
            )
    for start in range(0, BCELLS, rows):
        at = slice(start, start + rows)
        last = None
        for chunk in range(CHUNKS + 1):
            source = jnp.clip(own_tile + chunk, 0, CAP // LANES - 1) * LANES
            now = pltpu.roll(
                old_ref[at, lanes(source)], (LANES - own_shift) & (LANES - 1), 1
            )
            if chunk > 0:
                place = chunk - 1
                column = lane + place * LANES
                value = jnp.where(lane < LANES - own_shift, last, now)
                if place >= 2 * MOVE // LANES:
                    low_half = turned_ref[jnp.clip(up_tile + place, 0, 1), at, :]
                    high_half = turned_ref[jnp.clip(up_tile + place + 1, 0, 1), at, :]
                    above = jnp.where(lane < LANES - up_shift, low_half, high_half)
                    value = jnp.where(column < before + stay, value, above)
                if place < MOVE // LANES:
                    half = slice(place * BCELLS + start, place * BCELLS + start + rows)
                    below = jnp.where(odd, inside_ref[half, :], cross_ref[half, :])
                    value = jnp.where(column < before, below, value)
                out_ref[place * BCELLS + start : place * BCELLS + start + rows, :] = value
            last = now


def prepare_kernel(
    rank_ref, inverse_ref, codes_ref, send_ref,
    split_ref, core_ref, theta_ref, sent_ref, taken_ref, local_ref,
):
    select(rank_ref[0] & 1, codes_ref, send_ref, sent_ref, taken_ref, local_ref)
    inverse = inverse_ref[...]
    size = jnp.abs(inverse)
    by_row = jnp.max(jnp.sum(size, axis=1, keepdims=True), axis=0, keepdims=True)
    by_column = jnp.max(jnp.sum(size, axis=0, keepdims=True), axis=1, keepdims=True)
    bound = 14.5 * jnp.sqrt(by_row) * jnp.sqrt(by_column)
    scale = jnp.full((1, 1), 0.5, F32)
    for power in (64, 32, 16, 8, 4, 2, 1):
        large = bound >= 2.0**power
        bound = jnp.where(large, bound * 2.0**-power, bound)
        scale = jnp.where(large, scale * 2.0**-power, scale)
    for power in (64, 32, 16, 8, 4, 2, 1):
        small = bound < 2.0**-power
        bound = jnp.where(small, bound * 2.0**power, bound)
        scale = jnp.where(small, scale * 2.0**power, scale)
    scaled = inverse * scale
    high = scaled.astype(jnp.bfloat16)
    low = (scaled - high.astype(F32)).astype(jnp.bfloat16)
    at = lax.broadcasted_iota(jnp.int32, (2 * FACE, BCELLS), 0)
    cell = lax.broadcasted_iota(jnp.int32, (2 * FACE, BCELLS), 1)
    wanted = jnp.where(at < FACE, at * BE, (at - FACE) * BE + BE - 1)
    ends = jnp.where(cell == wanted, 1.0, 0.0).astype(jnp.bfloat16)

    def tiles(value, which):
        return [value[(i * BE + j) * BE : (i * BE + j + 1) * BE, :] for i, j in which]

    for part, value in ((0, high), (2 * BCELLS, low)):
        wide = value.astype(F32)
        end_rows = jnp.dot(ends, value, preferred_element_type=F32)
        shell = jnp.concatenate(tiles(wide, SHELL) + [end_rows], axis=0).astype(jnp.bfloat16)
        core = jnp.concatenate(tiles(wide, CORE), axis=0).astype(jnp.bfloat16)
        for column in (part, BCELLS) if part == 0 else (part,):
            split_ref[:, column : column + BCELLS] = shell
            core_ref[:, column : column + BCELLS] = core
    row = lax.broadcasted_iota(jnp.int32, (BCELLS, BCELLS), 0)
    column = lax.broadcasted_iota(jnp.int32, (BCELLS, BCELLS), 1)
    theta = jnp.sum(jnp.where(row == column, scaled, 0.0)) * (6.5 / BCELLS)
    theta_ref[...] = jnp.full((SUB, LANES), theta)


def precondition(split_ref, field_ref, pair):
    base = pair * 2 * BCELLS
    field = jnp.concatenate(
        [field_ref[base + half * BCELLS : base + (half + 1) * BCELLS, :] for half in range(2)],
        axis=1,
    )
    top = field.astype(jnp.bfloat16)
    rest = (field - top.astype(F32)).astype(jnp.bfloat16)
    stacked = jnp.concatenate([top, rest, top], axis=0)
    return jnp.dot(split_ref[...], stacked, preferred_element_type=F32)


def put_tiles(found, which, out_ref, pair):
    for half in range(2):
        for index, (i, j) in enumerate(which):
            row = (2 * pair + half) * BCELLS + (i * BE + j) * BE
            out_ref[row : row + SUB, :] = found[
                index * SUB : (index + 1) * SUB, half * LANES : (half + 1) * LANES
            ]


def one_hot(code, out_ref, row, count, column):
    rows = 512
    width = code.shape[1]
    base = lax.broadcasted_iota(jnp.int32, (rows, width), 0).astype(jnp.int16)
    one = jnp.ones((rows, width), jnp.bfloat16)
    zero = jnp.zeros((rows, width), jnp.bfloat16)
    for start in range(0, count, rows):
        here = base == jnp.broadcast_to((code - start).astype(jnp.int16), (rows, width))
        out_ref[row + start : row + start + rows, column : column + width] = jnp.where(
            here, one, zero
        )


def select(odd, codes_ref, send_ref, sent_ref, taken_ref, local_ref):
    low, high = send_ref[0:1, :], send_ref[1:2, :]
    for index, which in enumerate(SENT):
        for column, code in (
            (0, jnp.where(odd == 1, high, low)), (HMAX, jnp.where(odd == 1, low, high))
        ):
            one_hot(code - which * BDEV, sent_ref, index * BDEV, BDEV, column)
    for index, which in enumerate(PRODUCT):
        for half in range(2):
            code = codes_ref[which : which + 1, half * BCELLS : (half + 1) * BCELLS]
            at = index * BDEV + half * BCELLS
            one_hot((code - REMOTE) ^ (odd * HMAX), taken_ref, 0, 2 * HMAX, at)
            one_hot(code - (which ^ 1) * BDEV, local_ref, 0, BDEV, at)


def halves(value):
    top = value.astype(jnp.bfloat16)
    return jnp.concatenate([top, (value - top.astype(F32)).astype(jnp.bfloat16)], axis=0)


def whole_layer(field_ref, which, chunk):
    start = chunk * BCELLS
    if which < 2:
        row = start + which * (BE - 1) * FACE
        return field_ref[row : row + FACE, :]
    rows = [start + part * FACE + (which - 2) * (BE - 1) * BE for part in range(BE)]
    return jnp.concatenate([field_ref[row : row + SUB, :] for row in rows], axis=0)


def split_layers(field_ref, ends, pair, layers_ref):
    for half in range(2):
        chunk = 2 * pair + half
        for index, which in enumerate(SPLIT):
            at = (index * CHUNKS + chunk) * LANES
            if which >= 4:
                value = ends[
                    (which - 4) * FACE : (which - 3) * FACE, half * LANES : (half + 1) * LANES
                ]
            else:
                value = whole_layer(field_ref, which, chunk)
            layers_ref[:, at : at + LANES] = halves(value)


def pack(field_ref, layers_ref, sent_ref, send_ref, odd, cross_ref, inside_ref):
    low, high = send_ref[0:1, :], send_ref[1:2, :]
    odd = jnp.concatenate([odd, odd], axis=1) == 1
    for out_ref, start, codes in (
        (cross_ref, 0, jnp.where(odd, high, low)), (inside_ref, HMAX, jnp.where(odd, low, high))
    ):
        product = jnp.dot(
            layers_ref[:, BDEV:], sent_ref[:, start : start + HMAX], preferred_element_type=F32
        )
        product = product[:FACE, :] + product[FACE:, :]
        for step in range(2):
            code = jnp.broadcast_to(codes[:, step * LANES : (step + 1) * LANES], (SUB, LANES))
            lane = code & (LANES - 1)
            tile = code >> 7
            found = [
                product[part * SUB : (part + 1) * SUB, step * LANES : (step + 1) * LANES]
                for part in range(8)
            ]
            for which in range(6):
                if which in SENT:
                    continue
                for source in range(CHUNKS):
                    here = tile == which * CHUNKS + source
                    for part in range(8):
                        values = layer_tile(field_ref, which, part, source)
                        found[part] = jnp.where(here, pick(values, lane), found[part])
            for part in range(8):
                row = step * FACE + part * SUB
                out_ref[row : row + SUB, :] = found[part]


def layer_tile(field_ref, which, part, chunk):
    row = (part * BE, (BE - 1) * FACE + part * BE, part * FACE, part * FACE + (BE - 1) * BE)[which]
    row = row + chunk * BCELLS
    return field_ref[row : row + SUB, :]


def layer(faces_ref, chunk, which, part):
    base = (chunk * 6 + which) * FACE + part * SUB
    return faces_ref[base : base + SUB, :]


def gather_layers(pair, codes_ref, field_ref, layers_ref, local_ref, faces_ref):
    for index, which in enumerate(PRODUCT):
        at = index * BDEV + pair * (2 * LANES)
        start = SPLIT.index(which ^ 1) * BDEV
        found = jnp.dot(
            layers_ref[:, start : start + BDEV],
            local_ref[:, at : at + 2 * LANES],
            preferred_element_type=F32,
        )
        found = found[:FACE, :] + found[FACE:, :]
        for half in range(2):
            base = ((2 * pair + half) * 6 + which) * FACE
            faces_ref[base : base + FACE, :] = found[:, half * LANES : (half + 1) * LANES]
    for chunk in (2 * pair, 2 * pair + 1):
        at = slice(chunk * LANES, (chunk + 1) * LANES)
        for which in range(6):
            if which in PRODUCT:
                continue
            partner = which ^ 1
            code = jnp.broadcast_to(codes_ref[which : which + 1, at], (SUB, LANES))
            code = code - partner * BDEV
            lane = code & (LANES - 1)
            tile = code >> 7
            found = [jnp.zeros((SUB, LANES), F32) for _ in range(8)]
            for source in range(CHUNKS):
                here = tile == source
                for part in range(8):
                    values = layer_tile(field_ref, partner, part, source)
                    found[part] = jnp.where(here, pick(values, lane), found[part])
            for part in range(8):
                base = (chunk * 6 + which) * FACE + part * SUB
                faces_ref[base : base + SUB, :] = found[part]


def local_kernel(
    known, theta_ref, codes_ref, old_field_ref, layers_ref, local_ref, core_ref, *refs
):
    basis = refs[:known]
    del old_field_ref
    refs = refs[known:]
    faces_ref, beside_ref, sums_ref = refs[-3:]
    if known > 1:
        diagonal_ref, gram_in_ref, out_ref, gram_ref, field_ref = refs[:5]
        gram_in = gram_in_ref[...]
    else:
        counts_ref, before_ref, old_ref, cross_ref, inside_ref = refs[:5]
        out_ref, gram_ref, field_ref, diagonal_ref, turned_ref = refs[5:10]
        gram_in = jnp.zeros((SUB, LANES), F32)
        assemble(
            counts_ref, count_of(before_ref, 0), old_ref, cross_ref, inside_ref, diagonal_ref, turned_ref
        )
    theta = theta_ref[...]
    sums = [jnp.zeros((SUB, LANES), F32) for _ in range(known)]

    def stencil(chunk):
        start = chunk * BCELLS

        def block(i, j):
            row = start + (i * BE + j) * BE
            return field_ref[row : row + SUB, :]

        for i in range(BE):
            row = [layer(faces_ref, chunk, 4, i)]
            row += [field_ref[pl.ds(start + i * FACE + k, SUB, stride=BE), :] for k in range(BE)]
            row += [layer(faces_ref, chunk, 5, i)]
            for k in range(BE):
                beside_ref[pl.ds(start + i * FACE + k, SUB, stride=BE), :] = row[k] + row[k + 2]
        for i in range(BE):
            for j in range(BE):
                rows = slice(start + (i * BE + j) * BE, start + (i * BE + j + 1) * BE)
                beside = beside_ref[rows, :]
                beside = beside + (block(i - 1, j) if i > 0 else layer(faces_ref, chunk, 0, j))
                beside = beside + (
                    block(i + 1, j) if i < BE - 1 else layer(faces_ref, chunk, 1, j)
                )
                beside = beside + (block(i, j - 1) if j > 0 else layer(faces_ref, chunk, 2, i))
                beside = beside + (
                    block(i, j + 1) if j < BE - 1 else layer(faces_ref, chunk, 3, i)
                )
                newest = basis[-1][rows, :]
                value = (6.0 + diagonal_ref[rows, :]) * block(i, j) - beside
                out_ref[rows, :] = value - theta * newest
                for k, ref in enumerate(basis):
                    old = newest if k == known - 1 else ref[rows, :]
                    sums[k] = sums[k] + newest * old

    for pair in range(CHUNKS // 2):
        put_tiles(precondition(core_ref, basis[-1], pair), CORE, field_ref, pair)
    gather_layers(0, codes_ref, field_ref, layers_ref, local_ref, faces_ref)
    for pair in range(CHUNKS // 2):
        if pair + 1 < CHUNKS // 2:
            gather_layers(pair + 1, codes_ref, field_ref, layers_ref, local_ref, faces_ref)
        stencil(2 * pair)
        stencil(2 * pair + 1)
    for k, part in enumerate(sums):
        sums_ref[k] = part
    place_sums(sums_ref, known, gram_in, gram_ref, (known - 1) * known // 2)


def receive(cross_ref, inside_ref):
    parts = [
        ref[part * FACE : (part + 1) * FACE, :]
        for ref in (cross_ref, inside_ref)
        for part in range(2)
    ]
    return halves(jnp.concatenate(parts, axis=1))


def finish(odd, codes_ref, taken_ref, received, cross_ref, inside_ref, out_ref, pair):
    for which in range(6):
        if which in PRODUCT:
            at = PRODUCT.index(which) * BDEV + pair * 2 * LANES
            product = jnp.dot(
                received, taken_ref[:, at : at + 2 * LANES], preferred_element_type=F32
            )
            product = product[:FACE, :] + product[FACE:, :]
        for half in range(2):
            chunk = pair * 2 + half
            start = chunk * BCELLS
            if which in PRODUCT:
                beside = product[:, half * LANES : (half + 1) * LANES]
            else:
                code = codes_ref[which : which + 1, chunk * LANES : (chunk + 1) * LANES] - REMOTE
                lane = jnp.broadcast_to(code & (LANES - 1), (SUB, LANES))
                tile = jnp.broadcast_to((code >> 7) ^ (odd * 2), (SUB, LANES))
                found = [jnp.zeros((SUB, LANES), F32) for _ in range(8)]
                for source in range(2 * HMAX // LANES):
                    here = tile == source
                    from_ref = cross_ref if source < HMAX // LANES else inside_ref
                    base = source % (HMAX // LANES) * FACE
                    for part in range(8):
                        values = from_ref[base + part * SUB : base + (part + 1) * SUB, :]
                        found[part] = jnp.where(here, pick(values, lane), found[part])
                beside = jnp.concatenate(found, axis=0)
            if which >= 4:
                rows = pl.ds(start + (which - 4) * (BE - 1), FACE, stride=BE)
                out_ref[rows, :] = out_ref[rows, :] - beside
            elif which < 2:
                row = start + which * (BE - 1) * FACE
                out_ref[row : row + FACE, :] = out_ref[row : row + FACE, :] - beside
            else:
                for part in range(BE):
                    row = start + part * FACE + (which - 2) * (BE - 1) * BE
                    out_ref[row : row + SUB, :] = (
                        out_ref[row : row + SUB, :] - beside[part * SUB : (part + 1) * SUB, :]
                    )


def place_sums(sums_ref, count, gram_in, gram_out_ref, first):
    lane = lax.broadcasted_iota(jnp.int32, (SUB, LANES), 1)
    row = gram_in
    for k in range(count):
        row = row + jnp.where(lane == first + k, jnp.sum(sums_ref[k]), 0.0)
    for start in range(0, gram_out_ref.shape[0], SUB):
        gram_out_ref[start : start + SUB, :] = row


def send(
    split_ref, value_ref, field_ref, layers_ref, sent_ref, send_ref, odd, cross_ref, inside_ref,
    before,
):
    for pair in range(CHUNKS // 2):
        before(pair)
        found = precondition(split_ref, value_ref, pair)
        put_tiles(found, SHELL, field_ref, pair)
        split_layers(field_ref, found[SHELL_ROWS:, :], pair, layers_ref)
    pack(field_ref, layers_ref, sent_ref, send_ref, odd, cross_ref, inside_ref)


def first_kernel(
    counts_ref, old_ref, cross_ref, inside_ref, split_ref, sent_ref, send_ref,
    before_ref, rhs_ref, field_ref, layers_ref, to_cross_ref, to_inside_ref,
    turned_ref,
):
    odd = count_of(counts_ref, 3) == 1
    before = count_before(odd, cross_ref, inside_ref)
    before_ref[...] = jnp.full((SUB, LANES), before)
    assemble(counts_ref, before, old_ref, cross_ref, inside_ref, rhs_ref, turned_ref)
    send(
        split_ref, rhs_ref, field_ref, layers_ref, sent_ref, send_ref, counts_ref[3:4, :],
        to_cross_ref, to_inside_ref, lambda pair: None,
    )


def next_kernel(
    counts_ref, codes_ref, send_ref, cross_ref, inside_ref, partial_ref, taken_ref, split_ref,
    sent_ref,
    out_ref, field_ref, layers_ref, to_cross_ref, to_inside_ref,
):
    del partial_ref
    odd = counts_ref[3:4, :]
    received = receive(cross_ref, inside_ref)

    def before(pair):
        finish(odd, codes_ref, taken_ref, received, cross_ref, inside_ref, out_ref, pair)

    send(
        split_ref, out_ref, field_ref, layers_ref, sent_ref, send_ref, odd, to_cross_ref,
        to_inside_ref, before,
    )


def end_kernel(
    counts_ref, codes_ref, cross_ref, inside_ref, partial_ref, taken_ref, gram_in_ref, *refs
):
    del partial_ref
    basis = refs[: BASIS - 1]
    out_ref, gram_ref, sums_ref = refs[BASIS - 1 :]
    odd = counts_ref[3:4, :]
    received = receive(cross_ref, inside_ref)
    sums = [jnp.zeros((SUB, LANES), F32) for _ in range(BASIS)]
    for pair in range(CHUNKS // 2):
        finish(odd, codes_ref, taken_ref, received, cross_ref, inside_ref, out_ref, pair)
        for row in range(pair * 2 * BCELLS, (pair + 1) * 2 * BCELLS, SUB):
            rows = slice(row, row + SUB)
            value = out_ref[rows, :]
            for k, ref in enumerate(basis):
                sums[k] = sums[k] + value * ref[rows, :]
            sums[-1] = sums[-1] + value * value
    for k, part in enumerate(sums):
        sums_ref[k] = part
    place_sums(sums_ref, BASIS, gram_in_ref[...], gram_ref, BASIS * (BASIS - 1) // 2)


def recurrence(gram, theta):
    def dot(left, right):
        total = None
        for a, x in enumerate(left):
            if x is None:
                continue
            part = None
            for b, y in enumerate(right):
                if y is not None:
                    term = gram[max(a, b)][min(a, b)] * y
                    part = term if part is None else part + term
            total = x * part if total is None else total + x * part
        return total

    def add(left, right):
        return [
            y if x is None else x if y is None else x + y for x, y in zip(left, right)
        ]

    def times(factor, vector):
        return [None if x is None else factor * x for x in vector]

    def apply(vector):
        return add([None] + vector[:-1], times(theta, vector))

    one = jnp.ones_like(theta)
    shadow = [one] + [None] * (BASIS - 1)
    residual = shadow
    direction = residual
    rho = gram[0][0]
    rho_next = rho
    total = [None] * BASIS
    along = alpha = omega = None
    for step in range(ITERS):
        if step > 0:
            beta = (rho_next / rho) * (alpha / omega)
            rho = rho_next
            direction = add(residual, times(beta, add(direction, times(-omega, along))))
        along = apply(direction)
        alpha = rho / dot(shadow, along)
        middle = add(residual, times(-alpha, along))
        image = apply(middle)
        omega = dot(image, middle) / dot(image, image)
        total = add(total, add(times(alpha, direction), times(omega, middle)))
        residual = add(middle, times(-omega, image))
        rho_next = dot(shadow, residual)
    return total, residual


def last_kernel(theta_ref, gathered_ref, *refs):
    basis = refs[:BASIS]
    fields = refs[BASIS : 2 * BASIS - 1]
    outs = refs[2 * BASIS - 1 : 2 * BASIS + 1]
    solution_ref, residual_ref, sems = refs[2 * BASIS + 1 :]
    row = jnp.sum(gathered_ref[...], axis=0, keepdims=True)
    lane = lax.broadcasted_iota(jnp.int32, (1, LANES), 1)

    def entry(k):
        return jnp.sum(jnp.where(lane == k, row, 0.0), axis=1, keepdims=True)

    gram = [[entry(a * (a + 1) // 2 + b) for b in range(a + 1)] for a in range(BASIS)]
    theta = theta_ref[0:1, 0:1]
    total, residual = recurrence(gram, theta)
    total = [None if x is None else jnp.broadcast_to(x, (SUB, LANES)) for x in total]
    residual = [jnp.broadcast_to(x, (SUB, LANES)) for x in residual]
    part = BCELLS // PARTS
    copies = []
    for block in range(PARTS):

        def body(step, carry, block=block):
            start = pl.multiple_of(block * part + step * SUB, SUB)
            for chunk in range(CHUNKS):
                rows = pl.ds(chunk * BCELLS + start, SUB)
                at = slice(chunk * LANES, (chunk + 1) * LANES)
                value = total[0] * fields[0][rows, :]
                for k in range(1, BASIS - 1):
                    value = value + total[k] * fields[k][rows, :]
                solution_ref[pl.ds(start, SUB), at] = value
                value = residual[0] * basis[0][rows, :]
                for k in range(1, BASIS):
                    value = value + residual[k] * basis[k][rows, :]
                residual_ref[pl.ds(start, SUB), at] = value
            return carry

        lax.fori_loop(0, part // SUB, body, 0, unroll=4)
        for k, ref in enumerate((solution_ref, residual_ref)):
            at = slice(block * part, (block + 1) * part)
            copies.append(
                pltpu.make_async_copy(ref.at[at, :], outs[k].at[at, :], sems.at[k, block])
            )
            copies[-1].start()
    for copy in copies:
        copy.wait()


def per_device(rhs_old, diagonal_old, new_owner, face_source, send_layers, block_inverse):
    def of(rows):
        return jax.ShapeDtypeStruct((rows, LANES), F32)

    field_type = of(CHUNKS * BCELLS)
    out_type = jax.ShapeDtypeStruct((BCELLS, BDEV), F32)
    halo_type = of(2 * FACE)
    split_type = jax.ShapeDtypeStruct((SHELL_ROWS + 2 * FACE, 3 * BCELLS), jnp.bfloat16)
    core_type = jax.ShapeDtypeStruct((BCELLS - SHELL_ROWS, 3 * BCELLS), jnp.bfloat16)
    turned = pltpu.VMEM((2, BCELLS, LANES), F32)
    layers = [
        pltpu.VMEM((CHUNKS * 6 * FACE, LANES), F32),
        pltpu.VMEM((CHUNKS * BCELLS, LANES), F32),
    ]
    packed_type = jax.ShapeDtypeStruct((2 * FACE, len(SPLIT) * BDEV), jnp.bfloat16)
    sums = pltpu.VMEM((BASIS, SUB, LANES), F32)

    rank = lax.axis_index(AXES).astype(jnp.int32).reshape(1)
    counts, cross, inside = call(
        front_kernel,
        (
            jax.ShapeDtypeStruct((SUB, LANES), jnp.int32),
            of(2 * BCELLS + SUB),
            of(2 * BCELLS + SUB),
        ),
        (rank, new_owner.reshape(CAP // LANES, LANES), rhs_old),
        [SMEM, VMEM, HBM],
        (VMEM, VMEM, VMEM),
        [
            pltpu.VMEM((BCELLS, MOVE), F32),
            pltpu.VMEM((BCELLS, CAP - 2 * MOVE), F32),
            pltpu.SemaphoreType.DMA((2,)),
        ],
        limit=FRONT,
    )
    rhs_cross = swapped(cross, True)
    rhs_inside = swapped(inside, False)
    cross, inside = call(
        cut_kernel,
        (of(2 * BCELLS), of(2 * BCELLS)),
        (counts, diagonal_old),
        [VMEM, VMEM],
        (VMEM, VMEM),
    )
    diagonal_cross = swapped(cross, True)
    diagonal_inside = swapped(inside, False)
    split, core, theta, sent, taken, local = call(
        prepare_kernel,
        (
            split_type,
            core_type,
            of(SUB),
            jax.ShapeDtypeStruct((len(SENT) * BDEV, 2 * HMAX), jnp.bfloat16),
            jax.ShapeDtypeStruct((2 * HMAX, len(PRODUCT) * BDEV), jnp.bfloat16),
            jax.ShapeDtypeStruct((BDEV, len(PRODUCT) * BDEV), jnp.bfloat16),
        ),
        (rank, block_inverse, face_source, send_layers),
        [SMEM] + [VMEM] * 3,
        (VMEM,) * 6,
    )
    before, rhs, field, packed, to_cross, to_inside = call(
        first_kernel,
        (jax.ShapeDtypeStruct((SUB, LANES), jnp.int32),)
        + (field_type, field_type, packed_type, halo_type, halo_type),
        (counts, rhs_old, rhs_cross, rhs_inside, split, sent, send_layers),
        [VMEM] * 7,
        (VMEM,) * 6,
        [turned],
        flops=10**9,
        bytes_accessed=8 * MIB,
    )
    diagonal = gram = None
    basis = [rhs]
    fields = []
    for known in range(1, BASIS):
        from_cross = swapped(to_cross, True)
        from_inside = swapped(to_inside, False)
        args = [theta, face_source, field, packed, local, core] + basis
        outs = [field_type, of(SUB), field_type]
        if known > 1:
            args += [diagonal, gram]
            scratch = layers + [sums]
        else:
            args += [counts, before, diagonal_old, diagonal_cross, diagonal_inside]
            outs.append(field_type)
            scratch = [turned] + layers + [sums]
        found = call(
            functools.partial(local_kernel, known),
            tuple(outs),
            tuple(args),
            [VMEM] * len(args),
            (VMEM,) * len(outs),
            scratch,
            flops=10**9,
            bytes_accessed=4 * MIB,
            aliases={2: 2},
        )
        partial, gram, field = found[:3]
        fields.append(field)
        if known == 1:
            diagonal = found[3]
        if known < BASIS - 1:
            value, field, packed, to_cross, to_inside = call(
                next_kernel,
                (field_type, field_type, packed_type, halo_type, halo_type),
                (
                    counts, face_source, send_layers, from_cross, from_inside, partial, taken,
                    split, sent,
                ),
                [VMEM] * 9,
                (VMEM,) * 5,
                flops=10**9,
                bytes_accessed=12 * MIB,
                aliases={5: 0},
            )
        else:
            value, copies = call(
                end_kernel,
                (field_type, of(lax.axis_size(AXES))),
                (counts, face_source, from_cross, from_inside, partial, taken, gram, *basis),
                [VMEM] * (7 + len(basis)),
                (VMEM, VMEM),
                [sums],
                flops=10**9,
                bytes_accessed=12 * MIB,
                aliases={4: 0},
            )
        basis.append(value)
    gathered = lax.all_to_all(copies, AXES, split_axis=0, concat_axis=0, tiled=True)
    return call(
        last_kernel,
        (out_type, out_type),
        (theta, gathered, *basis, *fields),
        [VMEM] * (2 * BASIS + 1),
        (HBM, HBM),
        [pltpu.VMEM((BCELLS, BDEV), F32)] * 2 + [pltpu.SemaphoreType.DMA((2, PARTS))],
        limit=16,
    )


def solution(mesh):
    return jax.shard_map(
        per_device,
        mesh=mesh,
        in_specs=(
            P(None, AXES),
            P(None, AXES),
            P(AXES),
            P(None, AXES),
            P(None, AXES),
            P(),
        ),
        out_specs=(P(None, AXES), P(None, AXES)),
        check_vma=False,
    )
```
